32 devices in a mesh: section: 2 (over core), seq: 4 (over y, x), dp: 4 (over z).
Axes of the slice: x: 2, y: 2, z: 4, core: 2. Of those that a mesh axis runs over, the one named last changes fastest.
Arguments:
- section_inputs: bfloat16 [2, 2, 8, 736, 1152], P('section', None, 'dp', 'seq'), may hold values from -6 to 6
- key_mask: int32 [2, 8, 736], P(None, 'dp'), may hold values from 0 to 1, as said below
- attention_in: bfloat16 [2, 1152, 3456], P('section', 'dp'), may hold values from -0.25 to 0.25
- attention_out: bfloat16 [2, 1152, 1152], P('section', 'dp'), may hold values from -0.5 to 0.5
- expand_weight: bfloat16 [2, 1152, 4304], P('section', 'dp'), may hold values from -0.1875 to 0.1875
- contract_weight: bfloat16 [2, 4304, 1152], P('section', 'dp'), may hold values from -0.125 to 0.125
- norm_gains: bfloat16 [2, 2, 1152], P('section', None, 'dp'), may hold values from 0.099609375 to 1.8984375
- biases: bfloat16 [2, 6, 1152], P('section', None, 'dp'), may hold values from -1.796875 to 1.796875
- expand_bias: bfloat16 [2, 4304], P('section', 'dp'), may hold values from -1.796875 to 1.796875
Outputs:
- section_results: float32 [2, 2, 8, 736, 1152], P('section', None, 'dp', 'seq')
- attention_in_grad: float32 [2, 1152, 3456], P('section', 'dp')
- attention_out_grad: float32 [2, 1152, 1152], P('section', 'dp')
- expand_weight_grad: float32 [2, 1152, 4304], P('section', 'dp')
- contract_weight_grad: float32 [2, 4304, 1152], P('section', 'dp')
- norm_gains_grad: float32 [2, 2, 1152], P('section', None, 'dp')
- biases_grad: float32 [2, 6, 1152], P('section', None, 'dp')
- expand_bias_grad: float32 [2, 4304], P('section', 'dp')
The draws below stay inside these ranges and needn't reach their ends.
Inputs may be any that keep to these rules, and one draw needn't show every extreme that they name: `key_mask`: each image has exactly 7 padding positions (zeros), placed anywhere among its 736 positions.
All inputs are finite; a program needn't handle non-finite values.
Results may differ from the reference program's by a relative error of at most 0.025.
Values may be sent and summed in bfloat16 or wider, within the bound.
No kernel may reach another device: no remote copies, remote signals or barrier semaphores. Data moves between devices by JAX's collectives and lax.ppermute only.
A program may use at most 384 MiB of HBM per device.

```python
import jax
import jax.numpy as jnp
from jax import lax

HEADS = 16
HEAD_DIM = 72
D = 1152
FF = 4304
L = 736
PAD = 7
MB = 2
IMAGES = 8


def draw_key_mask(key, part):
    key = jax.random.fold_in(key, 11)
    row_keys = jax.random.split(key, MB * IMAGES)
    orders = jax.vmap(lambda single: jax.random.permutation(single, L))(row_keys)
    return (orders >= PAD).astype(jnp.int32).reshape(MB, IMAGES, L)


def shard_levels(stream_key, dims, cuts, least, high):
    factor_of = 1.0
    for dim, parts in cuts:
        heights = jax.random.uniform(jax.random.fold_in(jax.random.fold_in(stream_key, 6), dim), (parts,), jnp.float32, least / len(cuts), high / len(cuts))
        factor_of = factor_of * jnp.repeat(jnp.exp(heights), dims[dim] // parts).reshape((-1,) + (1,) * (len(dims) - 1 - dim))
    return factor_of


def bell_draw(stream_key, dims, scale, limit, pieces=(), dtype=jnp.bfloat16):
    values = scale * jax.random.normal(stream_key, dims, jnp.float32)
    if pieces:
        values = values * shard_levels(stream_key, dims, pieces, -0.22, 0.18)
    return jnp.clip(values, -limit, limit).astype(dtype)


def setup_inputs(seed: int = 0) -> dict:
    keys = jax.random.split(jax.random.key(seed), 10)
    section_inputs = bell_draw(keys[0], (2, MB, IMAGES, L, D), 1.0, 6.0, ((0, 2), (2, 4), (3, 4)))
    key_mask = draw_key_mask(jax.random.fold_in(keys[9], 71), 0)
    attention_in = bell_draw(keys[2], (2, D, 3 * D), (D // 2) ** -0.5, 0.25, ((0, 2), (1, 4)))
    attention_out = bell_draw(keys[3], (2, D, D), (D // 8) ** -0.5, 0.5, ((0, 2), (1, 4)))
    expand_weight = bell_draw(keys[4], (2, D, FF), D ** -0.5, 0.1875, ((0, 2), (1, 4)))
    contract_weight = bell_draw(keys[5], (2, FF, D), (FF // 2) ** -0.5, 0.125, ((0, 2), (1, 4)))
    norm_gains = jnp.clip(1.0 + 0.18 * jax.random.normal(keys[6], (2, 2, D), jnp.float32), 0.099609375, 1.8984375).astype(jnp.bfloat16)
    biases = bell_draw(keys[7], (2, 6, D), 0.3, 1.796875, ((0, 2), (2, 4)))
    expand_bias = bell_draw(keys[8], (2, FF), 0.3, 1.796875, ((0, 2), (1, 4)))
    return {"section_inputs": section_inputs, "key_mask": key_mask, "attention_in": attention_in, "attention_out": attention_out, "expand_weight": expand_weight, "contract_weight": contract_weight, "norm_gains": norm_gains, "biases": biases, "expand_bias": expand_bias}


@jax.custom_vjp
def low(v):
    return lax.optimization_barrier(v.astype(jnp.bfloat16)).astype(jnp.float32)

@jax.custom_vjp
def low_back(v):
    return v

def low_keep(v):
    return (low(v), None)

def low_pass(kept, grad):
    return (grad,)

def back_keep(v):
    return (v, None)

def back_low(kept, grad):
    return (low(grad),)
low.defvjp(low_keep, low_pass)
low_back.defvjp(back_keep, back_low)
HIGHEST = lax.Precision.HIGHEST

def layer_norm(stream, gain, shift):
    centre = lax.optimization_barrier(jnp.mean(stream, axis=-1, keepdims=True))
    offset = stream - centre
    spread = lax.optimization_barrier(jnp.mean(offset * offset, axis=-1, keepdims=True))
    return offset * lax.rsqrt(spread + 1e-06) * gain + shift

def encoder_layer(stream, visible, weights):
    attn_in, attn_out, expand, contract, gains, shifts, expand_shift = weights
    count = stream.shape[0]
    normed = low(layer_norm(stream, gains[0], shifts[0]))
    projected = jnp.einsum('nld,de->nle', normed, attn_in, precision=HIGHEST)
    queries = low_back(low(projected[..., :D] + shifts[2]))
    key_rows = low_back(low(projected[..., D:2 * D]))
    value_rows = low_back(low(projected[..., 2 * D:] + shifts[3]))
    queries = queries.reshape(count, L, HEADS, HEAD_DIM)
    key_rows = key_rows.reshape(count, L, HEADS, HEAD_DIM)
    value_rows = value_rows.reshape(count, L, HEADS, HEAD_DIM)
    scores = jnp.einsum('nqhd,nkhd->nhqk', queries, key_rows, precision=HIGHEST) * HEAD_DIM ** (-0.5)
    scores = low_back(scores)
    scores = jnp.where(visible[:, None, None, :], scores, -1000000000.0)
    row_max = lax.optimization_barrier(jnp.max(scores, axis=-1, keepdims=True))
    expon = jnp.exp(scores - row_max)
    softmaxed = low(expon / lax.optimization_barrier(jnp.sum(expon, axis=-1, keepdims=True)))
    mixture = jnp.einsum('nhqk,nkhd->nqhd', softmaxed, value_rows, precision=HIGHEST).reshape(count, L, D)
    mixture = low_back(low(mixture))
    attended = low_back(jnp.einsum('nld,de->nle', mixture, attn_out, precision=HIGHEST) + shifts[4])
    middle = stream + attended
    normed_mid = low(layer_norm(middle, gains[1], shifts[1]))
    hidden_pre = low_back(jnp.einsum('nld,df->nlf', normed_mid, expand, precision=HIGHEST) + expand_shift)
    hidden = low(jax.nn.gelu(hidden_pre, approximate=True))
    return middle + jnp.einsum('nlf,fd->nld', hidden, contract, precision=HIGHEST) + shifts[5]

def both_layers(stream, visible, first_layer, second_layer):
    between = low_back(low(encoder_layer(stream, visible, first_layer)))
    return encoder_layer(between, visible, second_layer)

def reference(section_inputs, key_mask, attention_in, attention_out, expand_weight, contract_weight, norm_gains, biases, expand_bias):
    params = tuple((w.astype(jnp.float32) for w in (attention_in, attention_out, expand_weight, contract_weight, norm_gains, biases, expand_bias)))
    first_layer = tuple((w[0] for w in params))
    second_layer = tuple((w[1] for w in params))
    groups = MB * IMAGES // 4
    inputs = section_inputs[0].astype(jnp.float32).reshape(groups, 4, L, D)
    cotangent = section_inputs[1].astype(jnp.float32).reshape(groups, 4, L, D)
    visible = (key_mask > 0).reshape(groups, 4, L)
    blocked = jax.checkpoint(both_layers)

    def model(inputs, first_layer, second_layer):
        return lax.map(lambda pair: blocked(pair[0], pair[1], first_layer, second_layer), (inputs, visible))
    outputs, pullback = jax.vjp(model, inputs, first_layer, second_layer)
    d_inputs, d_first, d_second = pullback(cotangent)
    results = jnp.stack([d_inputs.reshape(MB, IMAGES, L, D), outputs.reshape(MB, IMAGES, L, D)])
    grads = tuple((jnp.stack([one_grad, two_grad]) for one_grad, two_grad in zip(d_first, d_second)))
    return (results, grads[0], grads[1], grads[2], grads[3], grads[4], grads[5], grads[6])
```

```python
import jax
import jax.numpy as jnp
from jax import lax
from jax.experimental import pallas as pl
from jax.experimental.pallas import tpu as pltpu
from jax.sharding import PartitionSpec as P

HEAD_DIM = 72
SCALE = HEAD_DIM**-0.5
VMEM_LIMIT = 56 * 1024 * 1024
F32 = jnp.float32
BF16 = jnp.bfloat16
LIGHT = pl.CostEstimate(flops=1, bytes_accessed=1, transcendentals=0)


def round_up(value, step):
    return -(-value // step) * step


def pick(array, index, axis=0):
    return lax.dynamic_index_in_dim(array, index, axis, keepdims=False)


def swap_cores(value):
    swap = [(0, 1), (1, 0)]
    return jax.tree.map(lambda array: lax.ppermute(array, "section", swap), value)


def swap_seq(value, bit):
    count = lax.axis_size("seq")
    return lax.ppermute(value, "seq", [(index, index ^ bit) for index in range(count)])


def dot(left, right, left_axis, right_axis):
    return lax.dot_general(
        left, right, (((left_axis,), (right_axis,)), ((), ())), preferred_element_type=F32
    )


def params_of(limit=VMEM_LIMIT):
    return pltpu.CompilerParams(vmem_limit_bytes=limit)


def whole_vmem(count):
    return [pl.BlockSpec(memory_space=pltpu.VMEM)] * count


def half_runs(total, parts, half, width):
    size = total // parts
    runs = [[], []]
    for part in range(parts):
        runs[0].append((part * size, half, part * width))
        runs[1].append((part * size + half, size - half, part * width))
    return runs


def split_columns(weight, runs, width, core):
    rows = weight.shape[0]

    def kernel(core_ref, whole_ref, keep_ref, send_ref):
        def write(ref, pieces):
            if sum(size for _, size, _ in pieces) < width:
                ref[...] = jnp.zeros_like(ref)
            for start, size, place in pieces:
                ref[:, place : place + size] = whole_ref[:, start : start + size]

        @pl.when(core_ref[0] == 0)
        def _():
            write(keep_ref, runs[0])
            write(send_ref, runs[1])

        @pl.when(core_ref[0] == 1)
        def _():
            write(keep_ref, runs[1])
            write(send_ref, runs[0])

    shape = jax.ShapeDtypeStruct((rows, width), weight.dtype)
    return pl.pallas_call(
        kernel,
        out_shape=(shape, shape),
        in_specs=[pl.BlockSpec(memory_space=pltpu.SMEM)] + whole_vmem(1),
        out_specs=tuple(whole_vmem(2)),
        compiler_params=params_of(),
        cost_estimate=LIGHT,
        name="split_columns",
    )(core, weight)


def join_columns(mine, other, runs, total, place):
    count, rows, width = mine.shape

    def kernel(place_ref, mine_ref, other_ref, out_ref):
        def write(first, second):
            for ref, pieces in ((first, runs[0]), (second, runs[1])):
                for start, size, at in pieces:
                    out_ref[0, :, start : start + size] = ref[0, :, at : at + size].astype(F32)

        @pl.when(place_ref[0] == 0)
        def _():
            write(mine_ref, other_ref)

        @pl.when(place_ref[0] == 1)
        def _():
            write(other_ref, mine_ref)

    block = pl.BlockSpec((1, rows, width), lambda j, place: (j, 0, 0))
    out = pl.pallas_call(
        kernel,
        out_shape=jax.ShapeDtypeStruct((count, rows, total), F32),
        grid_spec=pltpu.PrefetchScalarGridSpec(
            num_scalar_prefetch=1,
            grid=(count,),
            in_specs=[block, block],
            out_specs=pl.BlockSpec((1, rows, total), lambda j, place: (j ^ place[1], 0, 0)),
        ),
        compiler_params=params_of(),
        cost_estimate=LIGHT,
        name="join_columns",
    )(place, mine, other)
    return out.reshape(count * rows, total)


def join_rows(mine, other, total, place):
    count, rows, width = mine.shape

    def kernel(place_ref, mine_ref, other_ref, out_ref):
        half = pl.program_id(0) // count

        @pl.when(half == place_ref[0])
        def _():
            out_ref[...] = mine_ref[0].astype(F32)

        @pl.when(half != place_ref[0])
        def _():
            out_ref[...] = other_ref[0].astype(F32)

    def quarter(step):
        return lax.rem(step, count)

    return pl.pallas_call(
        kernel,
        out_shape=jax.ShapeDtypeStruct((total, width), F32),
        grid_spec=pltpu.PrefetchScalarGridSpec(
            num_scalar_prefetch=1,
            grid=(2 * count,),
            in_specs=[
                pl.BlockSpec((1, rows, width), lambda t, place: (quarter(t), 0, 0)),
                pl.BlockSpec((1, rows, width), lambda t, place: (quarter(t), 0, 0)),
            ],
            out_specs=pl.BlockSpec(
                (rows, width),
                lambda t, place: (lax.div(t, count) * count + (quarter(t) ^ place[1]), 0),
            ),
        ),
        compiler_params=params_of(),
        cost_estimate=LIGHT,
        name="join_rows",
    )(place, mine, other)


def assemble(own, near, side, front, across):
    parts, rows, columns = near.shape
    count = parts + 1
    place = jnp.stack([lax.axis_index("dp"), lax.axis_index("seq")]).astype(jnp.int32)

    def kernel(place_ref, own_ref, near_ref, side_ref, front_ref, across_ref, out_ref, sem):
        along, here = place_ref[0], place_ref[1]
        copies = [pltpu.make_async_copy(own_ref, out_ref.at[along], sem.at[0])]
        for step in range(parts):
            there = lax.rem(along + step + 1, count)
            for bits, ref in enumerate((near_ref, side_ref, front_ref, across_ref)):
                copies.append(
                    pltpu.make_async_copy(
                        ref.at[step], out_ref.at[there, here ^ bits], sem.at[len(copies)]
                    )
                )
        for copy in copies:
            copy.start()
        for copy in copies:
            copy.wait()

    return pl.pallas_call(
        kernel,
        out_shape=jax.ShapeDtypeStruct((count, 4, rows, columns), own.dtype),
        in_specs=[pl.BlockSpec(memory_space=pltpu.SMEM)]
        + [pl.BlockSpec(memory_space=pl.ANY)] * 5,
        out_specs=pl.BlockSpec(memory_space=pltpu.VMEM),
        scratch_shapes=[pltpu.SemaphoreType.DMA((1 + 4 * parts,))],
        compiler_params=params_of(),
        cost_estimate=LIGHT,
        name="assemble",
    )(place, own, near, side, front, across)


def line_shifts(value):
    count = lax.axis_size("dp")
    return jnp.stack(
        [
            lax.ppermute(value, "dp", [((to + step) % count, to) for to in range(count)])
            for step in range(1, count)
        ]
    )


def line_gather(value):
    count = lax.axis_size("dp")
    line = lax.all_gather(value, "dp", axis=0)
    return lax.dynamic_slice_in_dim(
        jnp.concatenate([line, line], 0), lax.axis_index("dp") + 1, count - 1, 0
    )


def quarters_of(shard):
    return shard.reshape(4, shard.shape[0] // 4, shard.shape[1])


def spread(near):
    return swap_seq(near, 1), swap_seq(near, 2)


def spread_on(neighbours, by_side):
    side, front = neighbours
    return swap_seq(front, 1) if by_side else swap_seq(side, 2)


def bits_of_place():
    here = lax.axis_index("seq")
    return lax.rem(here, 2), lax.div(here, 2)


def grad_halves(left, right, count, by_side, start, end):
    length, depth = left.shape
    columns = end - start
    rows = depth // count
    quarter = round_up(rows, 32) // 4
    x, y = bits_of_place()
    bit = (x if by_side else y).astype(jnp.int32).reshape(1)

    def kernel(bit_ref, left_ref, right_ref, keep_ref, send_ref, turned):
        block = pl.program_id(0)

        @pl.when(block == 0)
        def _():
            turned[...] = left_ref[...].astype(F32).T.astype(BF16).reshape(turned.shape)

        grad = dot(turned[block], right_ref[:, start:end], 1, 0)
        if 4 * quarter > rows:
            empty = jnp.zeros((4 * quarter - rows, columns), F32)
            grad = jnp.concatenate([grad, empty], axis=0)
        parts = [grad[at * quarter : (at + 1) * quarter].astype(BF16) for at in range(4)]
        zeros, ones = ((0, 2), (1, 3)) if by_side else ((0, 1), (2, 3))

        def write(ref, which):
            for index, at in enumerate(which):
                ref[0, index] = parts[at]

        @pl.when(bit_ref[0] == 0)
        def _():
            write(keep_ref, zeros)
            write(send_ref, ones)

        @pl.when(bit_ref[0] == 1)
        def _():
            write(keep_ref, ones)
            write(send_ref, zeros)

    out = pl.BlockSpec((1, 2, quarter, columns), lambda z, bit: (z, 0, 0, 0))
    shape = jax.ShapeDtypeStruct((count, 2, quarter, columns), BF16)
    return pl.pallas_call(
        kernel,
        out_shape=(shape, shape),
        grid_spec=pltpu.PrefetchScalarGridSpec(
            num_scalar_prefetch=1,
            grid=(count,),
            in_specs=[
                pl.BlockSpec((length, depth), lambda z, bit: (0, 0)),
                pl.BlockSpec(right.shape, lambda z, bit: (0, 0)),
            ],
            out_specs=(out, out),
            scratch_shapes=[pltpu.VMEM((count, rows, length), BF16)],
        ),
        compiler_params=params_of(),
        cost_estimate=LIGHT,
        name="grad_halves",
    )(bit, left, right)


def add_half(held, moved, by_side):
    count, _, rows, columns = held.shape
    x, y = bits_of_place()
    bit = (y if by_side else x).astype(jnp.int32).reshape(1)

    def kernel(bit_ref, held_ref, moved_ref, keep_ref, send_ref):
        def total(index):
            return (held_ref[0, index].astype(F32) + moved_ref[0, index].astype(F32)).astype(BF16)

        keep_ref[0] = total(bit_ref[0])
        send_ref[0] = total(1 - bit_ref[0])

    both = pl.BlockSpec((1, 2, rows, columns), lambda z, bit: (z, 0, 0, 0))
    out = pl.BlockSpec((1, rows, columns), lambda z, bit: (z, 0, 0))
    shape = jax.ShapeDtypeStruct((count, rows, columns), BF16)
    return pl.pallas_call(
        kernel,
        out_shape=(shape, shape),
        grid_spec=pltpu.PrefetchScalarGridSpec(
            num_scalar_prefetch=1, grid=(count,), in_specs=[both, both], out_specs=(out, out)
        ),
        compiler_params=params_of(),
        cost_estimate=LIGHT,
        name="add_half",
    )(bit, held, moved)


def add_low(left, right):
    return (left.astype(F32) + right.astype(F32)).astype(BF16)


class Sum:
    def __init__(self, left, right, count, by_side, columns=None):
        self.by_side = by_side
        start, end = columns or (0, right.shape[1])
        self.keep, self.send = grad_halves(left, right, count, by_side, start, end)

    def first(self):
        self.moved = swap_seq(self.send, 1 if self.by_side else 2)

    def add(self):
        self.keep, self.send = add_half(self.keep, self.moved, self.by_side)

    def second(self):
        self.moved = swap_seq(self.send, 2 if self.by_side else 1)

    def over_line(self, gate):
        part = gate(add_low(self.keep, self.moved))
        self.line = lax.psum_scatter(part, "dp", scatter_dimension=0, tiled=True)[0]

    def over_line_shifts(self):
        line, count = lax.axis_index("dp"), lax.axis_size("dp")
        part = self.keep.astype(F32) + self.moved.astype(F32)
        total = pick(part, line)
        for step in range(1, count):
            moved = lax.ppermute(
                pick(part, lax.rem(line + step, count)).astype(BF16),
                "dp",
                [(source, (source + step) % count) for source in range(count)],
            )
            total = total + moved.astype(F32)
        self.line = total.astype(BF16)


def plain_grad(left, right):
    depth, columns = left.shape[1], right.shape[1]

    def kernel(left_ref, right_ref, out_ref):
        turned = left_ref[...].astype(F32).T.astype(BF16)
        for start, end in tiles(columns):
            out_ref[:, start:end] = dot(turned, right_ref[:, start:end], 1, 0).astype(BF16)

    return whole_call(kernel, "plain_grad", [((depth, columns), BF16)], left, right)[0]


class Order:
    def __init__(self, token):
        self.token = token

    def __call__(self, *values):
        values, self.token = lax.optimization_barrier((values, self.token))
        return values if len(values) > 1 else values[0]

    def sent(self, *sums):
        for each in sums:
            each.send = self(each.send)

    def summed(self, *sums):
        for each in sums:
            each.line = self(each.line)

    def arrived(self, *sums):
        for each in sums:
            each.moved = self(each.moved)


def in_order(pieces):
    here = lax.axis_index("seq")
    return jnp.stack([pick(pieces, here ^ index) for index in range(4)])


def attention_forward(qkv, hidden_keys):
    length, width = qkv.shape
    width //= 3
    heads = width // HEAD_DIM

    def kernel(qkv_ref, hidden_ref, out_ref, lse_ref, q_s, k_s, v_s, o_s):
        head = pl.program_id(0)

        @pl.when(head == 0)
        def _():
            for index in range(heads):
                at = index * HEAD_DIM
                q_s[index] = qkv_ref[:, at : at + HEAD_DIM]
                k_s[index] = qkv_ref[:, width + at : width + at + HEAD_DIM]
                v_s[index] = qkv_ref[:, 2 * width + at : 2 * width + at + HEAD_DIM]

        scores = dot(k_s[head], q_s[head], 1, 1) * SCALE
        scores = jnp.where(hidden_ref[...] > 0, -1e9, scores)
        top = jnp.max(scores, axis=0, keepdims=True)
        expon = jnp.exp(scores - top)
        total = jnp.sum(expon, axis=0, keepdims=True)
        lse_ref[0] = top + jnp.log(total)
        mixed = dot(v_s[head], expon.astype(BF16), 0, 0) / total
        o_s[head] = mixed.T.astype(BF16)

        @pl.when(head == heads - 1)
        def _():
            for index in range(heads):
                out_ref[:, index * HEAD_DIM : (index + 1) * HEAD_DIM] = o_s[index]

    slab = pltpu.VMEM((heads, length, HEAD_DIM), BF16)
    return pl.pallas_call(
        kernel,
        grid=(heads,),
        out_shape=(
            jax.ShapeDtypeStruct((length, width), BF16),
            jax.ShapeDtypeStruct((heads, 1, length), F32),
        ),
        in_specs=[
            pl.BlockSpec((length, 3 * width), lambda h: (0, 0)),
            pl.BlockSpec((length, 1), lambda h: (0, 0)),
        ],
        out_specs=(
            pl.BlockSpec((length, width), lambda h: (0, 0)),
            pl.BlockSpec((1, 1, length), lambda h: (h, 0, 0)),
        ),
        scratch_shapes=[slab, slab, slab, slab],
        compiler_params=params_of(),
        cost_estimate=LIGHT,
        name="attention_forward",
    )(qkv, hidden_keys)


def attention_backward(qkv, d_out, lse, hidden_keys):
    length, width = d_out.shape
    heads = width // HEAD_DIM

    def kernel(qkv_ref, do_ref, lse_ref, hidden_ref, out_ref, q_s, k_s, v_s, do_s, dq_s, dk_s, dv_s):
        head = pl.program_id(0)

        @pl.when(head == 0)
        def _():
            for index in range(heads):
                at = index * HEAD_DIM
                q_s[index] = qkv_ref[:, at : at + HEAD_DIM]
                k_s[index] = qkv_ref[:, width + at : width + at + HEAD_DIM]
                v_s[index] = qkv_ref[:, 2 * width + at : 2 * width + at + HEAD_DIM]
                do_s[index] = do_ref[:, at : at + HEAD_DIM]

        queries, keys, values, d_rows = q_s[head], k_s[head], v_s[head], do_s[head]
        scores = dot(keys, queries, 1, 1) * SCALE
        scores = jnp.where(hidden_ref[...] > 0, -1e9, scores)
        soft = jnp.exp(scores - lse_ref[0])
        d_soft = dot(values, d_rows, 1, 1)
        inner = jnp.sum(soft * d_soft, axis=0, keepdims=True)
        d_scores = (soft * (d_soft - inner)).astype(BF16)
        dv_s[head] = dot(soft.astype(BF16), d_rows, 1, 0).astype(BF16)
        dk_s[head] = (dot(d_scores, queries, 1, 0) * SCALE).astype(BF16)
        dq_s[head] = (dot(keys, d_scores, 0, 0) * SCALE).T.astype(BF16)

        @pl.when(head == heads - 1)
        def _():
            for index in range(heads):
                at = index * HEAD_DIM
                out_ref[:, at : at + HEAD_DIM] = dq_s[index]
                out_ref[:, width + at : width + at + HEAD_DIM] = dk_s[index]
                out_ref[:, 2 * width + at : 2 * width + at + HEAD_DIM] = dv_s[index]

    slab = pltpu.VMEM((heads, length, HEAD_DIM), BF16)
    return pl.pallas_call(
        kernel,
        grid=(heads,),
        out_shape=jax.ShapeDtypeStruct((length, 3 * width), BF16),
        in_specs=[
            pl.BlockSpec((length, 3 * width), lambda h: (0, 0)),
            pl.BlockSpec((length, width), lambda h: (0, 0)),
            pl.BlockSpec((1, 1, length), lambda h: (h, 0, 0)),
            pl.BlockSpec((length, 1), lambda h: (0, 0)),
        ],
        out_specs=pl.BlockSpec((length, 3 * width), lambda h: (0, 0)),
        scratch_shapes=[slab] * 7,
        compiler_params=params_of(),
        cost_estimate=LIGHT,
        name="attention_backward",
    )(qkv, d_out, lse, hidden_keys)


def norm_parts(stream):
    centre = jnp.mean(stream, axis=-1, keepdims=True)
    offset = stream - centre
    spread = jnp.mean(offset * offset, axis=-1, keepdims=True)
    inverse = lax.rsqrt(spread + 1e-06)
    return offset * inverse, inverse


def tiles(total, step=256):
    return [(at, min(at + step, total)) for at in range(0, total, step)]


def whole_call(kernel, name, out_shapes, *arrays):
    shapes = tuple(jax.ShapeDtypeStruct(shape, dtype) for shape, dtype in out_shapes)
    return pl.pallas_call(
        kernel,
        out_shape=shapes,
        in_specs=whole_vmem(len(arrays)),
        out_specs=tuple(whole_vmem(len(shapes))),
        compiler_params=params_of(),
        cost_estimate=LIGHT,
        name=name,
    )(*arrays)


PIECES = 3


def join_pieces(refs):
    return jnp.concatenate([ref[...] for ref in refs], axis=1).astype(F32)


def partial_product(left, weight, turned, name):
    length = left.shape[0]
    columns = weight.shape[0 if turned else 1]
    piece = columns // PIECES

    def kernel(left_ref, weight_ref, *out_refs):
        for start, end in tiles(columns):
            if turned:
                product = dot(left_ref[...], weight_ref[start:end, :], 1, 1)
            else:
                product = dot(left_ref[...], weight_ref[:, start:end], 1, 0)
            product = product.astype(BF16)
            for index, ref in enumerate(out_refs):
                low, high = max(start, index * piece), min(end, (index + 1) * piece)
                if low < high:
                    ref[:, low - index * piece : high - index * piece] = product[
                        :, low - start : high - start
                    ]

    return whole_call(kernel, name, [((length, piece), BF16)] * PIECES, left, weight)


def project_in(base, partials, vectors, weight, shift):
    length, width = base.shape
    columns = weight.shape[1]

    def kernel(*refs):
        if partials is None:
            base_ref, vectors_ref, weight_ref, shift_ref, normed_ref, qkv_ref = refs
            stream = base_ref[...].astype(F32)
        else:
            base_ref, *refs = refs
            own_refs, other_refs = refs[:PIECES], refs[PIECES : 2 * PIECES]
            bias_ref, vectors_ref, weight_ref, shift_ref = refs[2 * PIECES : 2 * PIECES + 4]
            normed_ref, qkv_ref, stream_ref = refs[2 * PIECES + 4 :]
            stream = base_ref[...] + join_pieces(own_refs) + join_pieces(other_refs)
            stream_ref[...] = (stream + bias_ref[...]).astype(BF16)
            stream = stream_ref[...].astype(F32)
        normed = norm_parts(stream)[0] * vectors_ref[0:1, :] + vectors_ref[2:3, :]
        normed_ref[...] = normed.astype(BF16)
        for start, end in tiles(columns):
            product = dot(normed_ref[...], weight_ref[:, start:end], 1, 0)
            qkv_ref[:, start:end] = (product + shift_ref[:, start:end]).astype(BF16)

    shapes = [((length, width), BF16), ((length, columns), BF16)]
    if partials is None:
        normed, qkv = whole_call(kernel, "project_in", shapes, base, vectors, weight, shift)
        return base, normed, qkv
    shapes.append(((length, width), BF16))
    normed, qkv, stream = whole_call(
        kernel,
        "project_in",
        shapes,
        base,
        *partials[0],
        *partials[1],
        partials[2],
        vectors,
        weight,
        shift,
    )
    return stream, normed, qkv


def expand_hidden(stream, own, other, vectors, weight, shift):
    length, width = stream.shape
    columns = weight.shape[1]
    root = 0.7978845608028654

    def kernel(stream_ref, *refs):
        own_refs, other_refs, refs = refs[:PIECES], refs[PIECES : 2 * PIECES], refs[2 * PIECES :]
        vectors_ref, weight_ref, shift_ref, mid_ref, normed_ref, hidden_ref, slope_ref = refs
        middle = stream_ref[...].astype(F32) + join_pieces(own_refs)
        middle = middle + join_pieces(other_refs) + vectors_ref[6:7, :]
        mid_ref[...] = middle
        normed = norm_parts(middle)[0] * vectors_ref[1:2, :] + vectors_ref[3:4, :]
        normed_ref[...] = normed.astype(BF16)
        for start, end in tiles(columns):
            inner = dot(normed_ref[...], weight_ref[:, start:end], 1, 0) + shift_ref[:, start:end]
            square = inner * inner
            half_tanh = 0.5 * jnp.tanh(root * (inner + 0.044715 * square * inner))
            hidden_ref[:, start:end] = (inner * (0.5 + half_tanh)).astype(BF16)
            bend = (0.5 - 2.0 * half_tanh * half_tanh) * (root + 3 * 0.044715 * root * square)
            slope_ref[:, start:end] = (0.5 + half_tanh + inner * bend).astype(BF16)

    return whole_call(
        kernel,
        "expand_hidden",
        [
            ((length, width), F32),
            ((length, width), BF16),
            ((length, columns), BF16),
            ((length, columns), BF16),
        ],
        stream, *own, *other, vectors, weight, shift,
    )


def back_hidden(d_result, weight, slope):
    length, columns = slope.shape

    def kernel(d_ref, weight_ref, slope_ref, out_ref, sums_ref):
        for start, end in tiles(columns):
            d_hidden = dot(d_ref[...], weight_ref[start:end, :], 1, 1)
            d_pre = (d_hidden * slope_ref[:, start:end].astype(F32)).astype(BF16)
            out_ref[:, start:end] = d_pre
            sums_ref[:, start:end] = jnp.sum(d_pre.astype(F32), axis=0, keepdims=True)

    return whole_call(
        kernel,
        "back_hidden",
        [((length, columns), BF16), ((1, columns), F32)],
        d_result, weight, slope,
    )


def back_norm(base, own, other, stream, gain, weight):
    length, width = base.shape

    def kernel(*refs):
        base_ref, *refs = refs
        own_refs, other_refs, refs = refs[:PIECES], refs[PIECES : 2 * PIECES], refs[2 * PIECES :]
        stream_ref, gain_ref, *refs = refs
        unit, inverse = norm_parts(stream_ref[...].astype(F32))
        d_normed = join_pieces(own_refs) + join_pieces(other_refs)
        d_unit = d_normed * gain_ref[...]
        mean_d = jnp.mean(d_unit, axis=-1, keepdims=True)
        mean_du = jnp.mean(d_unit * unit, axis=-1, keepdims=True)
        base_wide = base_ref[...].astype(F32)
        total = base_wide + inverse * (d_unit - mean_d - unit * mean_du)
        if weight is None:
            low_ref, sums_ref = refs
        else:
            weight_ref, low_ref, sums_ref, wide_ref, product_ref = refs
            wide_ref[...] = total
        low_ref[...] = total.astype(BF16)
        sums_ref[0:1, :] = jnp.sum(d_normed * unit, axis=0, keepdims=True)
        sums_ref[1:2, :] = jnp.sum(d_normed, axis=0, keepdims=True)
        sums_ref[2:3, :] = jnp.sum(low_ref[...].astype(F32), axis=0, keepdims=True)
        sums_ref[3:4, :] = jnp.sum(base_wide, axis=0, keepdims=True)
        if weight is not None:
            for start, end in tiles(weight.shape[0]):
                product = dot(low_ref[...], weight_ref[start:end, :], 1, 1)
                product_ref[:, start:end] = product.astype(BF16)

    shapes = [((length, width), BF16), ((4, width), F32)]
    arrays = [base, *own, *other, stream, gain]
    if weight is not None:
        arrays.append(weight)
        shapes += [((length, width), F32), ((length, weight.shape[0]), BF16)]
    return whole_call(kernel, "back_norm", shapes, *arrays)


def column_sums(array):
    return jnp.sum(array.astype(F32), axis=0)


def on_device(
    section_inputs,
    key_mask,
    attention_in,
    attention_out,
    expand_weight,
    contract_weight,
    norm_gains,
    biases,
    expand_bias,
):
    core = lax.axis_index("section")
    here = lax.axis_index("seq")
    line = lax.axis_index("dp")
    count = lax.axis_size("dp")
    first = core == 0
    core_ref = core.astype(jnp.int32).reshape(1)
    place_ref = jnp.stack([core, here]).astype(jnp.int32)

    width = attention_out.shape[2]
    own_rows = attention_out.shape[1]
    half_heads = own_rows // 2
    own_hidden = contract_weight.shape[1]
    half_hidden = round_up(round_up(own_hidden, 2) // 2, 16)
    in_runs = half_runs(3 * count * own_rows, 3 * count, half_heads, half_heads)
    hidden_runs = half_runs(count * own_hidden, count, half_hidden, half_hidden)
    in_width = 3 * count * half_heads
    hidden_width = count * half_hidden

    gate = Order(core)

    def both_layers(keep, send):
        received = swap_cores(send)
        return jnp.where(first, keep, received), jnp.where(first, received, keep)

    def pad_rows(array, step=32):
        extra = round_up(array.shape[-2], step) - array.shape[-2]
        if extra == 0:
            return array
        spec = [(0, 0)] * (array.ndim - 2) + [(0, extra), (0, 0)]
        return jnp.pad(array, spec)

    def prepared(halves):
        quarters = [quarters_of(pad_rows(half)) for half in halves]
        return quarters, [pick(quarter, here) for quarter in quarters]

    def built(own, near, others, rows):
        whole = assemble(own, near, *others)
        whole = whole.reshape(count, -1, whole.shape[3])[:, :rows]
        return whole.reshape(count * rows, whole.shape[2])

    in_own, in_mine = prepared(
        both_layers(*split_columns(attention_in[0], in_runs, in_width, core_ref))
    )
    in_mine, attention_out, expand_weight, contract_weight, norm_gains, biases, expand_bias = gate(
        in_mine, attention_out, expand_weight, contract_weight, norm_gains, biases, expand_bias
    )

    near_in_0 = line_shifts(in_mine[0])
    hidden_shift = jnp.pad(expand_bias[0], (0, 2 * half_hidden - own_hidden))
    packed = jnp.concatenate([norm_gains[0].reshape(-1), biases[0].reshape(-1), hidden_shift])
    packed = both_layers(packed, packed)
    packed_rows = round_up(packed[0].size, width) // width
    out_parts = attention_out[0].reshape(2, half_heads, width)
    out_halves = both_layers(pick(out_parts, core), pick(out_parts, 1 - core))
    out_whole = []
    for half, vector in zip(out_halves, packed):
        vector = jnp.pad(vector, (0, packed_rows * width - vector.size)).reshape(-1, width)
        out_whole.append(pad_rows(jnp.concatenate([half, vector], axis=0)))
    out_0 = lax.all_gather(out_whole[0], "dp", axis=0)
    expand_own, expand_mine = prepared(
        both_layers(*split_columns(expand_weight[0], hidden_runs, hidden_width, core_ref))
    )
    near_expand_0 = line_gather(expand_mine[0])
    near_in_0, expand_mine, out_whole, contract_weight, section_inputs = gate(
        near_in_0, expand_mine, out_whole, contract_weight, section_inputs
    )

    beside_in_0 = spread(near_in_0)
    contract_parts = jnp.pad(
        contract_weight[0], ((0, 2 * half_hidden - own_hidden), (0, 0))
    ).reshape(2, half_hidden, width)
    contract_own, contract_mine = prepared(
        both_layers(pick(contract_parts, core), pick(contract_parts, 1 - core))
    )
    near_contract_0 = line_gather(contract_mine[0])
    beside_in_0, out_0, near_expand_0, contract_mine, in_mine, section_inputs = gate(
        beside_in_0, out_0, near_expand_0, contract_mine, in_mine, section_inputs
    )

    across_in_0 = spread_on(beside_in_0, False)
    micro, images, block, _ = section_inputs.shape[1:]
    tokens = section_inputs[0].reshape(micro * images, block, width)
    pieces = [pick(tokens, here)]
    pieces += [swap_seq(pick(tokens, here ^ bits), bits) for bits in range(1, 4)]
    in_padded = jnp.pad(in_mine[1], ((0, 8), (0, 0)))
    near_in_1 = line_gather(in_padded)[:, : in_mine[1].shape[0]]
    mask = pick(key_mask.reshape(micro * images, 4, block), here)
    mask = jnp.concatenate([pick(mask, here ^ bits) for bits in range(4)])
    hidden_keys = jnp.where(mask > 0, 0.0, 1.0).astype(F32)[:, None]

    def small_of(gathered):
        packed = gathered[:, half_heads : half_heads + packed_rows].reshape(count, -1)
        packed = packed.astype(F32)
        vectors = packed[:, : 8 * own_rows].reshape(count, 8, own_rows)
        hidden = packed[:, 8 * own_rows :][:, : 2 * half_hidden].reshape(count, 2, half_hidden)
        heads_part = pick(vectors.reshape(count, 8, 2, half_heads), core, 2)
        vectors = vectors.transpose(1, 0, 2).reshape(8, width)
        query, value = heads_part[:, 4].reshape(-1), heads_part[:, 5].reshape(-1)
        qkv_shift = jnp.concatenate([query, jnp.zeros_like(query), value])
        hidden_shift = pick(hidden, core, 1).reshape(1, -1)
        return vectors, qkv_shift.reshape(1, -1), hidden_shift

    def heads_of(gathered):
        return gathered[:, :half_heads].reshape(count * half_heads, width)

    vectors_0, qkv_shift_0, hidden_shift_0 = small_of(out_0)
    attn_out_0 = heads_of(out_0)
    pieces, across_in_0, near_expand_0, out_whole, qkv_shift_0 = gate(
        pieces, across_in_0, near_expand_0, out_whole, qkv_shift_0
    )
    beside_expand_0 = spread(near_expand_0)
    image = jnp.concatenate(pieces, axis=0)
    other = swap_cores(image)
    start = jnp.where(first, image, other)
    cotangent = jnp.where(first, other, image)
    attn_in_0 = built(in_own[0], near_in_0, (*beside_in_0, across_in_0), own_rows)
    out_1 = lax.all_gather(out_whole[1], "dp", axis=0)
    beside_expand_0, near_contract_0, start, attn_in_0, hidden_keys, expand_mine = gate(
        beside_expand_0, near_contract_0, start, attn_in_0, hidden_keys, expand_mine
    )

    across_expand_0 = spread_on(beside_expand_0, True)
    beside_contract_0 = spread(near_contract_0)
    near_expand_1 = line_gather(expand_mine[1])
    stream_0, normed_0, qkv_0 = project_in(start, None, vectors_0, attn_in_0, qkv_shift_0)
    mixed_0, lse_0 = attention_forward(qkv_0, hidden_keys)
    own = partial_product(mixed_0, attn_out_0, False, "project_heads")
    across_expand_0, beside_contract_0, contract_mine, own = gate(
        across_expand_0, beside_contract_0, contract_mine, own
    )
    expand_0 = built(expand_own[0], near_expand_0, (*beside_expand_0, across_expand_0), own_rows)
    own, other, expand_0, near_in_1 = gate(own, swap_cores(own), expand_0, near_in_1)

    across_contract_0 = spread_on(beside_contract_0, False)
    beside_in_1 = spread(near_in_1)
    near_contract_1 = line_gather(contract_mine[1])
    middle_0, normed_mid_0, hidden_0, slope_0 = expand_hidden(
        stream_0, own, other, vectors_0, expand_0, hidden_shift_0
    )
    across_contract_0, beside_in_1, near_expand_1, hidden_0 = gate(
        across_contract_0, beside_in_1, near_expand_1, hidden_0
    )

    across_in_1 = spread_on(beside_in_1, True)
    beside_expand_1 = spread(near_expand_1)
    contract_0 = built(
        contract_own[0], near_contract_0, (*beside_contract_0, across_contract_0), half_hidden
    )
    own = partial_product(hidden_0, contract_0, False, "contract_hidden")
    vectors_1, qkv_shift_1, hidden_shift_1 = small_of(out_1)
    attn_out_1 = heads_of(out_1)
    own, across_in_1, beside_expand_1, qkv_shift_1, attn_out_1 = gate(
        own, across_in_1, beside_expand_1, qkv_shift_1, attn_out_1
    )
    attn_in_1 = built(in_own[1], near_in_1, (*beside_in_1, across_in_1), own_rows)
    own, other, attn_in_1, near_contract_1 = gate(own, swap_cores(own), attn_in_1, near_contract_1)

    across_expand_1 = spread_on(beside_expand_1, False)
    beside_contract_1 = spread(near_contract_1)
    partials = (own, other, vectors_0[7:8])
    stream_1, normed_1, qkv_1 = project_in(middle_0, partials, vectors_1, attn_in_1, qkv_shift_1)
    mixed_1, lse_1 = attention_forward(qkv_1, hidden_keys)
    own = partial_product(mixed_1, attn_out_1, False, "project_heads")
    across_expand_1, beside_contract_1, own = gate(across_expand_1, beside_contract_1, own)
    expand_1 = built(expand_own[1], near_expand_1, (*beside_expand_1, across_expand_1), own_rows)
    own, other, expand_1 = gate(own, swap_cores(own), expand_1)

    across_contract_1 = spread_on(beside_contract_1, True)
    middle_1, normed_mid_1, hidden_1, slope_1 = expand_hidden(
        stream_1, own, other, vectors_1, expand_1, hidden_shift_1
    )
    hidden_1, across_contract_1, cotangent = gate(hidden_1, across_contract_1, cotangent)
    contract_1 = built(
        contract_own[1], near_contract_1, (*beside_contract_1, across_contract_1), half_hidden
    )

    def rows_of(pieces, rows, total):
        mine, other = jnp.stack(pieces, axis=1)
        if 4 * mine.shape[1] == rows:
            return join_rows(mine, other, total, place_ref)
        halves = [jnp.where(first, mine, other), jnp.where(first, other, mine)]
        halves = [in_order(half).reshape(-1, width)[:rows] for half in halves]
        return jnp.concatenate(halves, axis=0).astype(F32)[:total]

    def columns_of(pieces, runs, total, place):
        mine, other = jnp.stack(pieces, axis=1)
        return join_columns(mine, other, runs, total, place)[:own_rows]

    contract_sum_1 = Sum(hidden_1, cotangent, count, True)
    gate.sent(contract_sum_1)
    contract_sum_1.first()
    own_out = partial_product(hidden_1, contract_1, False, "contract_hidden")
    d_pre_1, hidden_sums_1 = back_hidden(cotangent, contract_1, slope_1)
    d_pre_1 = gate(d_pre_1)
    expand_sum_1 = Sum(normed_mid_1, d_pre_1, count, False)
    gate.sent(expand_sum_1)
    expand_sum_1.first()
    own = partial_product(d_pre_1, expand_1, True, "back_expand")
    own, other, other_out = gate(own, swap_cores(own), swap_cores(own_out))
    own_out, other_out = jnp.concatenate(own_out, axis=1), jnp.concatenate(other_out, axis=1)
    output = middle_1 + own_out.astype(F32) + other_out.astype(F32) + vectors_1[7:8]
    output = output.astype(BF16)
    d_branch_1, mid_sums_1, d_middle_1, d_mixed_1 = back_norm(
        cotangent, own, other, middle_1, vectors_1[1:2], attn_out_1
    )
    d_branch_1, d_mixed_1 = gate(d_branch_1, d_mixed_1)
    out_grad_1 = gate(plain_grad(mixed_1, d_branch_1))
    out_line_1 = lax.psum_scatter(out_grad_1, "dp", scatter_dimension=0, tiled=True)
    gate.arrived(contract_sum_1)
    contract_sum_1.add()
    gate.sent(contract_sum_1)
    contract_sum_1.second()
    d_qkv_1 = attention_backward(qkv_1, gate(d_mixed_1), lse_1, hidden_keys)
    d_qkv_1 = gate(d_qkv_1)
    in_sum_1 = Sum(normed_1, d_qkv_1, count, False)
    gate.sent(in_sum_1)
    in_sum_1.first()
    gate.arrived(expand_sum_1)
    expand_sum_1.add()
    gate.sent(expand_sum_1)
    expand_sum_1.second()
    own = partial_product(gate(d_qkv_1), attn_in_1, True, "back_in")
    gate.arrived(contract_sum_1)
    own = gate(own)
    own, other, output = gate(own, swap_cores(own), output)
    d_result_0, in_sums_1 = back_norm(d_middle_1, own, other, stream_1, vectors_1[0:1], None)
    d_result_0 = gate(d_result_0)
    contract_sum_0 = Sum(hidden_0, d_result_0, count, True)
    gate.sent(contract_sum_0)
    contract_sum_0.first()
    contract_sum_1.over_line(gate)
    d_pre_0, hidden_sums_0 = back_hidden(gate(d_result_0), contract_0, slope_0)
    d_pre_0 = gate(d_pre_0)
    expand_sum_0 = Sum(normed_mid_0, d_pre_0, count, False)
    gate.sent(expand_sum_0)
    gate.arrived(expand_sum_1)
    expand_sum_0.first()
    expand_sum_1.over_line(gate)
    own = partial_product(gate(d_pre_0), expand_0, True, "back_expand")
    gate.arrived(in_sum_1)
    in_sum_1.add()
    gate.sent(in_sum_1)
    own = gate(own)
    own, other, out_line_1 = gate(own, swap_cores(own), out_line_1)
    in_sum_1.second()
    d_branch_0, mid_sums_0, d_middle_0, d_mixed_0 = back_norm(
        d_result_0, own, other, middle_0, vectors_0[1:2], attn_out_0
    )
    d_branch_0, d_mixed_0 = gate(d_branch_0, d_mixed_0)
    out_grad_0 = gate(plain_grad(mixed_0, d_branch_0))
    out_line_0 = lax.psum_scatter(out_grad_0, "dp", scatter_dimension=0, tiled=True)
    gate.summed(contract_sum_1)
    d_qkv_0 = gate(attention_backward(qkv_0, gate(d_mixed_0), lse_0, hidden_keys))
    gate.arrived(contract_sum_0)
    contract_sum_0.add()
    gate.sent(contract_sum_0)
    contract_sum_0.second()
    cut = round_up(in_width // 2, 128)
    in_sums_a = Sum(normed_0, gate(d_qkv_0), count, True, (0, cut))
    gate.sent(in_sums_a)
    gate.arrived(in_sum_1)
    in_sums_a.first()
    in_sum_1.over_line(gate)
    in_sums_b = Sum(normed_0, gate(d_qkv_0), count, False, (cut, in_width))
    gate.sent(in_sums_b)
    gate.arrived(expand_sum_0)
    in_sums_b.first()
    expand_sum_0.add()
    gate.sent(expand_sum_0)
    own = partial_product(gate(d_qkv_0), attn_in_0, True, "back_in")
    own = gate(own)
    gate.summed(expand_sum_1)
    gate.arrived(contract_sum_0)
    own, other = gate(own, swap_cores(own))
    expand_sum_0.second()
    contract_sum_0.over_line(gate)
    d_input_0, in_sums_0 = back_norm(d_middle_0, gate(own), other, stream_0, vectors_0[0:1], None)
    d_input_0 = gate(d_input_0)
    gate.arrived(in_sums_a, in_sums_b)
    in_sums_a.add()
    in_sums_b.add()
    gate.sent(in_sums_a, in_sums_b)
    in_sums_a.second()
    in_sums_b.second()
    gate.summed(in_sum_1)
    gate.arrived(expand_sum_0)
    expand_sum_0.over_line(gate)

    def own_layer(low, high):
        return jnp.stack([jnp.where(first, low, high), swap_cores(jnp.where(first, high, low))])

    out_line_0 = gate(out_line_0)
    out_near = gate(own_layer(out_line_0, out_line_1))
    gate.arrived(in_sums_a, in_sums_b)
    in_sums_a.over_line_shifts()
    in_sums_b.over_line_shifts()
    gate.summed(contract_sum_0)
    contract_near = gate(own_layer(contract_sum_0.line, contract_sum_1.line))
    contract_beside = gate(spread(contract_near))
    contract_across = spread_on(contract_beside, True)
    out_moved = swap_seq(out_near, 2)
    gate.summed(in_sums_a, in_sums_b)
    contract_across, out_moved = gate(contract_across, out_moved)
    out_near = add_low(out_near, out_moved)
    in_line_0 = jnp.concatenate([in_sums_a.line, in_sums_b.line], axis=1)
    in_near = gate(own_layer(in_line_0, in_sum_1.line))
    in_beside = spread(in_near)
    grad_contract = rows_of(
        [contract_near, *contract_beside, contract_across], half_hidden, own_hidden
    )
    gate.summed(expand_sum_0)
    expand_near = gate(own_layer(expand_sum_0.line, expand_sum_1.line))
    in_beside, grad_contract = gate(in_beside, grad_contract)
    in_across = spread_on(in_beside, True)
    expand_beside = spread(expand_near)
    in_across, expand_beside = gate(in_across, expand_beside)
    expand_across = spread_on(expand_beside, False)
    out_moved = swap_seq(out_near, 1)
    last_place = jnp.stack([gate.token, here]).astype(jnp.int32)
    grad_in = columns_of([in_near, *in_beside, in_across], in_runs, 3 * width, last_place)
    expand_across, out_moved, grad_in = gate(expand_across, out_moved, grad_in)
    out_near = add_low(out_near, out_moved).astype(F32)
    grad_out = jnp.concatenate(
        [jnp.where(first, out_near[0], out_near[1]), jnp.where(first, out_near[1], out_near[0])]
    )
    last_place = jnp.stack([gate.token, here]).astype(jnp.int32)
    grad_expand = columns_of(
        [expand_near, *expand_beside, expand_across],
        hidden_runs,
        count * own_hidden,
        last_place,
    )

    def small_sums(in_sums, mid_sums, hidden_sums, d_qkv):
        heads = column_sums(d_qkv).reshape(3, -1)
        shared = jnp.stack(
            [in_sums[0], mid_sums[0], in_sums[1], mid_sums[1], mid_sums[2], mid_sums[3]]
        )
        return shared, heads[0], heads[2], hidden_sums[0]

    small_0 = small_sums(in_sums_0, mid_sums_0, hidden_sums_0, d_qkv_0)
    small_1 = small_sums(in_sums_1, mid_sums_1, hidden_sums_1, d_qkv_1)

    def pack_small(small):
        shared, query, value, hidden = small
        shared = jnp.where(first, shared, 0.0)
        none = jnp.zeros((count, half_heads), F32)

        def spread(vector, size):
            vector = vector.reshape(count, size)
            nothing = jnp.zeros_like(vector)
            return jnp.concatenate(
                [jnp.where(first, vector, nothing), jnp.where(first, nothing, vector)], axis=1
            )

        shared = shared.reshape(6, count, own_rows)
        return jnp.concatenate(
            [
                shared[0],
                shared[1],
                shared[2],
                shared[3],
                spread(query, half_heads),
                spread(value, half_heads),
                shared[4],
                shared[5],
                spread(hidden, half_hidden),
            ],
            axis=1,
        )

    low_sums, high_sums = pack_small(small_0), pack_small(small_1)
    sums = jnp.where(first, low_sums, high_sums)
    sums = sums + swap_cores(jnp.where(first, high_sums, low_sums))
    sums = sums + swap_seq(sums, 1)
    sums = sums + swap_seq(sums, 2)
    total = pick(sums, line)
    for step in range(1, count):
        total = total + lax.ppermute(
            pick(sums, lax.rem(line + step, count)),
            "dp",
            [(source, (source + step) % count) for source in range(count)],
        )
    sums = total

    result = jnp.where(first, d_input_0, output).reshape(4, block, width)
    returned = jnp.stack([result[0]] + [swap_seq(result[bits], bits) for bits in range(1, 4)])
    results = in_order(returned).astype(F32).reshape(1, micro, images, block, width)

    return (
        results,
        grad_in[None],
        grad_out[None],
        grad_expand[None],
        grad_contract[None],
        sums[: 2 * own_rows].reshape(1, 2, own_rows),
        sums[2 * own_rows : 8 * own_rows].reshape(1, 6, own_rows),
        sums[8 * own_rows : 8 * own_rows + own_hidden][None],
    )


def plain_passed_along(value, axis, steps):
    count = lax.axis_size(axis)
    initial, last = (max(0, -steps), min(count, count - steps))
    return lax.ppermute(value, axis, [(source, source + steps) for source in range(initial, last)])


def plain_layer_norm(stream, gain, shift):
    centre = jnp.mean(stream, axis=-1, keepdims=True)
    offset = stream - centre
    spread = jnp.mean(offset * offset, axis=-1, keepdims=True)
    return offset * lax.rsqrt(spread + 1e-06) * gain + shift


def plain_matmul(left, right):
    return jnp.dot(left, right, preferred_element_type=F32)


def plain_left_matmul(left, right):
    return lax.dot_general(
        left, right, (((0,), (0,)), ((), ())), preferred_element_type=F32
    )


def plain_right_matmul(left, right):
    return lax.dot_general(
        left, right, (((1,), (1,)), ((), ())), preferred_element_type=F32
    )


def plain_gather_once(local):
    whole = (
        lax.all_gather(local[0], "dp", axis=1, tiled=True),
        lax.all_gather(local[1], "dp", axis=1, tiled=True),
        lax.all_gather(local[2], "dp", axis=1, tiled=True),
        lax.all_gather(local[3], "dp", axis=1, tiled=True),
        lax.all_gather(local[4], "dp", axis=2, tiled=True),
        lax.all_gather(local[5], "dp", axis=2, tiled=True),
        lax.all_gather(local[6], "dp", axis=1, tiled=True),
    )
    return tuple((piece[0] for piece in whole))


def plain_split_heads(heads):
    images, length, _, width = heads.shape
    count = width // HEAD_DIM
    queries = heads[:, :, 0].reshape(images, length, count, HEAD_DIM)
    key_rows = heads[:, :, 1].reshape(images, length, count, HEAD_DIM)
    value_rows = heads[:, :, 2].reshape(images, length, count, HEAD_DIM)
    return (queries, key_rows, value_rows)


def plain_head_scores(queries, key_rows, visible):
    scores = jnp.einsum(
        "nqhd,nkhd->nhqk", queries, key_rows, preferred_element_type=F32
    ) * HEAD_DIM ** (-0.5)
    return jnp.where(visible[:, None, None, :], scores, -1000000000.0)


def plain_attend(heads, visible):
    images, length, _, width = heads.shape
    queries, key_rows, value_rows = plain_split_heads(heads)
    scores = plain_head_scores(queries, key_rows, visible)
    row_max = jnp.max(scores, axis=-1, keepdims=True)
    expon = jnp.exp(scores - row_max)
    total = jnp.sum(expon, axis=-1, keepdims=True)
    softmaxed = (expon / total).astype(BF16)
    log_total = (row_max + jnp.log(total))[..., 0]
    mixture = jnp.einsum(
        "nhqk,nkhd->nqhd", softmaxed, value_rows, preferred_element_type=F32
    )
    return (mixture.astype(BF16).reshape(images, length, width), log_total)


def plain_attend_back(heads, log_total, visible, d_mixture):
    images, length, _, width = heads.shape
    queries, key_rows, value_rows = plain_split_heads(heads)
    d_rows = d_mixture.reshape(queries.shape)
    scores = plain_head_scores(queries, key_rows, visible)
    softmaxed = jnp.exp(scores - log_total[..., None])
    d_soft = jnp.einsum("nqhd,nkhd->nhqk", d_rows, value_rows, preferred_element_type=F32)
    inner = jnp.sum(softmaxed * d_soft, axis=-1, keepdims=True)
    d_scores = (softmaxed * (d_soft - inner)).astype(BF16)
    scale = HEAD_DIM ** (-0.5)
    d_queries = (
        jnp.einsum("nhqk,nkhd->nqhd", d_scores, key_rows, preferred_element_type=F32)
        * scale
    ).astype(BF16)
    d_keys = (
        jnp.einsum("nhqk,nqhd->nkhd", d_scores, queries, preferred_element_type=F32) * scale
    ).astype(BF16)
    d_values = jnp.einsum(
        "nhqk,nqhd->nkhd",
        softmaxed.astype(BF16),
        d_rows,
        preferred_element_type=F32,
    ).astype(BF16)
    return jnp.stack([d_queries, d_keys, d_values], axis=2).reshape(images, length, 3, width)


def plain_forward_layer(stream_in, visible, params):
    attn_in, attn_out, expand, contract, gains, shifts, expand_shift = params
    images, rows_seq, width = stream_in.shape
    stream = stream_in.astype(F32).reshape(-1, width)
    gains32 = gains.astype(F32)
    shifts32 = shifts.astype(F32)
    normed = plain_layer_norm(stream, gains32[0], shifts32[0]).astype(BF16)
    qkv_shift = jnp.stack([shifts32[2], jnp.zeros_like(shifts32[2]), shifts32[3]])
    projected = (plain_matmul(normed, attn_in).reshape(images, rows_seq, 3, width) + qkv_shift).astype(
        BF16
    )
    heads = lax.all_to_all(projected, "seq", split_axis=3, concat_axis=1, tiled=True)
    mixture, log_total = plain_attend(heads, visible)
    mixed_rows = lax.all_to_all(mixture, "seq", split_axis=1, concat_axis=2, tiled=True).reshape(
        -1, width
    )
    middle = stream + plain_matmul(mixed_rows, attn_out) + shifts32[4]
    normed_mid = plain_layer_norm(middle, gains32[1], shifts32[1]).astype(BF16)
    hidden_pre = plain_matmul(normed_mid, expand) + expand_shift.astype(F32)
    hidden = jax.nn.gelu(hidden_pre, approximate=True).astype(BF16)
    result = middle + plain_matmul(hidden, contract) + shifts32[5]
    saved = (
        stream_in,
        normed,
        heads,
        log_total,
        mixed_rows,
        middle,
        normed_mid,
        hidden_pre,
        hidden,
        visible,
    )
    return (result.reshape(images, rows_seq, width), saved)


def plain_backward_layer(d_result, saved, params):
    attn_in, attn_out, expand, contract, gains, shifts, expand_shift = params
    (
        stream_in,
        normed,
        heads,
        log_total,
        mixed_rows,
        middle,
        normed_mid,
        hidden_pre,
        hidden,
        visible,
    ) = saved
    images, rows_seq, width = d_result.shape
    gains32 = gains.astype(F32)
    shifts32 = shifts.astype(F32)
    d_flat = d_result.reshape(-1, width)
    d_wide = d_flat.astype(F32)
    grad_contract = plain_left_matmul(hidden, d_flat)
    grad_last_bias = jnp.sum(d_wide, axis=0)
    d_hidden = plain_right_matmul(d_flat, contract)
    _, gelu_back = jax.vjp(lambda inner: jax.nn.gelu(inner, approximate=True), hidden_pre)
    d_pre = gelu_back(d_hidden)[0].astype(BF16)
    grad_expand = plain_left_matmul(normed_mid, d_pre)
    grad_expand_bias = jnp.sum(d_pre.astype(F32), axis=0)
    d_normed_mid = plain_right_matmul(d_pre, expand)
    _, norm_back_mid = jax.vjp(plain_layer_norm, middle, gains32[1], shifts32[1])
    d_middle_part, grad_gain_mid, grad_shift_mid = norm_back_mid(d_normed_mid)
    d_middle = d_wide + d_middle_part
    d_branch = d_middle.astype(BF16)
    grad_out_bias = jnp.sum(d_branch.astype(F32), axis=0)
    grad_attn_out = plain_left_matmul(mixed_rows, d_branch)
    d_mixture = (
        plain_right_matmul(d_branch, attn_out).astype(BF16).reshape(images, rows_seq, width)
    )
    d_heads = lax.all_to_all(d_mixture, "seq", split_axis=2, concat_axis=1, tiled=True)
    d_projected_heads = plain_attend_back(heads, log_total, visible, d_heads)
    d_projected = lax.all_to_all(
        d_projected_heads, "seq", split_axis=1, concat_axis=3, tiled=True
    ).reshape(-1, 3 * width)
    grad_attn_in = plain_left_matmul(normed, d_projected)
    column_sums = jnp.sum(d_projected.astype(F32), axis=0).reshape(3, width)
    d_normed = plain_right_matmul(d_projected, attn_in)
    stream = stream_in.astype(F32).reshape(-1, width)
    _, norm_back_in = jax.vjp(plain_layer_norm, stream, gains32[0], shifts32[0])
    d_stream_part, grad_gain_in, grad_shift_in = norm_back_in(d_normed)
    d_stream = d_middle + d_stream_part
    grad_gains = jnp.stack([grad_gain_in, grad_gain_mid])
    grad_shifts = jnp.stack(
        [
            grad_shift_in,
            grad_shift_mid,
            column_sums[0],
            column_sums[2],
            grad_out_bias,
            grad_last_bias,
        ]
    )
    grads = (
        grad_attn_in,
        grad_attn_out,
        grad_expand,
        grad_contract,
        grad_gains,
        grad_shifts,
        grad_expand_bias,
    )
    return (d_stream.reshape(images, rows_seq, width), grads)


def plain_send_forward(values):
    return plain_passed_along(values, "section", 1)


def plain_send_backward(values):
    return plain_passed_along(values, "section", -1)


def on_device_any(
    section_inputs,
    key_mask,
    attention_in,
    attention_out,
    expand_weight,
    contract_weight,
    norm_gains,
    biases,
    expand_bias,
):
    micro = section_inputs.shape[1]
    leading = lax.axis_index("section") == 0
    local = (
        attention_in,
        attention_out,
        expand_weight,
        contract_weight,
        norm_gains,
        biases,
        expand_bias,
    )
    sources = section_inputs[0]
    visible_all = key_mask > 0
    blank = jnp.zeros_like(sources[0])
    recv_forward = blank
    recv_backward = blank
    saves = {}
    outputs = [None] * micro
    input_grads = [None] * micro
    totals = None
    params = plain_gather_once(local)
    for tick in range(micro + 2):
        if tick <= micro:
            source = sources[tick] if tick < micro else blank
            stream_now = jnp.where(leading, source, recv_forward)
            visible_now = jnp.where(
                leading, visible_all[min(tick, micro - 1)], visible_all[max(tick - 1, 0)]
            )
            result, saved = plain_forward_layer(stream_now, visible_now, params)
            saves[tick] = saved
            if tick >= 1:
                outputs[tick - 1] = result
            sent_forward = plain_send_forward(result.astype(BF16))
        if tick >= 1:
            early = saves[tick - 2] if tick - 2 in saves else saves[tick]
            later = saves[tick] if tick in saves else saves[tick - 2]
            chosen = jax.tree.map(
                lambda left_one, right_one: jnp.where(leading, left_one, right_one), early, later
            )
            cotangent = sources[tick - 1] if tick <= micro else blank
            d_result = jnp.where(leading, recv_backward, cotangent)
            d_stream, grads = plain_backward_layer(d_result, chosen, params)
            active = jnp.where(leading, tick >= 2, tick <= micro)
            grads = tuple((jnp.where(active, piece, 0.0) for piece in grads))
            if tick >= 2:
                input_grads[tick - 2] = d_stream
            totals = (
                grads if totals is None else tuple((old + new for old, new in zip(totals, grads)))
            )
            recv_backward = plain_send_backward(d_stream.astype(BF16))
        if tick <= micro:
            recv_forward = sent_forward
    totals = (
        lax.psum_scatter(
            totals[0].astype(BF16), "dp", scatter_dimension=0, tiled=True
        ).astype(F32),
        lax.psum_scatter(
            totals[1].astype(BF16), "dp", scatter_dimension=0, tiled=True
        ).astype(F32),
        lax.psum_scatter(
            totals[2].astype(BF16), "dp", scatter_dimension=0, tiled=True
        ).astype(F32),
        lax.psum_scatter(
            totals[3].astype(BF16), "dp", scatter_dimension=0, tiled=True
        ).astype(F32),
        lax.psum_scatter(
            totals[4].astype(BF16), "dp", scatter_dimension=1, tiled=True
        ).astype(F32),
        lax.psum_scatter(
            totals[5].astype(BF16), "dp", scatter_dimension=1, tiled=True
        ).astype(F32),
        lax.psum_scatter(
            totals[6].astype(BF16), "dp", scatter_dimension=0, tiled=True
        ).astype(F32),
    )
    totals = (
        lax.psum(totals[0].astype(BF16), "seq").astype(F32),
        lax.psum(totals[1].astype(BF16), "seq").astype(F32),
        lax.psum(totals[2].astype(BF16), "seq").astype(F32),
        lax.psum(totals[3].astype(BF16), "seq").astype(F32),
        lax.psum(totals[4].astype(BF16), "seq").astype(F32),
        lax.psum(totals[5].astype(BF16), "seq").astype(F32),
        lax.psum(totals[6].astype(BF16), "seq").astype(F32),
    )
    results = jnp.stack(
        [jnp.where(leading, input_grads[index], outputs[index]) for index in range(micro)]
    )[None]
    return (
        results,
        totals[0][None],
        totals[1][None],
        totals[2][None],
        totals[3][None],
        totals[4][None],
        totals[5][None],
        totals[6][None],
    )


def solution(mesh):
    in_specs = (
        P("section", None, "dp", "seq", None),
        P(None, "dp", None),
        P("section", "dp", None),
        P("section", "dp", None),
        P("section", "dp", None),
        P("section", "dp", None),
        P("section", None, "dp"),
        P("section", None, "dp"),
        P("section", "dp"),
    )
    out_specs = (
        P("section", None, "dp", "seq", None),
        P("section", "dp", None),
        P("section", "dp", None),
        P("section", "dp", None),
        P("section", "dp", None),
        P("section", None, "dp"),
        P("section", None, "dp"),
        P("section", "dp"),
    )

    def by_size(section_inputs, *others):
        _, micro, images, _, _ = section_inputs.shape
        one_image_each = micro * images == lax.axis_size("seq") == 4
        plan = on_device if one_image_each else on_device_any
        return plan(section_inputs, *others)

    return jax.shard_map(
        by_size, mesh=mesh, in_specs=in_specs, out_specs=out_specs, check_vma=False
    )
```

```python
import jax
import jax.numpy as jnp
from jax import lax
from jax.experimental import pallas as pl
from jax.experimental.pallas import tpu as pltpu
from jax.sharding import PartitionSpec as P

HEAD_DIM = 72
SCALE = HEAD_DIM**-0.5
VMEM_LIMIT = 32 * 1024 * 1024
F32 = jnp.float32
BF16 = jnp.bfloat16
LIGHT = pl.CostEstimate(flops=1, bytes_accessed=1, transcendentals=0)


def round_up(value, step):
    return -(-value // step) * step


def pick(array, index, axis=0):
    return lax.dynamic_index_in_dim(array, index, axis, keepdims=False)


def swap_cores(value):
    swap = [(0, 1), (1, 0)]
    return jax.tree.map(lambda array: lax.ppermute(array, "section", swap), value)


def swap_seq(value, bits):
    bits = bits if isinstance(bits, tuple) else (bits, bits)
    count = lax.axis_size("seq")
    pairs = [
        (core * count + index, core * count + (index ^ bits[core]))
        for core in range(2)
        for index in range(count)
        if bits[core]
    ]
    return lax.ppermute(value, ("section", "seq"), pairs)


FIRST, SECOND = (1, 2), (2, 1)


def relative_bits():
    core = lax.axis_index("section")
    return (0, 1 + core, 2 - core, 3)


def dot(left, right, left_axis, right_axis):
    return lax.dot_general(
        left, right, (((left_axis,), (right_axis,)), ((), ())), preferred_element_type=F32
    )


def params_of(limit=VMEM_LIMIT):
    return pltpu.CompilerParams(vmem_limit_bytes=limit)


def whole_vmem(count):
    return [pl.BlockSpec(memory_space=pltpu.VMEM)] * count


def half_runs(total, parts, half, width):
    size = total // parts
    runs = [[], []]
    for part in range(parts):
        runs[0].append((part * size, half, part * width))
        runs[1].append((part * size + half, size - half, part * width))
    return runs


def split_columns(weight, runs, width, core):
    rows = weight.shape[0]

    def kernel(core_ref, whole_ref, keep_ref, send_ref):
        def write(ref, pieces):
            if sum(size for _, size, _ in pieces) < width:
                ref[...] = jnp.zeros_like(ref)
            for start, size, place in pieces:
                ref[:, place : place + size] = whole_ref[:, start : start + size]

        @pl.when(core_ref[0] == 0)
        def _():
            write(keep_ref, runs[0])
            write(send_ref, runs[1])

        @pl.when(core_ref[0] == 1)
        def _():
            write(keep_ref, runs[1])
            write(send_ref, runs[0])

    shape = jax.ShapeDtypeStruct((rows, width), weight.dtype)
    return pl.pallas_call(
        kernel,
        out_shape=(shape, shape),
        in_specs=[pl.BlockSpec(memory_space=pltpu.SMEM)] + whole_vmem(1),
        out_specs=tuple(whole_vmem(2)),
        compiler_params=params_of(),
        cost_estimate=LIGHT,
        name="split_columns",
    )(core, weight)


def join_columns(mine, other, runs, total, place):
    count, rows, width = mine.shape

    def kernel(place_ref, mine_ref, other_ref, out_ref):
        def write(first, second):
            for ref, pieces in ((first, runs[0]), (second, runs[1])):
                for start, size, at in pieces:
                    out_ref[0, :, start : start + size] = ref[0, :, at : at + size].astype(F32)

        @pl.when(place_ref[0] == 0)
        def _():
            write(mine_ref, other_ref)

        @pl.when(place_ref[0] == 1)
        def _():
            write(other_ref, mine_ref)

    block = pl.BlockSpec((1, rows, width), lambda j, place: (j, 0, 0))
    out = pl.pallas_call(
        kernel,
        out_shape=jax.ShapeDtypeStruct((count, rows, total), F32),
        grid_spec=pltpu.PrefetchScalarGridSpec(
            num_scalar_prefetch=1,
            grid=(count,),
            in_specs=[block, block],
            out_specs=pl.BlockSpec((1, rows, total), lambda j, place: (place[1 + j], 0, 0)),
        ),
        compiler_params=params_of(),
        cost_estimate=LIGHT,
        name="join_columns",
    )(place, mine, other)
    return out.reshape(count * rows, total)


def join_rows(mine, other, total, place):
    count, rows, width = mine.shape

    def kernel(place_ref, mine_ref, other_ref, out_ref):
        half = pl.program_id(0) // count

        @pl.when(half == place_ref[0])
        def _():
            out_ref[:, 0, :] = mine_ref[0].astype(F32)

        @pl.when(half != place_ref[0])
        def _():
            out_ref[:, 0, :] = other_ref[0].astype(F32)

    def quarter(step):
        return lax.rem(step, count)

    return pl.pallas_call(
        kernel,
        out_shape=jax.ShapeDtypeStruct((total, 1, width), F32),
        grid_spec=pltpu.PrefetchScalarGridSpec(
            num_scalar_prefetch=1,
            grid=(2 * count,),
            in_specs=[
                pl.BlockSpec((1, rows, width), lambda t, place: (quarter(t), 0, 0)),
                pl.BlockSpec((1, rows, width), lambda t, place: (quarter(t), 0, 0)),
            ],
            out_specs=pl.BlockSpec(
                (rows, 1, width),
                lambda t, place: (lax.div(t, count) * count + place[1 + quarter(t)], 0, 0),
            ),
        ),
        compiler_params=params_of(),
        cost_estimate=LIGHT,
        name="join_rows",
    )(place, mine, other)


def assemble(own, near, first, second, across):
    parts, rows, columns = near.shape
    count = parts + 1
    here = lax.axis_index("seq")
    place = [lax.axis_index("dp")] + [here ^ bits for bits in relative_bits()]
    place = jnp.stack(place).astype(jnp.int32)

    def kernel(place_ref, own_ref, near_ref, first_ref, second_ref, across_ref, out_ref, sem):
        along = place_ref[0]
        copies = [pltpu.make_async_copy(own_ref, out_ref.at[along], sem.at[0])]
        for step in range(parts):
            there = lax.rem(along + step + 1, count)
            for index, ref in enumerate((near_ref, first_ref, second_ref, across_ref)):
                copies.append(
                    pltpu.make_async_copy(
                        ref.at[step], out_ref.at[there, place_ref[1 + index]], sem.at[len(copies)]
                    )
                )
        for copy in copies:
            copy.start()
        for copy in copies:
            copy.wait()

    return pl.pallas_call(
        kernel,
        out_shape=jax.ShapeDtypeStruct((count, 4, rows, columns), own.dtype),
        in_specs=[pl.BlockSpec(memory_space=pltpu.SMEM)]
        + [pl.BlockSpec(memory_space=pl.ANY)] * 5,
        out_specs=pl.BlockSpec(memory_space=pltpu.VMEM),
        scratch_shapes=[pltpu.SemaphoreType.DMA((1 + 4 * parts,))],
        compiler_params=params_of(),
        cost_estimate=LIGHT,
        name="assemble",
    )(place, own, near, first, second, across)


def line_shifts(value):
    count = lax.axis_size("dp")
    return [
        lax.ppermute(value, "dp", [((to + step) % count, to) for to in range(count)])
        for step in range(1, count)
    ]


def line_gather(value):
    count = lax.axis_size("dp")
    line = lax.all_gather(value, "dp", axis=0)
    return lax.dynamic_slice_in_dim(
        jnp.concatenate([line, line], 0), lax.axis_index("dp") + 1, count - 1, 0
    )


def quarters_of(shard):
    return shard.reshape(4, shard.shape[0] // 4, shard.shape[1])


def spread(near):
    return swap_seq(near, FIRST), swap_seq(near, SECOND)


def spread_on(neighbours):
    return swap_seq(neighbours[1], FIRST)


def bits_of_place():
    core, here = lax.axis_index("section"), lax.axis_index("seq")
    x, y = lax.rem(here, 2), lax.div(here, 2)
    first, second = jnp.where(core == 0, x, y), jnp.where(core == 0, y, x)
    return jnp.stack([core, first, second]).astype(jnp.int32)


def grad_halves(left, right, count):
    length, depth = left.shape
    columns = right.shape[1]
    rows = depth // count
    quarter = round_up(rows, 32) // 4

    def kernel(bits_ref, left_ref, right_ref, keep_ref, send_ref, turned):
        block = pl.program_id(0)

        @pl.when(block == 0)
        def _():
            turned[...] = left_ref[...].astype(F32).T.astype(BF16).reshape(turned.shape)

        grad = dot(turned[block], right_ref[...], 1, 0)
        if 4 * quarter > rows:
            empty = jnp.zeros((4 * quarter - rows, columns), F32)
            grad = jnp.concatenate([grad, empty], axis=0)
        for at in range(4):
            part = grad[at * quarter : (at + 1) * quarter].astype(BF16)
            x, y = at % 2, at // 2
            first = jnp.where(bits_ref[0] == 0, x, y)
            second = jnp.where(bits_ref[0] == 0, y, x)

            @pl.when(first == bits_ref[1])
            def _():
                keep_ref[0, second] = part

            @pl.when(first != bits_ref[1])
            def _():
                send_ref[0, second] = part

    out = pl.BlockSpec((1, 2, quarter, columns), lambda z, bits: (z, 0, 0, 0))
    shape = jax.ShapeDtypeStruct((count, 2, quarter, columns), BF16)
    return pl.pallas_call(
        kernel,
        out_shape=(shape, shape),
        grid_spec=pltpu.PrefetchScalarGridSpec(
            num_scalar_prefetch=1,
            grid=(count,),
            in_specs=[
                pl.BlockSpec((length, depth), lambda z, bits: (0, 0)),
                pl.BlockSpec((length, columns), lambda z, bits: (0, 0)),
            ],
            out_specs=(out, out),
            scratch_shapes=[pltpu.VMEM((count, rows, length), BF16)],
        ),
        compiler_params=params_of(),
        cost_estimate=LIGHT,
        name="grad_halves",
    )(bits_of_place(), left, right)


def add_half(held, moved):
    count, _, rows, columns = held.shape

    def kernel(bits_ref, held_ref, moved_ref, keep_ref, send_ref):
        def total(index):
            return (held_ref[0, index].astype(F32) + moved_ref[0, index].astype(F32)).astype(BF16)

        keep_ref[0] = total(bits_ref[2])
        send_ref[0] = total(1 - bits_ref[2])

    both = pl.BlockSpec((1, 2, rows, columns), lambda z, bits: (z, 0, 0, 0))
    out = pl.BlockSpec((1, rows, columns), lambda z, bits: (z, 0, 0))
    shape = jax.ShapeDtypeStruct((count, rows, columns), BF16)
    return pl.pallas_call(
        kernel,
        out_shape=(shape, shape),
        grid_spec=pltpu.PrefetchScalarGridSpec(
            num_scalar_prefetch=1, grid=(count,), in_specs=[both, both], out_specs=(out, out)
        ),
        compiler_params=params_of(),
        cost_estimate=LIGHT,
        name="add_half",
    )(bits_of_place(), held, moved)


def add_low(left, right):
    return (left.astype(F32) + right.astype(F32)).astype(BF16)


class Sum:
    def __init__(self, left, right, count):
        self.keep, self.send = grad_halves(left, right, count)

    def first(self):
        self.moved = swap_seq(self.send, FIRST)

    def add(self):
        self.keep, self.send = add_half(self.keep, self.moved)

    def second(self):
        self.moved = swap_seq(self.send, SECOND)

    def over_line(self, gate):
        part = gate(add_low(self.keep, self.moved))
        self.line = lax.psum_scatter(part, "dp", scatter_dimension=0, tiled=True)[0]


def line_sum(part):
    line, count = lax.axis_index("dp"), lax.axis_size("dp")
    total = pick(part, line).astype(F32)
    for step in range(1, count):
        moved = lax.ppermute(
            pick(part, lax.rem(line + step, count)),
            "dp",
            [(source, (source + step) % count) for source in range(count)],
        )
        total = total + moved.astype(F32)
    return total.astype(BF16)


def plain_grad(left, right):
    depth, columns = left.shape[1], right.shape[1]

    def kernel(left_ref, right_ref, out_ref):
        turned = left_ref[...].astype(F32).T.astype(BF16)
        for start, end in tiles(columns):
            out_ref[:, start:end] = dot(turned, right_ref[:, start:end], 1, 0).astype(BF16)

    return whole_call(kernel, "plain_grad", [((depth, columns), BF16)], left, right)[0]


class Order:
    def __init__(self, token):
        self.token = token

    def __call__(self, *values):
        values, self.token = lax.optimization_barrier((values, self.token))
        return values if len(values) > 1 else values[0]

    def sent(self, *sums):
        for each in sums:
            each.send = self(each.send)

    def summed(self, *sums):
        for each in sums:
            each.line = self(each.line)

    def arrived(self, *sums):
        for each in sums:
            each.moved = self(each.moved)


def in_order(pieces):
    here = lax.axis_index("seq")
    return jnp.stack([pick(pieces, here ^ index) for index in range(4)])


def attention_forward(qkv, hidden_keys):
    length, width = qkv.shape
    width //= 3
    heads = width // HEAD_DIM

    def kernel(qkv_ref, hidden_ref, out_ref, lse_ref, q_s, k_s, v_s, o_s):
        head = pl.program_id(0)

        @pl.when(head == 0)
        def _():
            for index in range(heads):
                at = index * HEAD_DIM
                q_s[index] = qkv_ref[:, at : at + HEAD_DIM]
                k_s[index] = qkv_ref[:, width + at : width + at + HEAD_DIM]
                v_s[index] = qkv_ref[:, 2 * width + at : 2 * width + at + HEAD_DIM]

        scores = dot(k_s[head], q_s[head], 1, 1) * SCALE
        scores = jnp.where(hidden_ref[...] > 0, -1e9, scores)
        top = jnp.max(scores, axis=0, keepdims=True)
        expon = jnp.exp(scores - top)
        total = jnp.sum(expon, axis=0, keepdims=True)
        lse_ref[0] = top + jnp.log(total)
        mixed = dot(v_s[head], expon.astype(BF16), 0, 0) / total
        o_s[head] = mixed.T.astype(BF16)

        @pl.when(head == heads - 1)
        def _():
            for index in range(heads):
                out_ref[:, index * HEAD_DIM : (index + 1) * HEAD_DIM] = o_s[index]

    slab = pltpu.VMEM((heads, length, HEAD_DIM), BF16)
    return pl.pallas_call(
        kernel,
        grid=(heads,),
        out_shape=(
            jax.ShapeDtypeStruct((length, width), BF16),
            jax.ShapeDtypeStruct((heads, 1, length), F32),
        ),
        in_specs=[
            pl.BlockSpec((length, 3 * width), lambda h: (0, 0)),
            pl.BlockSpec((length, 1), lambda h: (0, 0)),
        ],
        out_specs=(
            pl.BlockSpec((length, width), lambda h: (0, 0)),
            pl.BlockSpec((1, 1, length), lambda h: (h, 0, 0)),
        ),
        scratch_shapes=[slab, slab, slab, slab],
        compiler_params=params_of(),
        cost_estimate=LIGHT,
        name="attention_forward",
    )(qkv, hidden_keys)


def attention_backward(qkv, d_out, lse, hidden_keys):
    length, width = d_out.shape
    heads = width // HEAD_DIM

    def kernel(
        qkv_ref, do_ref, lse_ref, hidden_ref, out_ref, sums_ref, q_s, k_s, v_s, do_s, dq_s, dk_s, dv_s
    ):
        head = pl.program_id(0)

        @pl.when(head == 0)
        def _():
            for index in range(heads):
                at = index * HEAD_DIM
                q_s[index] = qkv_ref[:, at : at + HEAD_DIM]
                k_s[index] = qkv_ref[:, width + at : width + at + HEAD_DIM]
                v_s[index] = qkv_ref[:, 2 * width + at : 2 * width + at + HEAD_DIM]
                do_s[index] = do_ref[:, at : at + HEAD_DIM]

        queries, keys, values, d_rows = q_s[head], k_s[head], v_s[head], do_s[head]
        scores = dot(keys, queries, 1, 1) * SCALE
        scores = jnp.where(hidden_ref[...] > 0, -1e9, scores)
        soft = jnp.exp(scores - lse_ref[0])
        d_soft = dot(values, d_rows, 1, 1)
        inner = jnp.sum(soft * d_soft, axis=0, keepdims=True)
        d_scores = (soft * (d_soft - inner)).astype(BF16)
        dv_s[head] = dot(soft.astype(BF16), d_rows, 1, 0).astype(BF16)
        dk_s[head] = (dot(d_scores, queries, 1, 0) * SCALE).astype(BF16)
        dq_s[head] = (dot(keys, d_scores, 0, 0) * SCALE).T.astype(BF16)

        @pl.when(head == heads - 1)
        def _():
            for index in range(heads):
                at = index * HEAD_DIM
                out_ref[:, at : at + HEAD_DIM] = dq_s[index]
                out_ref[:, width + at : width + at + HEAD_DIM] = dk_s[index]
                out_ref[:, 2 * width + at : 2 * width + at + HEAD_DIM] = dv_s[index]
            sums_ref[...] = jnp.sum(out_ref[...].astype(F32), axis=0, keepdims=True)

    slab = pltpu.VMEM((heads, length, HEAD_DIM), BF16)
    return pl.pallas_call(
        kernel,
        grid=(heads,),
        out_shape=(
            jax.ShapeDtypeStruct((length, 3 * width), BF16),
            jax.ShapeDtypeStruct((1, 3 * width), F32),
        ),
        in_specs=[
            pl.BlockSpec((length, 3 * width), lambda h: (0, 0)),
            pl.BlockSpec((length, width), lambda h: (0, 0)),
            pl.BlockSpec((1, 1, length), lambda h: (h, 0, 0)),
            pl.BlockSpec((length, 1), lambda h: (0, 0)),
        ],
        out_specs=(
            pl.BlockSpec((length, 3 * width), lambda h: (0, 0)),
            pl.BlockSpec((1, 3 * width), lambda h: (0, 0)),
        ),
        scratch_shapes=[slab] * 7,
        compiler_params=params_of(),
        cost_estimate=LIGHT,
        name="attention_backward",
    )(qkv, d_out, lse, hidden_keys)


def norm_parts(stream):
    centre = jnp.mean(stream, axis=-1, keepdims=True)
    offset = stream - centre
    spread = jnp.mean(offset * offset, axis=-1, keepdims=True)
    inverse = lax.rsqrt(spread + 1e-06)
    return offset * inverse, inverse


def tiles(total, step=256):
    return [(at, min(at + step, total)) for at in range(0, total, step)]


def whole_call(kernel, name, out_shapes, *arrays):
    shapes = tuple(jax.ShapeDtypeStruct(shape, dtype) for shape, dtype in out_shapes)
    return pl.pallas_call(
        kernel,
        out_shape=shapes,
        in_specs=whole_vmem(len(arrays)),
        out_specs=tuple(whole_vmem(len(shapes))),
        compiler_params=params_of(),
        cost_estimate=LIGHT,
        name=name,
    )(*arrays)


PIECES = 2


def piece_bounds(columns):
    step = round_up(columns // PIECES, 128)
    return [(at * step, min((at + 1) * step, columns)) for at in range(PIECES)]


def join_pieces(refs):
    return jnp.concatenate([ref[...] for ref in refs], axis=1).astype(F32)


def partial_product(left, weight, turned, name):
    length, depth = left.shape
    columns = weight.shape[0 if turned else 1]
    bounds = piece_bounds(columns)

    def kernel(left_ref, weight_ref, *out_refs):
        for start, end in tiles(columns):
            if turned:
                product = dot(left_ref[...], weight_ref[start:end, :depth], 1, 1)
            else:
                product = dot(left_ref[...], weight_ref[:, start:end], 1, 0)
            product = product.astype(BF16)
            for ref, (first, last) in zip(out_refs, bounds):
                low, high = max(start, first), min(end, last)
                if low < high:
                    ref[:, low - first : high - first] = product[:, low - start : high - start]

    shapes = [((length, last - first), BF16) for first, last in bounds]
    return whole_call(kernel, name, shapes, left, weight)


def project_in(base, partials, vectors, weight, shift):
    length, width = base.shape
    columns = weight.shape[1]

    def kernel(*refs):
        if partials is None:
            base_ref, vectors_ref, weight_ref, shift_ref, normed_ref, qkv_ref = refs
            stream = base_ref[...].astype(F32)
        else:
            base_ref, *refs = refs
            own_refs, other_refs = refs[:PIECES], refs[PIECES : 2 * PIECES]
            bias_ref, vectors_ref, weight_ref, shift_ref = refs[2 * PIECES : 2 * PIECES + 4]
            normed_ref, qkv_ref, stream_ref = refs[2 * PIECES + 4 :]
            stream = base_ref[...] + join_pieces(own_refs) + join_pieces(other_refs)
            stream_ref[...] = (stream + bias_ref[...]).astype(BF16)
            stream = stream_ref[...].astype(F32)
        normed = norm_parts(stream)[0] * vectors_ref[0:1, :] + vectors_ref[2:3, :]
        normed_ref[...] = normed.astype(BF16)
        for start, end in tiles(columns):
            product = dot(normed_ref[...], weight_ref[:, start:end], 1, 0)
            qkv_ref[:, start:end] = (product + shift_ref[:, start:end]).astype(BF16)

    shapes = [((length, width), BF16), ((length, columns), BF16)]
    if partials is None:
        normed, qkv = whole_call(kernel, "project_in", shapes, base, vectors, weight, shift)
        return base, normed, qkv
    shapes.append(((length, width), BF16))
    normed, qkv, stream = whole_call(
        kernel,
        "project_in",
        shapes,
        base,
        *partials[0],
        *partials[1],
        partials[2],
        vectors,
        weight,
        shift,
    )
    return stream, normed, qkv


def expand_hidden(stream, own, other, vectors, weight, shift):
    length, width = stream.shape
    columns = shift.shape[1]
    root = 0.7978845608028654

    def kernel(stream_ref, *refs):
        own_refs, other_refs, refs = refs[:PIECES], refs[PIECES : 2 * PIECES], refs[2 * PIECES :]
        vectors_ref, weight_ref, shift_ref, mid_ref, normed_ref, hidden_ref, slope_ref = refs
        middle = stream_ref[...].astype(F32) + join_pieces(own_refs)
        middle = middle + join_pieces(other_refs) + vectors_ref[6:7, :]
        mid_ref[...] = middle
        normed = norm_parts(middle)[0] * vectors_ref[1:2, :] + vectors_ref[3:4, :]
        normed_ref[...] = normed.astype(BF16)
        for start, end in tiles(columns):
            inner = dot(normed_ref[...], weight_ref[:, start:end], 1, 0) + shift_ref[:, start:end]
            square = inner * inner
            half_tanh = 0.5 * jnp.tanh(root * (inner + 0.044715 * square * inner))
            hidden_ref[:, start:end] = (inner * (0.5 + half_tanh)).astype(BF16)
            bend = (0.5 - 2.0 * half_tanh * half_tanh) * (root + 3 * 0.044715 * root * square)
            slope_ref[:, start:end] = (0.5 + half_tanh + inner * bend).astype(BF16)

    return whole_call(
        kernel,
        "expand_hidden",
        [
            ((length, width), F32),
            ((length, width), BF16),
            ((length, columns), BF16),
            ((length, columns), BF16),
        ],
        stream, *own, *other, vectors, weight, shift,
    )


def back_hidden(d_result, weight, slope):
    length, columns = slope.shape

    def kernel(d_ref, weight_ref, slope_ref, out_ref, sums_ref):
        for start, end in tiles(columns):
            d_hidden = dot(d_ref[...], weight_ref[start:end, :], 1, 1)
            d_pre = (d_hidden * slope_ref[:, start:end].astype(F32)).astype(BF16)
            out_ref[:, start:end] = d_pre
            sums_ref[:, start:end] = jnp.sum(d_pre.astype(F32), axis=0, keepdims=True)

    return whole_call(
        kernel,
        "back_hidden",
        [((length, columns), BF16), ((1, columns), F32)],
        d_result, weight, slope,
    )


def back_norm(base, own, other, stream, gain, weight):
    length, width = base.shape

    def kernel(*refs):
        base_ref, *refs = refs
        own_refs, other_refs, refs = refs[:PIECES], refs[PIECES : 2 * PIECES], refs[2 * PIECES :]
        stream_ref, gain_ref, *refs = refs
        unit, inverse = norm_parts(stream_ref[...].astype(F32))
        d_normed = join_pieces(own_refs) + join_pieces(other_refs)
        d_unit = d_normed * gain_ref[...]
        mean_d = jnp.mean(d_unit, axis=-1, keepdims=True)
        mean_du = jnp.mean(d_unit * unit, axis=-1, keepdims=True)
        base_wide = base_ref[...].astype(F32)
        total = base_wide + inverse * (d_unit - mean_d - unit * mean_du)
        if weight is None:
            low_ref, sums_ref = refs
        else:
            weight_ref, low_ref, sums_ref, wide_ref, product_ref = refs
            wide_ref[...] = total
        low_ref[...] = total.astype(BF16)
        sums_ref[0:1, :] = jnp.sum(d_normed * unit, axis=0, keepdims=True)
        sums_ref[1:2, :] = jnp.sum(d_normed, axis=0, keepdims=True)
        sums_ref[2:3, :] = jnp.sum(low_ref[...].astype(F32), axis=0, keepdims=True)
        sums_ref[3:4, :] = jnp.sum(base_wide, axis=0, keepdims=True)
        if weight is not None:
            for start, end in tiles(weight.shape[0]):
                product = dot(low_ref[...], weight_ref[start:end, :], 1, 1)
                product_ref[:, start:end] = product.astype(BF16)

    shapes = [((length, width), BF16), ((4, width), F32)]
    arrays = [base, *own, *other, stream, gain]
    if weight is not None:
        arrays.append(weight)
        shapes += [((length, width), F32), ((length, weight.shape[0]), BF16)]
    return whole_call(kernel, "back_norm", shapes, *arrays)


def column_sums(array):
    return jnp.sum(array.astype(F32), axis=0)


def on_device(
    section_inputs,
    key_mask,
    attention_in,
    attention_out,
    expand_weight,
    contract_weight,
    norm_gains,
    biases,
    expand_bias,
):
    core = lax.axis_index("section")
    here = lax.axis_index("seq")
    line = lax.axis_index("dp")
    count = lax.axis_size("dp")
    first = core == 0
    core_ref = core.astype(jnp.int32).reshape(1)

    width = attention_out.shape[2]
    own_rows = attention_out.shape[1]
    half_heads = own_rows // 2
    own_hidden = contract_weight.shape[1]
    half_hidden = round_up(round_up(own_hidden, 2) // 2, 16)
    in_runs = half_runs(3 * count * own_rows, 3 * count, half_heads, half_heads)
    hidden_runs = half_runs(count * own_hidden, count, half_hidden, half_hidden)
    in_width = 3 * count * half_heads
    hidden_width = count * half_hidden

    gate = Order(core)

    def both_layers(keep, send):
        received = swap_cores(send)
        return jnp.where(first, keep, received), jnp.where(first, received, keep)

    def pad_rows(array, step=32):
        extra = round_up(array.shape[-2], step) - array.shape[-2]
        if extra == 0:
            return array
        spec = [(0, 0)] * (array.ndim - 2) + [(0, extra), (0, 0)]
        return jnp.pad(array, spec)

    def prepared(halves):
        quarters = [quarters_of(pad_rows(half)) for half in halves]
        return quarters, [pick(quarter, here) for quarter in quarters]

    def built(own, near, others, rows):
        whole = assemble(own, near, *others)
        whole = whole.reshape(count, -1, whole.shape[3])[:, :rows]
        return whole.reshape(count * rows, whole.shape[2])

    micro, images, block, _ = section_inputs.shape[1:]
    tokens = section_inputs[0].reshape(micro * images, block, width)
    token_blocks = [pick(tokens, here ^ bits) for bits in range(4)]
    hidden_shift = jnp.pad(expand_bias[0], (0, 2 * half_hidden - own_hidden))
    packed = jnp.concatenate([norm_gains[0].reshape(-1), biases[0].reshape(-1), hidden_shift])
    small_size = packed.size
    packed = jnp.concatenate(both_layers(packed, packed))
    in_own, in_mine = prepared(
        both_layers(*split_columns(attention_in[0], in_runs, in_width, core_ref))
    )
    packed_rows = round_up(round_up(packed.size, in_width) // in_width, 8)
    packed = jnp.pad(packed, (0, packed_rows * in_width - packed.size)).reshape(-1, in_width)
    first_rows = in_mine[0].shape[0]
    in_first = jnp.concatenate([in_mine[0], packed], axis=0)
    token_blocks, in_first, expand_weight, attention_out, contract_weight = gate(
        token_blocks, in_first, expand_weight, attention_out, contract_weight
    )
    near_in_0 = line_shifts(in_first)
    inputs = [swap_seq(token_blocks[bits], (bits, 0)) for bits in range(1, 4)]
    out_parts = attention_out[0].reshape(2, half_heads, width)
    out_halves = both_layers(pick(out_parts, core), pick(out_parts, 1 - core))
    expand_halves = both_layers(
        *split_columns(expand_weight[0], hidden_runs, hidden_width, core_ref)
    )
    expand_own, expand_mine = prepared(
        [
            jnp.concatenate([high, low.reshape(own_rows, -1)], axis=1)
            for high, low in zip(expand_halves, out_halves)
        ]
    )
    expand_mine = gate(expand_mine)
    near_expand_0 = line_gather(expand_mine[0])

    def heads_of(merged):
        return merged[:, hidden_width:].reshape(count * half_heads, width)

    contract_parts = jnp.pad(
        contract_weight[0], ((0, 2 * half_hidden - own_hidden), (0, 0))
    ).reshape(2, half_hidden, width)
    contract_own, contract_mine = prepared(
        both_layers(pick(contract_parts, core), pick(contract_parts, 1 - core))
    )
    contract_mine = gate(contract_mine)
    near_contract_0 = line_gather(contract_mine[0])
    near_in_0, inputs = gate(near_in_0, inputs)
    packed = [packed] + [part[first_rows:] for part in near_in_0]
    near_in_0 = jnp.stack([part[:first_rows] for part in near_in_0])
    beside_in_0, near_expand_0 = gate(spread(near_in_0), near_expand_0)
    across_in_0 = spread_on(beside_in_0)
    image = jnp.concatenate([token_blocks[0], *inputs], axis=0)
    start = jnp.where(first, image, swap_cores(image))
    mask = pick(key_mask.reshape(micro * images, 4, block), here)
    mask = jnp.concatenate([pick(mask, here ^ bits) for bits in range(4)])
    hidden_keys = jnp.where(mask > 0, 0.0, 1.0).astype(F32)[:, None]

    packed = jnp.stack([part.reshape(-1) for part in packed])
    packed = lax.dynamic_slice_in_dim(
        jnp.concatenate([packed, packed], 0), lax.rem(count - line, count), count, 0
    ).astype(F32)

    def small_of(packed):
        vectors = packed[:, : 8 * own_rows].reshape(count, 8, own_rows)
        hidden = packed[:, 8 * own_rows :].reshape(count, 2, half_hidden)
        heads_part = pick(vectors.reshape(count, 8, 2, half_heads), core, 2)
        vectors = vectors.transpose(1, 0, 2).reshape(8, width)
        query, value = heads_part[:, 4].reshape(-1), heads_part[:, 5].reshape(-1)
        qkv_shift = jnp.concatenate([query, jnp.zeros_like(query), value])
        hidden_shift = pick(hidden, core, 1).reshape(1, -1)
        return vectors, qkv_shift.reshape(1, -1), hidden_shift

    vectors_0, qkv_shift_0, hidden_shift_0 = small_of(packed[:, :small_size])
    vectors_1, qkv_shift_1, hidden_shift_1 = small_of(packed[:, small_size : 2 * small_size])
    across_in_0, start, hidden_keys, qkv_shift_0, in_mine, expand_mine = gate(
        across_in_0, start, hidden_keys, qkv_shift_0, in_mine, expand_mine
    )

    beside_expand_0 = spread(near_expand_0)
    near_in_1 = line_shifts(in_mine[1])
    attn_in_0 = built(in_own[0], near_in_0, (*beside_in_0, across_in_0), own_rows)
    stream_0, normed_0, qkv_0 = project_in(start, None, vectors_0, attn_in_0, qkv_shift_0)
    beside_expand_0, near_in_1, qkv_0, expand_mine = gate(
        beside_expand_0, near_in_1, qkv_0, expand_mine
    )
    across_expand_0 = spread_on(beside_expand_0)
    near_in_1 = jnp.stack(near_in_1)
    beside_in_1 = spread(near_in_1)
    near_expand_1 = line_gather(expand_mine[1])
    mixed_0, lse_0 = attention_forward(qkv_0, hidden_keys)
    mixed_0, across_expand_0 = gate(mixed_0, across_expand_0)
    expand_0 = built(expand_own[0], near_expand_0, (*beside_expand_0, across_expand_0), own_rows)
    attn_out_0 = heads_of(expand_0)
    own = partial_product(mixed_0, attn_out_0, False, "project_heads")
    own, beside_in_1, near_contract_0, contract_mine = gate(
        own, beside_in_1, near_contract_0, contract_mine
    )
    across_in_1 = spread_on(beside_in_1)
    beside_contract_0 = spread(near_contract_0)
    near_contract_1 = line_gather(contract_mine[1])
    own, other = gate(own, swap_cores(own))
    middle_0, normed_mid_0, hidden_0, slope_0 = expand_hidden(
        stream_0, own, other, vectors_0, expand_0, hidden_shift_0
    )
    hidden_0, across_in_1, beside_contract_0, near_expand_1 = gate(
        hidden_0, across_in_1, beside_contract_0, near_expand_1
    )
    across_contract_0 = spread_on(beside_contract_0)
    beside_expand_1 = spread(near_expand_1)
    attn_in_1 = built(in_own[1], near_in_1, (*beside_in_1, across_in_1), own_rows)
    attn_in_1, across_contract_0 = gate(attn_in_1, across_contract_0)
    contract_0 = built(
        contract_own[0], near_contract_0, (*beside_contract_0, across_contract_0), half_hidden
    )
    own = gate(partial_product(hidden_0, contract_0, False, "contract_hidden"))
    own, other, token_blocks = gate(own, swap_cores(own), token_blocks)

    cotangents = [swap_seq(token_blocks[bits], (0, bits)) for bits in range(1, 3)]
    partials = (own, other, vectors_0[7:8])
    stream_1, normed_1, qkv_1 = project_in(middle_0, partials, vectors_1, attn_in_1, qkv_shift_1)
    beside_expand_1, near_contract_1, qkv_1, cotangents, token_blocks = gate(
        beside_expand_1, near_contract_1, qkv_1, cotangents, token_blocks
    )
    across_expand_1 = spread_on(beside_expand_1)
    beside_contract_1 = spread(near_contract_1)
    cotangents.append(swap_seq(token_blocks[3], (0, 3)))
    mixed_1, lse_1 = attention_forward(qkv_1, hidden_keys)
    mixed_1, across_expand_1 = gate(mixed_1, across_expand_1)
    expand_1 = built(expand_own[1], near_expand_1, (*beside_expand_1, across_expand_1), own_rows)
    attn_out_1 = heads_of(expand_1)
    own = partial_product(mixed_1, attn_out_1, False, "project_heads")
    own, beside_contract_1, cotangents = gate(own, beside_contract_1, cotangents)
    across_contract_1 = spread_on(beside_contract_1)
    image = jnp.concatenate([token_blocks[0], *cotangents], axis=0)
    own, other = gate(own, swap_cores(own))
    cotangent = jnp.where(first, swap_cores(image), image)
    middle_1, normed_mid_1, hidden_1, slope_1 = expand_hidden(
        stream_1, own, other, vectors_1, expand_1, hidden_shift_1
    )
    hidden_1, across_contract_1, cotangent = gate(hidden_1, across_contract_1, cotangent)

    small_rows = round_up(7 + round_up(hidden_width, width) // width, 16)

    def out_sum(grad, in_sums, mid_sums, hidden_sums, qkv_sums):
        heads = [qkv_sums[:, : width // 2], qkv_sums[:, width:]]
        rows = [in_sums[:1], mid_sums[:1], in_sums[1:2], mid_sums[1:], jnp.concatenate(heads, axis=1)]
        spare = (small_rows - 7) * width - hidden_width
        rows.append(jnp.pad(hidden_sums, ((0, 0), (0, spare))).reshape(-1, width))
        small = jnp.concatenate(rows, axis=0).astype(BF16)
        small = jnp.broadcast_to(small, (count, small_rows, width))
        parts = [grad.reshape(count, half_heads, width), small]
        part = gate(jnp.concatenate(parts, axis=1))
        return lax.psum_scatter(part, "dp", scatter_dimension=0, tiled=True)[0]

    def own_layer(low, high):
        return jnp.stack([jnp.where(first, low, high), swap_cores(jnp.where(first, high, low))])

    def last_place():
        return jnp.stack([gate.token, *(here ^ bits for bits in relative_bits())]).astype(jnp.int32)

    def rows_of(pieces, total):
        mine, other = jnp.stack(pieces, axis=1)
        return join_rows(mine, other, total, last_place())

    def columns_of(pieces, runs, total):
        mine, other = jnp.stack(pieces, axis=1)
        return join_columns(mine, other, runs, total, last_place())

    contract_sum_1 = Sum(hidden_1, cotangent, count)
    gate.sent(contract_sum_1)
    contract_sum_1.first()
    contract_1 = built(
        contract_own[1], near_contract_1, (*beside_contract_1, across_contract_1), half_hidden
    )
    d_pre_1, hidden_sums_1 = back_hidden(cotangent, contract_1, slope_1)
    d_pre_1 = gate(d_pre_1)
    expand_sum_1 = Sum(normed_mid_1, d_pre_1, count)
    gate.sent(expand_sum_1)
    expand_sum_1.first()
    own = gate(partial_product(gate(d_pre_1), expand_1, True, "back_expand"))
    gate.arrived(contract_sum_1)
    contract_sum_1.add()
    own_out = partial_product(hidden_1, contract_1, False, "contract_hidden")
    own, other, own_out = gate(own, swap_cores(own), own_out)
    gate.sent(contract_sum_1)
    contract_sum_1.second()
    d_branch_1, mid_sums_1, d_middle_1, d_mixed_1 = back_norm(
        cotangent, own, other, middle_1, vectors_1[1:2], attn_out_1
    )
    d_branch_1, d_mixed_1 = gate(d_branch_1, d_mixed_1)
    out_grad_1 = plain_grad(mixed_1, d_branch_1)
    gate.arrived(expand_sum_1)
    expand_sum_1.add()
    gate.sent(expand_sum_1)
    expand_sum_1.second()
    d_qkv_1, qkv_sums_1 = gate(attention_backward(qkv_1, gate(d_mixed_1), lse_1, hidden_keys))
    gate.arrived(contract_sum_1)
    contract_sum_1.over_line(gate)
    in_sum_1 = Sum(normed_1, gate(d_qkv_1), count)
    gate.sent(in_sum_1)
    in_sum_1.first()
    gate.arrived(expand_sum_1)
    expand_sum_1.over_line(gate)
    own = gate(partial_product(gate(d_qkv_1), attn_in_1, True, "back_in"))
    own, other, other_out = gate(own, swap_cores(own), swap_cores(own_out))
    own_out, other_out = jnp.concatenate(own_out, axis=1), jnp.concatenate(other_out, axis=1)
    output = middle_1 + own_out.astype(F32) + other_out.astype(F32) + vectors_1[7:8]
    output = output.astype(BF16)
    d_result_0, in_sums_1 = back_norm(d_middle_1, own, other, stream_1, vectors_1[0:1], None)
    d_result_0 = gate(d_result_0)
    gate.arrived(in_sum_1)
    in_sum_1.add()
    gate.sent(in_sum_1)
    in_sum_1.second()

    contract_sum_0 = Sum(hidden_0, gate(d_result_0), count)
    gate.sent(contract_sum_0)
    contract_sum_0.first()
    d_pre_0, hidden_sums_0 = back_hidden(gate(d_result_0), contract_0, slope_0)
    d_pre_0, output = gate(d_pre_0, output)
    gate.arrived(in_sum_1)
    in_sum_1.over_line(gate)
    expand_sum_0 = Sum(normed_mid_0, gate(d_pre_0), count)
    gate.sent(expand_sum_0)
    expand_sum_0.first()
    gate.summed(contract_sum_1)
    own = gate(partial_product(gate(d_pre_0), expand_0, True, "back_expand"))
    gate.arrived(contract_sum_0)
    contract_sum_0.add()
    own, other = gate(own, swap_cores(own))
    gate.sent(contract_sum_0)
    contract_sum_0.second()
    d_branch_0, mid_sums_0, d_middle_0, d_mixed_0 = back_norm(
        d_result_0, gate(own), other, middle_0, vectors_0[1:2], attn_out_0
    )
    d_branch_0, d_mixed_0 = gate(d_branch_0, d_mixed_0)
    out_grad_0 = gate(plain_grad(mixed_0, d_branch_0))
    gate.summed(expand_sum_1)
    out_line_1 = out_sum(out_grad_1, in_sums_1, mid_sums_1, hidden_sums_1, qkv_sums_1)
    output = output.reshape(4, block, width)
    outputs = [swap_seq(output[bits], (0, bits)) for bits in range(1, 4)]
    d_qkv_0, qkv_sums_0 = gate(attention_backward(qkv_0, gate(d_mixed_0), lse_0, hidden_keys))
    outputs = gate(outputs)
    gate.arrived(expand_sum_0)
    expand_sum_0.add()
    gate.sent(expand_sum_0)
    expand_sum_0.second()
    gate.arrived(contract_sum_0)
    contract_sum_0.over_line(gate)
    in_sum_0 = Sum(normed_0, gate(d_qkv_0), count)
    gate.sent(in_sum_0)
    in_sum_0.first()
    gate.summed(in_sum_1)
    own = gate(partial_product(gate(d_qkv_0), attn_in_0, True, "back_in"))
    own, other = gate(own, swap_cores(own))
    gate.arrived(expand_sum_0)
    expand_sum_0.over_line(gate)
    d_input_0, in_sums_0 = back_norm(d_middle_0, gate(own), other, stream_0, vectors_0[0:1], None)
    d_input_0, out_line_1 = gate(d_input_0, out_line_1)

    d_input_0 = d_input_0.reshape(4, block, width)
    gate.arrived(in_sum_0)
    in_sum_0.add()
    gate.summed(contract_sum_0)
    gate.sent(in_sum_0)
    in_sum_0.second()
    contract_near = own_layer(contract_sum_0.line, contract_sum_1.line)
    gate.arrived(in_sum_0)
    contract_near = gate(contract_near)
    contract_beside = spread(contract_near)
    in_sum_0.over_line(gate)
    gate.summed(expand_sum_0)
    contract_beside = gate(contract_beside)
    contract_across = spread_on(contract_beside)
    inputs_back = [swap_seq(d_input_0[bits], (bits, 0)) for bits in range(1, 3)]
    expand_near = own_layer(expand_sum_0.line, expand_sum_1.line)
    contract_across, inputs_back, expand_near = gate(contract_across, inputs_back, expand_near)
    expand_beside = spread(expand_near)
    inputs_back.append(swap_seq(d_input_0[3], (3, 0)))
    grad_contract = rows_of([contract_near, *contract_beside, contract_across], own_hidden)
    gate.summed(in_sum_0)
    out_line_0 = out_sum(out_grad_0, in_sums_0, mid_sums_0, hidden_sums_0, qkv_sums_0)
    expand_beside, grad_contract, inputs_back = gate(expand_beside, grad_contract, inputs_back)
    in_near = gate(own_layer(in_sum_0.line, in_sum_1.line))
    in_beside = spread(in_near)
    expand_across = spread_on(expand_beside)
    in_beside, expand_across = gate(in_beside, expand_across)
    in_across = spread_on(in_beside)
    grad_expand = columns_of(
        [expand_near, *expand_beside, expand_across], hidden_runs, count * own_hidden
    )
    out_line_0, in_across, grad_expand = gate(out_line_0, in_across, grad_expand)
    out_near = gate(own_layer(out_line_0, out_line_1))
    out_moved = swap_seq(out_near, FIRST)
    grad_in = columns_of([in_near, *in_beside, in_across], in_runs, 3 * width)
    out_moved, grad_in = gate(out_moved, grad_in)
    out_near = add_low(out_near, out_moved)
    out_moved = swap_seq(out_near, SECOND)
    returned = [
        jnp.where(first, low, high)
        for low, high in zip([d_input_0[0], *inputs_back], [output[0], *outputs])
    ]
    results = in_order(jnp.stack(returned)).astype(F32)
    results = results.reshape(1, micro, images, block, width)
    out_near = add_low(out_near, gate(out_moved)).astype(F32)
    mine, other = out_near[0, :half_heads], out_near[1, :half_heads]
    grad_out = jnp.concatenate([jnp.where(first, mine, other), jnp.where(first, other, mine)])

    def own_part(rows, size):
        return lax.dynamic_slice_in_dim(rows, line * size, size, rows.ndim - 1)

    def halves_of(mine, other, size):
        mine, other = own_part(mine, size), own_part(other, size)
        low, high = jnp.where(first, mine, other), jnp.where(first, other, mine)
        return jnp.concatenate([low, high], axis=-1)

    mine, other = out_near[0, half_heads:], out_near[1, half_heads:]
    shared = own_part(mine[:6], own_rows)
    query = halves_of(mine[6, : width // 2], other[6, : width // 2], half_heads)
    value = halves_of(mine[6, width // 2 :], other[6, width // 2 :], half_heads)
    hidden = [rows[7:].reshape(-1)[:hidden_width] for rows in (mine, other)]
    hidden = halves_of(*hidden, half_hidden)[:own_hidden]
    grad_shifts = jnp.concatenate([shared[2:4], query[None], value[None], shared[4:6]])

    return (
        results,
        grad_in[None],
        grad_out[None],
        grad_expand[None],
        grad_contract.transpose(1, 0, 2),
        shared[None, :2],
        grad_shifts[None],
        hidden[None],
    )


def plain_passed_along(value, axis, steps):
    count = lax.axis_size(axis)
    initial, last = (max(0, -steps), min(count, count - steps))
    return lax.ppermute(value, axis, [(source, source + steps) for source in range(initial, last)])


def plain_layer_norm(stream, gain, shift):
    centre = jnp.mean(stream, axis=-1, keepdims=True)
    offset = stream - centre
    spread = jnp.mean(offset * offset, axis=-1, keepdims=True)
    return offset * lax.rsqrt(spread + 1e-06) * gain + shift


def plain_matmul(left, right):
    return jnp.dot(left, right, preferred_element_type=F32)


def plain_left_matmul(left, right):
    return lax.dot_general(
        left, right, (((0,), (0,)), ((), ())), preferred_element_type=F32
    )


def plain_right_matmul(left, right):
    return lax.dot_general(
        left, right, (((1,), (1,)), ((), ())), preferred_element_type=F32
    )


def plain_gather_once(local):
    whole = (
        lax.all_gather(local[0], "dp", axis=1, tiled=True),
        lax.all_gather(local[1], "dp", axis=1, tiled=True),
        lax.all_gather(local[2], "dp", axis=1, tiled=True),
        lax.all_gather(local[3], "dp", axis=1, tiled=True),
        lax.all_gather(local[4], "dp", axis=2, tiled=True),
        lax.all_gather(local[5], "dp", axis=2, tiled=True),
        lax.all_gather(local[6], "dp", axis=1, tiled=True),
    )
    return tuple((piece[0] for piece in whole))


def plain_split_heads(heads):
    images, length, _, width = heads.shape
    count = width // HEAD_DIM
    queries = heads[:, :, 0].reshape(images, length, count, HEAD_DIM)
    key_rows = heads[:, :, 1].reshape(images, length, count, HEAD_DIM)
    value_rows = heads[:, :, 2].reshape(images, length, count, HEAD_DIM)
    return (queries, key_rows, value_rows)


def plain_head_scores(queries, key_rows, visible):
    scores = jnp.einsum(
        "nqhd,nkhd->nhqk", queries, key_rows, preferred_element_type=F32
    ) * HEAD_DIM ** (-0.5)
    return jnp.where(visible[:, None, None, :], scores, -1000000000.0)


def plain_attend(heads, visible):
    images, length, _, width = heads.shape
    queries, key_rows, value_rows = plain_split_heads(heads)
    scores = plain_head_scores(queries, key_rows, visible)
    row_max = jnp.max(scores, axis=-1, keepdims=True)
    expon = jnp.exp(scores - row_max)
    total = jnp.sum(expon, axis=-1, keepdims=True)
    softmaxed = (expon / total).astype(BF16)
    log_total = (row_max + jnp.log(total))[..., 0]
    mixture = jnp.einsum(
        "nhqk,nkhd->nqhd", softmaxed, value_rows, preferred_element_type=F32
    )
    return (mixture.astype(BF16).reshape(images, length, width), log_total)


def plain_attend_back(heads, log_total, visible, d_mixture):
    images, length, _, width = heads.shape
    queries, key_rows, value_rows = plain_split_heads(heads)
    d_rows = d_mixture.reshape(queries.shape)
    scores = plain_head_scores(queries, key_rows, visible)
    softmaxed = jnp.exp(scores - log_total[..., None])
    d_soft = jnp.einsum("nqhd,nkhd->nhqk", d_rows, value_rows, preferred_element_type=F32)
    inner = jnp.sum(softmaxed * d_soft, axis=-1, keepdims=True)
    d_scores = (softmaxed * (d_soft - inner)).astype(BF16)
    scale = HEAD_DIM ** (-0.5)
    d_queries = (
        jnp.einsum("nhqk,nkhd->nqhd", d_scores, key_rows, preferred_element_type=F32)
        * scale
    ).astype(BF16)
    d_keys = (
        jnp.einsum("nhqk,nqhd->nkhd", d_scores, queries, preferred_element_type=F32) * scale
    ).astype(BF16)
    d_values = jnp.einsum(
        "nhqk,nqhd->nkhd",
        softmaxed.astype(BF16),
        d_rows,
        preferred_element_type=F32,
    ).astype(BF16)
    return jnp.stack([d_queries, d_keys, d_values], axis=2).reshape(images, length, 3, width)


def plain_forward_layer(stream_in, visible, params):
    attn_in, attn_out, expand, contract, gains, shifts, expand_shift = params
    images, rows_seq, width = stream_in.shape
    stream = stream_in.astype(F32).reshape(-1, width)
    gains32 = gains.astype(F32)
    shifts32 = shifts.astype(F32)
    normed = plain_layer_norm(stream, gains32[0], shifts32[0]).astype(BF16)
    qkv_shift = jnp.stack([shifts32[2], jnp.zeros_like(shifts32[2]), shifts32[3]])
    projected = (plain_matmul(normed, attn_in).reshape(images, rows_seq, 3, width) + qkv_shift).astype(
        BF16
    )
    heads = lax.all_to_all(projected, "seq", split_axis=3, concat_axis=1, tiled=True)
    mixture, log_total = plain_attend(heads, visible)
    mixed_rows = lax.all_to_all(mixture, "seq", split_axis=1, concat_axis=2, tiled=True).reshape(
        -1, width
    )
    middle = stream + plain_matmul(mixed_rows, attn_out) + shifts32[4]
    normed_mid = plain_layer_norm(middle, gains32[1], shifts32[1]).astype(BF16)
    hidden_pre = plain_matmul(normed_mid, expand) + expand_shift.astype(F32)
    hidden = jax.nn.gelu(hidden_pre, approximate=True).astype(BF16)
    result = middle + plain_matmul(hidden, contract) + shifts32[5]
    saved = (
        stream_in,
        normed,
        heads,
        log_total,
        mixed_rows,
        middle,
        normed_mid,
        hidden_pre,
        hidden,
        visible,
    )
    return (result.reshape(images, rows_seq, width), saved)


def plain_backward_layer(d_result, saved, params):
    attn_in, attn_out, expand, contract, gains, shifts, expand_shift = params
    (
        stream_in,
        normed,
        heads,
        log_total,
        mixed_rows,
        middle,
        normed_mid,
        hidden_pre,
        hidden,
        visible,
    ) = saved
    images, rows_seq, width = d_result.shape
    gains32 = gains.astype(F32)
    shifts32 = shifts.astype(F32)
    d_flat = d_result.reshape(-1, width)
    d_wide = d_flat.astype(F32)
    grad_contract = plain_left_matmul(hidden, d_flat)
    grad_last_bias = jnp.sum(d_wide, axis=0)
    d_hidden = plain_right_matmul(d_flat, contract)
    _, gelu_back = jax.vjp(lambda inner: jax.nn.gelu(inner, approximate=True), hidden_pre)
    d_pre = gelu_back(d_hidden)[0].astype(BF16)
    grad_expand = plain_left_matmul(normed_mid, d_pre)
    grad_expand_bias = jnp.sum(d_pre.astype(F32), axis=0)
    d_normed_mid = plain_right_matmul(d_pre, expand)
    _, norm_back_mid = jax.vjp(plain_layer_norm, middle, gains32[1], shifts32[1])
    d_middle_part, grad_gain_mid, grad_shift_mid = norm_back_mid(d_normed_mid)
    d_middle = d_wide + d_middle_part
    d_branch = d_middle.astype(BF16)
    grad_out_bias = jnp.sum(d_branch.astype(F32), axis=0)
    grad_attn_out = plain_left_matmul(mixed_rows, d_branch)
    d_mixture = (
        plain_right_matmul(d_branch, attn_out).astype(BF16).reshape(images, rows_seq, width)
    )
    d_heads = lax.all_to_all(d_mixture, "seq", split_axis=2, concat_axis=1, tiled=True)
    d_projected_heads = plain_attend_back(heads, log_total, visible, d_heads)
    d_projected = lax.all_to_all(
        d_projected_heads, "seq", split_axis=1, concat_axis=3, tiled=True
    ).reshape(-1, 3 * width)
    grad_attn_in = plain_left_matmul(normed, d_projected)
    column_sums = jnp.sum(d_projected.astype(F32), axis=0).reshape(3, width)
    d_normed = plain_right_matmul(d_projected, attn_in)
    stream = stream_in.astype(F32).reshape(-1, width)
    _, norm_back_in = jax.vjp(plain_layer_norm, stream, gains32[0], shifts32[0])
    d_stream_part, grad_gain_in, grad_shift_in = norm_back_in(d_normed)
    d_stream = d_middle + d_stream_part
    grad_gains = jnp.stack([grad_gain_in, grad_gain_mid])
    grad_shifts = jnp.stack(
        [
            grad_shift_in,
            grad_shift_mid,
            column_sums[0],
            column_sums[2],
            grad_out_bias,
            grad_last_bias,
        ]
    )
    grads = (
        grad_attn_in,
        grad_attn_out,
        grad_expand,
        grad_contract,
        grad_gains,
        grad_shifts,
        grad_expand_bias,
    )
    return (d_stream.reshape(images, rows_seq, width), grads)


def plain_send_forward(values):
    return plain_passed_along(values, "section", 1)


def plain_send_backward(values):
    return plain_passed_along(values, "section", -1)


def on_device_any(
    section_inputs,
    key_mask,
    attention_in,
    attention_out,
    expand_weight,
    contract_weight,
    norm_gains,
    biases,
    expand_bias,
):
    micro = section_inputs.shape[1]
    leading = lax.axis_index("section") == 0
    local = (
        attention_in,
        attention_out,
        expand_weight,
        contract_weight,
        norm_gains,
        biases,
        expand_bias,
    )
    sources = section_inputs[0]
    visible_all = key_mask > 0
    blank = jnp.zeros_like(sources[0])
    recv_forward = blank
    recv_backward = blank
    saves = {}
    outputs = [None] * micro
    input_grads = [None] * micro
    totals = None
    params = plain_gather_once(local)
    for tick in range(micro + 2):
        if tick <= micro:
            source = sources[tick] if tick < micro else blank
            stream_now = jnp.where(leading, source, recv_forward)
            visible_now = jnp.where(
                leading, visible_all[min(tick, micro - 1)], visible_all[max(tick - 1, 0)]
            )
            result, saved = plain_forward_layer(stream_now, visible_now, params)
            saves[tick] = saved
            if tick >= 1:
                outputs[tick - 1] = result
            sent_forward = plain_send_forward(result.astype(BF16))
        if tick >= 1:
            early = saves[tick - 2] if tick - 2 in saves else saves[tick]
            later = saves[tick] if tick in saves else saves[tick - 2]
            chosen = jax.tree.map(
                lambda left_one, right_one: jnp.where(leading, left_one, right_one), early, later
            )
            cotangent = sources[tick - 1] if tick <= micro else blank
            d_result = jnp.where(leading, recv_backward, cotangent)
            d_stream, grads = plain_backward_layer(d_result, chosen, params)
            active = jnp.where(leading, tick >= 2, tick <= micro)
            grads = tuple((jnp.where(active, piece, 0.0) for piece in grads))
            if tick >= 2:
                input_grads[tick - 2] = d_stream
            totals = (
                grads if totals is None else tuple((old + new for old, new in zip(totals, grads)))
            )
            recv_backward = plain_send_backward(d_stream.astype(BF16))
        if tick <= micro:
            recv_forward = sent_forward
    totals = (
        lax.psum_scatter(
            totals[0].astype(BF16), "dp", scatter_dimension=0, tiled=True
        ).astype(F32),
        lax.psum_scatter(
            totals[1].astype(BF16), "dp", scatter_dimension=0, tiled=True
        ).astype(F32),
        lax.psum_scatter(
            totals[2].astype(BF16), "dp", scatter_dimension=0, tiled=True
        ).astype(F32),
        lax.psum_scatter(
            totals[3].astype(BF16), "dp", scatter_dimension=0, tiled=True
        ).astype(F32),
        lax.psum_scatter(
            totals[4].astype(BF16), "dp", scatter_dimension=1, tiled=True
        ).astype(F32),
        lax.psum_scatter(
            totals[5].astype(BF16), "dp", scatter_dimension=1, tiled=True
        ).astype(F32),
        lax.psum_scatter(
            totals[6].astype(BF16), "dp", scatter_dimension=0, tiled=True
        ).astype(F32),
    )
    totals = (
        lax.psum(totals[0].astype(BF16), "seq").astype(F32),
        lax.psum(totals[1].astype(BF16), "seq").astype(F32),
        lax.psum(totals[2].astype(BF16), "seq").astype(F32),
        lax.psum(totals[3].astype(BF16), "seq").astype(F32),
        lax.psum(totals[4].astype(BF16), "seq").astype(F32),
        lax.psum(totals[5].astype(BF16), "seq").astype(F32),
        lax.psum(totals[6].astype(BF16), "seq").astype(F32),
    )
    results = jnp.stack(
        [jnp.where(leading, input_grads[index], outputs[index]) for index in range(micro)]
    )[None]
    return (
        results,
        totals[0][None],
        totals[1][None],
        totals[2][None],
        totals[3][None],
        totals[4][None],
        totals[5][None],
        totals[6][None],
    )


def solution(mesh):
    in_specs = (
        P("section", None, "dp", "seq", None),
        P(None, "dp", None),
        P("section", "dp", None),
        P("section", "dp", None),
        P("section", "dp", None),
        P("section", "dp", None),
        P("section", None, "dp"),
        P("section", None, "dp"),
        P("section", "dp"),
    )
    out_specs = (
        P("section", None, "dp", "seq", None),
        P("section", "dp", None),
        P("section", "dp", None),
        P("section", "dp", None),
        P("section", "dp", None),
        P("section", None, "dp"),
        P("section", None, "dp"),
        P("section", "dp"),
    )

    def by_size(section_inputs, *others):
        _, micro, images, _, _ = section_inputs.shape
        one_image_each = micro * images == lax.axis_size("seq") == 4
        rows, hidden = others[2].shape[1], others[4].shape[1]
        even = rows % (2 * HEAD_DIM) == 0 and rows % 32 == 0
        even = even and round_up(round_up(hidden, 2) // 2, 16) % 32 == 0
        plan = on_device if one_image_each and even else on_device_any
        return plan(section_inputs, *others)

    return jax.shard_map(
        by_size, mesh=mesh, in_specs=in_specs, out_specs=out_specs, check_vma=False
    )
```

```python
import jax
import jax.numpy as jnp
from jax import lax
from jax.experimental import pallas as pl
from jax.experimental.pallas import tpu as pltpu
from jax.sharding import PartitionSpec as P

HEAD_DIM = 72
SCALE = HEAD_DIM**-0.5
VMEM_LIMIT = 32 * 1024 * 1024
F32 = jnp.float32
BF16 = jnp.bfloat16
LIGHT = pl.CostEstimate(flops=1, bytes_accessed=1, transcendentals=0)


def round_up(value, step):
    return -(-value // step) * step


def pick(array, index, axis=0):
    return lax.dynamic_index_in_dim(array, index, axis, keepdims=False)


def swap_cores(value):
    swap = [(0, 1), (1, 0)]
    return jax.tree.map(lambda array: lax.ppermute(array, "section", swap), value)


def swap_seq(value, bits):
    bits = bits if isinstance(bits, tuple) else (bits, bits)
    count = lax.axis_size("seq")
    pairs = [
        (core * count + index, core * count + (index ^ bits[core]))
        for core in range(2)
        for index in range(count)
        if bits[core]
    ]
    return lax.ppermute(value, ("section", "seq"), pairs)


FIRST, SECOND = (1, 2), (2, 1)


def relative_bits():
    core = lax.axis_index("section")
    return (0, 1 + core, 2 - core, 3)


def dot(left, right, left_axis, right_axis):
    return lax.dot_general(
        left, right, (((left_axis,), (right_axis,)), ((), ())), preferred_element_type=F32
    )


def params_of(limit=VMEM_LIMIT):
    return pltpu.CompilerParams(vmem_limit_bytes=limit)


def whole_vmem(count):
    return [pl.BlockSpec(memory_space=pltpu.VMEM)] * count


def half_runs(total, parts, half, width):
    size = total // parts
    runs = [[], []]
    for part in range(parts):
        runs[0].append((part * size, half, part * width))
        runs[1].append((part * size + half, size - half, part * width))
    return runs


def split_columns(weight, runs, width, core):
    rows = weight.shape[0]

    def kernel(core_ref, whole_ref, keep_ref, send_ref):
        def write(ref, pieces):
            if sum(size for _, size, _ in pieces) < width:
                ref[...] = jnp.zeros_like(ref)
            for start, size, place in pieces:
                ref[:, place : place + size] = whole_ref[:, start : start + size]

        @pl.when(core_ref[0] == 0)
        def _():
            write(keep_ref, runs[0])
            write(send_ref, runs[1])

        @pl.when(core_ref[0] == 1)
        def _():
            write(keep_ref, runs[1])
            write(send_ref, runs[0])

    shape = jax.ShapeDtypeStruct((rows, width), weight.dtype)
    return pl.pallas_call(
        kernel,
        out_shape=(shape, shape),
        in_specs=[pl.BlockSpec(memory_space=pltpu.SMEM)] + whole_vmem(1),
        out_specs=tuple(whole_vmem(2)),
        compiler_params=params_of(),
        cost_estimate=LIGHT,
        name="split_columns",
    )(core, weight)


def join_columns(pieces, runs, total, place):
    count = len(pieces)
    _, rows, width = pieces[0].shape

    def kernel(place_ref, *refs):
        out_ref = refs[count]

        def write(piece_ref, halves):
            for half, parts in zip(halves, runs):
                for start, size, at in parts:
                    value = piece_ref[half, :, at : at + size]
                    out_ref[0, :, start : start + size] = value.astype(F32)

        for index in range(count):
            for core, halves in enumerate(((0, 1), (1, 0))):

                @pl.when(jnp.logical_and(pl.program_id(0) == index, place_ref[0] == core))
                def _(index=index, halves=halves):
                    write(refs[index], halves)

    whole = pl.BlockSpec((2, rows, width), lambda j, place: (0, 0, 0))
    out = pl.pallas_call(
        kernel,
        out_shape=jax.ShapeDtypeStruct((count, rows, total), F32),
        grid_spec=pltpu.PrefetchScalarGridSpec(
            num_scalar_prefetch=1,
            grid=(count,),
            in_specs=[whole] * count,
            out_specs=pl.BlockSpec((1, rows, total), lambda j, place: (place[1 + j], 0, 0)),
        ),
        compiler_params=params_of(),
        cost_estimate=LIGHT,
        name="join_columns",
    )(place, *pieces)
    return out.reshape(count * rows, total)


def join_rows(pieces, total, place):
    count = len(pieces)
    _, rows, width = pieces[0].shape

    def kernel(place_ref, *refs):
        out_ref = refs[count]
        half, step = pl.program_id(0) // count, lax.rem(pl.program_id(0), count)
        which = jnp.where(half == place_ref[0], 0, 1)
        for index in range(count):

            @pl.when(step == index)
            def _(index=index):
                out_ref[:, 0, :] = refs[index][which].astype(F32)

    whole = pl.BlockSpec((2, rows, width), lambda t, place: (0, 0, 0))
    return pl.pallas_call(
        kernel,
        out_shape=jax.ShapeDtypeStruct((total, 1, width), F32),
        grid_spec=pltpu.PrefetchScalarGridSpec(
            num_scalar_prefetch=1,
            grid=(2 * count,),
            in_specs=[whole] * count,
            out_specs=pl.BlockSpec(
                (rows, 1, width),
                lambda t, place: (
                    lax.div(t, count) * count + place[1 + lax.rem(t, count)],
                    0,
                    0,
                ),
            ),
        ),
        compiler_params=params_of(),
        cost_estimate=LIGHT,
        name="join_rows",
    )(place, *pieces)


def assemble(own, near, first, second, across):
    parts, rows, columns = near.shape
    count = parts + 1
    here = lax.axis_index("seq")
    place = [lax.axis_index("dp")] + [here ^ bits for bits in relative_bits()]
    place = jnp.stack(place).astype(jnp.int32)

    def kernel(place_ref, own_ref, near_ref, first_ref, second_ref, across_ref, out_ref, sem):
        along = place_ref[0]
        copies = [pltpu.make_async_copy(own_ref, out_ref.at[along], sem.at[0])]
        for step in range(parts):
            there = lax.rem(along + step + 1, count)
            for index, ref in enumerate((near_ref, first_ref, second_ref, across_ref)):
                copies.append(
                    pltpu.make_async_copy(
                        ref.at[step], out_ref.at[there, place_ref[1 + index]], sem.at[len(copies)]
                    )
                )
        for copy in copies:
            copy.start()
        for copy in copies:
            copy.wait()

    return pl.pallas_call(
        kernel,
        out_shape=jax.ShapeDtypeStruct((count, 4, rows, columns), own.dtype),
        in_specs=[pl.BlockSpec(memory_space=pltpu.SMEM)]
        + [pl.BlockSpec(memory_space=pl.ANY)] * 5,
        out_specs=pl.BlockSpec(memory_space=pltpu.VMEM),
        scratch_shapes=[pltpu.SemaphoreType.DMA((1 + 4 * parts,))],
        compiler_params=params_of(),
        cost_estimate=LIGHT,
        name="assemble",
    )(place, own, near, first, second, across)


def line_shifts(value):
    count = lax.axis_size("dp")
    return [
        lax.ppermute(value, "dp", [((to + step) % count, to) for to in range(count)])
        for step in range(1, count)
    ]


def line_gather(value):
    count = lax.axis_size("dp")
    line = lax.all_gather(value, "dp", axis=0)
    return lax.dynamic_slice_in_dim(
        jnp.concatenate([line, line], 0), lax.axis_index("dp") + 1, count - 1, 0
    )


def quarters_of(shard):
    return shard.reshape(4, shard.shape[0] // 4, shard.shape[1])


def spread(near):
    return swap_seq(near, FIRST), swap_seq(near, SECOND)


def spread_on(neighbours):
    return swap_seq(neighbours[1], FIRST)


def bits_of_place():
    core, here = lax.axis_index("section"), lax.axis_index("seq")
    x, y = lax.rem(here, 2), lax.div(here, 2)
    first, second = jnp.where(core == 0, x, y), jnp.where(core == 0, y, x)
    return jnp.stack([core, first, second]).astype(jnp.int32)


def grad_halves(left, right, count):
    length, depth = left.shape
    columns = right.shape[1]
    rows = depth // count
    quarter = round_up(rows, 32) // 4

    def kernel(bits_ref, left_ref, right_ref, keep_ref, send_ref, turned):
        block = pl.program_id(0)

        @pl.when(block == 0)
        def _():
            turned[...] = left_ref[...].astype(F32).T.astype(BF16).reshape(turned.shape)

        grad = dot(turned[block], right_ref[...], 1, 0)
        if 4 * quarter > rows:
            empty = jnp.zeros((4 * quarter - rows, columns), F32)
            grad = jnp.concatenate([grad, empty], axis=0)
        for at in range(4):
            part = grad[at * quarter : (at + 1) * quarter].astype(BF16)
            x, y = at % 2, at // 2
            first = jnp.where(bits_ref[0] == 0, x, y)
            second = jnp.where(bits_ref[0] == 0, y, x)

            @pl.when(first == bits_ref[1])
            def _():
                keep_ref[0, second] = part

            @pl.when(first != bits_ref[1])
            def _():
                send_ref[0, second] = part

    out = pl.BlockSpec((1, 2, quarter, columns), lambda z, bits: (z, 0, 0, 0))
    shape = jax.ShapeDtypeStruct((count, 2, quarter, columns), BF16)
    return pl.pallas_call(
        kernel,
        out_shape=(shape, shape),
        grid_spec=pltpu.PrefetchScalarGridSpec(
            num_scalar_prefetch=1,
            grid=(count,),
            in_specs=[
                pl.BlockSpec((length, depth), lambda z, bits: (0, 0)),
                pl.BlockSpec((length, columns), lambda z, bits: (0, 0)),
            ],
            out_specs=(out, out),
            scratch_shapes=[pltpu.VMEM((count, rows, length), BF16)],
        ),
        compiler_params=params_of(),
        cost_estimate=LIGHT,
        name="grad_halves",
    )(bits_of_place(), left, right)


def add_half(held, moved):
    count, _, rows, columns = held.shape

    def kernel(bits_ref, held_ref, moved_ref, keep_ref, send_ref):
        def total(index):
            return (held_ref[0, index].astype(F32) + moved_ref[0, index].astype(F32)).astype(BF16)

        keep_ref[0] = total(bits_ref[2])
        send_ref[0] = total(1 - bits_ref[2])

    both = pl.BlockSpec((1, 2, rows, columns), lambda z, bits: (z, 0, 0, 0))
    out = pl.BlockSpec((1, rows, columns), lambda z, bits: (z, 0, 0))
    shape = jax.ShapeDtypeStruct((count, rows, columns), BF16)
    return pl.pallas_call(
        kernel,
        out_shape=(shape, shape),
        grid_spec=pltpu.PrefetchScalarGridSpec(
            num_scalar_prefetch=1, grid=(count,), in_specs=[both, both], out_specs=(out, out)
        ),
        compiler_params=params_of(),
        cost_estimate=LIGHT,
        name="add_half",
    )(bits_of_place(), held, moved)


def add_low(left, right):
    return (left.astype(F32) + right.astype(F32)).astype(BF16)


class Sum:
    def __init__(self, left, right, count):
        self.keep, self.send = grad_halves(left, right, count)

    def first(self):
        self.moved = swap_seq(self.send, FIRST)

    def add(self):
        self.keep, self.send = add_half(self.keep, self.moved)

    def second(self):
        self.moved = swap_seq(self.send, SECOND)

    def over_line(self, gate):
        part = gate(add_low(self.keep, self.moved))
        self.line = lax.psum_scatter(part, "dp", scatter_dimension=0, tiled=True)[0]


def line_sum(part):
    line, count = lax.axis_index("dp"), lax.axis_size("dp")
    total = pick(part, line).astype(F32)
    for step in range(1, count):
        moved = lax.ppermute(
            pick(part, lax.rem(line + step, count)),
            "dp",
            [(source, (source + step) % count) for source in range(count)],
        )
        total = total + moved.astype(F32)
    return total.astype(BF16)


def plain_grad(left, right):
    depth, columns = left.shape[1], right.shape[1]

    def kernel(left_ref, right_ref, out_ref):
        turned = left_ref[...].astype(F32).T.astype(BF16)
        for start, end in tiles(columns):
            out_ref[:, start:end] = dot(turned, right_ref[:, start:end], 1, 0).astype(BF16)

    return whole_call(kernel, "plain_grad", [((depth, columns), BF16)], left, right)[0]


class Order:
    def __init__(self, token):
        self.token = token

    def __call__(self, *values):
        values, self.token = lax.optimization_barrier((values, self.token))
        return values if len(values) > 1 else values[0]

    def sent(self, *sums):
        for each in sums:
            each.send = self(each.send)

    def summed(self, *sums):
        for each in sums:
            each.line = self(each.line)

    def arrived(self, *sums):
        for each in sums:
            each.moved = self(each.moved)


def in_order(pieces):
    here = lax.axis_index("seq")
    return jnp.stack([pick(pieces, here ^ index) for index in range(4)])


def attention_forward(qkv, hidden_keys):
    length, width = qkv.shape
    width //= 3
    heads = width // HEAD_DIM

    def kernel(qkv_ref, hidden_ref, out_ref, lse_ref, q_s, k_s, v_s, o_s):
        head = pl.program_id(0)

        @pl.when(head == 0)
        def _():
            for index in range(heads):
                at = index * HEAD_DIM
                q_s[index] = qkv_ref[:, at : at + HEAD_DIM]
                k_s[index] = qkv_ref[:, width + at : width + at + HEAD_DIM]
                v_s[index] = qkv_ref[:, 2 * width + at : 2 * width + at + HEAD_DIM]

        scores = dot(k_s[head], q_s[head], 1, 1) * SCALE
        scores = jnp.where(hidden_ref[...] > 0, -1e9, scores)
        top = jnp.max(scores, axis=0, keepdims=True)
        expon = jnp.exp(scores - top)
        total = jnp.sum(expon, axis=0, keepdims=True)
        lse_ref[0] = top + jnp.log(total)
        mixed = dot(v_s[head], expon.astype(BF16), 0, 0) / total
        o_s[head] = mixed.T.astype(BF16)

        @pl.when(head == heads - 1)
        def _():
            for index in range(heads):
                out_ref[:, index * HEAD_DIM : (index + 1) * HEAD_DIM] = o_s[index]

    slab = pltpu.VMEM((heads, length, HEAD_DIM), BF16)
    return pl.pallas_call(
        kernel,
        grid=(heads,),
        out_shape=(
            jax.ShapeDtypeStruct((length, width), BF16),
            jax.ShapeDtypeStruct((heads, 1, length), F32),
        ),
        in_specs=[
            pl.BlockSpec((length, 3 * width), lambda h: (0, 0)),
            pl.BlockSpec((length, 1), lambda h: (0, 0)),
        ],
        out_specs=(
            pl.BlockSpec((length, width), lambda h: (0, 0)),
            pl.BlockSpec((1, 1, length), lambda h: (h, 0, 0)),
        ),
        scratch_shapes=[slab, slab, slab, slab],
        compiler_params=params_of(),
        cost_estimate=LIGHT,
        name="attention_forward",
    )(qkv, hidden_keys)


def attention_backward(qkv, d_out, lse, hidden_keys):
    length, width = d_out.shape
    heads = width // HEAD_DIM

    def kernel(
        qkv_ref, do_ref, lse_ref, hidden_ref, out_ref, sums_ref, q_s, k_s, v_s, do_s, dq_s, dk_s, dv_s
    ):
        head = pl.program_id(0)

        @pl.when(head == 0)
        def _():
            for index in range(heads):
                at = index * HEAD_DIM
                q_s[index] = qkv_ref[:, at : at + HEAD_DIM]
                k_s[index] = qkv_ref[:, width + at : width + at + HEAD_DIM]
                v_s[index] = qkv_ref[:, 2 * width + at : 2 * width + at + HEAD_DIM]
                do_s[index] = do_ref[:, at : at + HEAD_DIM]

        queries, keys, values, d_rows = q_s[head], k_s[head], v_s[head], do_s[head]
        scores = dot(keys, queries, 1, 1) * SCALE
        scores = jnp.where(hidden_ref[...] > 0, -1e9, scores)
        soft = jnp.exp(scores - lse_ref[0])
        d_soft = dot(values, d_rows, 1, 1)
        inner = jnp.sum(soft * d_soft, axis=0, keepdims=True)
        d_scores = (soft * (d_soft - inner)).astype(BF16)
        dv_s[head] = dot(soft.astype(BF16), d_rows, 1, 0).astype(BF16)
        dk_s[head] = (dot(d_scores, queries, 1, 0) * SCALE).astype(BF16)
        dq_s[head] = (dot(keys, d_scores, 0, 0) * SCALE).T.astype(BF16)

        @pl.when(head == heads - 1)
        def _():
            for index in range(heads):
                at = index * HEAD_DIM
                out_ref[:, at : at + HEAD_DIM] = dq_s[index]
                out_ref[:, width + at : width + at + HEAD_DIM] = dk_s[index]
                out_ref[:, 2 * width + at : 2 * width + at + HEAD_DIM] = dv_s[index]
            sums_ref[...] = jnp.sum(out_ref[...].astype(F32), axis=0, keepdims=True)

    slab = pltpu.VMEM((heads, length, HEAD_DIM), BF16)
    return pl.pallas_call(
        kernel,
        grid=(heads,),
        out_shape=(
            jax.ShapeDtypeStruct((length, 3 * width), BF16),
            jax.ShapeDtypeStruct((1, 3 * width), F32),
        ),
        in_specs=[
            pl.BlockSpec((length, 3 * width), lambda h: (0, 0)),
            pl.BlockSpec((length, width), lambda h: (0, 0)),
            pl.BlockSpec((1, 1, length), lambda h: (h, 0, 0)),
            pl.BlockSpec((length, 1), lambda h: (0, 0)),
        ],
        out_specs=(
            pl.BlockSpec((length, 3 * width), lambda h: (0, 0)),
            pl.BlockSpec((1, 3 * width), lambda h: (0, 0)),
        ),
        scratch_shapes=[slab] * 7,
        compiler_params=params_of(),
        cost_estimate=LIGHT,
        name="attention_backward",
    )(qkv, d_out, lse, hidden_keys)


def norm_parts(stream):
    centre = jnp.mean(stream, axis=-1, keepdims=True)
    offset = stream - centre
    spread = jnp.mean(offset * offset, axis=-1, keepdims=True)
    inverse = lax.rsqrt(spread + 1e-06)
    return offset * inverse, inverse


def tiles(total, step=256):
    return [(at, min(at + step, total)) for at in range(0, total, step)]


def whole_call(kernel, name, out_shapes, *arrays):
    shapes = tuple(jax.ShapeDtypeStruct(shape, dtype) for shape, dtype in out_shapes)
    return pl.pallas_call(
        kernel,
        out_shape=shapes,
        in_specs=whole_vmem(len(arrays)),
        out_specs=tuple(whole_vmem(len(shapes))),
        compiler_params=params_of(),
        cost_estimate=LIGHT,
        name=name,
    )(*arrays)


PIECES = 2


def piece_bounds(columns):
    step = round_up(columns // PIECES, 128)
    return [(at * step, min((at + 1) * step, columns)) for at in range(PIECES)]


def join_pieces(refs):
    return jnp.concatenate([ref[...] for ref in refs], axis=1).astype(F32)


def partial_product(left, weight, turned, name):
    length, depth = left.shape
    columns = weight.shape[0 if turned else 1]
    bounds = piece_bounds(columns)

    def kernel(left_ref, weight_ref, *out_refs):
        for start, end in tiles(columns):
            if turned:
                product = dot(left_ref[...], weight_ref[start:end, :depth], 1, 1)
            else:
                product = dot(left_ref[...], weight_ref[:, start:end], 1, 0)
            product = product.astype(BF16)
            for ref, (first, last) in zip(out_refs, bounds):
                low, high = max(start, first), min(end, last)
                if low < high:
                    ref[:, low - first : high - first] = product[:, low - start : high - start]

    shapes = [((length, last - first), BF16) for first, last in bounds]
    return whole_call(kernel, name, shapes, left, weight)


def project_in(base, partials, vectors, weight, shift):
    length, width = base.shape
    columns = weight.shape[1]

    def kernel(*refs):
        if partials is None:
            base_ref, vectors_ref, weight_ref, shift_ref, normed_ref, qkv_ref = refs
            stream = base_ref[...].astype(F32)
        else:
            base_ref, *refs = refs
            own_refs, other_refs = refs[:PIECES], refs[PIECES : 2 * PIECES]
            bias_ref, vectors_ref, weight_ref, shift_ref = refs[2 * PIECES : 2 * PIECES + 4]
            normed_ref, qkv_ref, stream_ref = refs[2 * PIECES + 4 :]
            stream = base_ref[...] + join_pieces(own_refs) + join_pieces(other_refs)
            stream_ref[...] = (stream + bias_ref[...]).astype(BF16)
            stream = stream_ref[...].astype(F32)
        normed = norm_parts(stream)[0] * vectors_ref[0:1, :] + vectors_ref[2:3, :]
        normed_ref[...] = normed.astype(BF16)
        for start, end in tiles(columns):
            product = dot(normed_ref[...], weight_ref[:, start:end], 1, 0)
            qkv_ref[:, start:end] = (product + shift_ref[:, start:end]).astype(BF16)

    shapes = [((length, width), BF16), ((length, columns), BF16)]
    if partials is None:
        normed, qkv = whole_call(kernel, "project_in", shapes, base, vectors, weight, shift)
        return base, normed, qkv
    shapes.append(((length, width), BF16))
    normed, qkv, stream = whole_call(
        kernel,
        "project_in",
        shapes,
        base,
        *partials[0],
        *partials[1],
        partials[2],
        vectors,
        weight,
        shift,
    )
    return stream, normed, qkv


def expand_hidden(stream, own, other, vectors, weight, shift):
    length, width = stream.shape
    columns = shift.shape[1]
    root = 0.7978845608028654

    def kernel(stream_ref, *refs):
        own_refs, other_refs, refs = refs[:PIECES], refs[PIECES : 2 * PIECES], refs[2 * PIECES :]
        vectors_ref, weight_ref, shift_ref, mid_ref, normed_ref, hidden_ref, slope_ref = refs
        middle = stream_ref[...].astype(F32) + join_pieces(own_refs)
        middle = middle + join_pieces(other_refs) + vectors_ref[6:7, :]
        mid_ref[...] = middle
        normed = norm_parts(middle)[0] * vectors_ref[1:2, :] + vectors_ref[3:4, :]
        normed_ref[...] = normed.astype(BF16)
        for start, end in tiles(columns):
            inner = dot(normed_ref[...], weight_ref[:, start:end], 1, 0) + shift_ref[:, start:end]
            square = inner * inner
            half_tanh = 0.5 * jnp.tanh(root * (inner + 0.044715 * square * inner))
            hidden_ref[:, start:end] = (inner * (0.5 + half_tanh)).astype(BF16)
            bend = (0.5 - 2.0 * half_tanh * half_tanh) * (root + 3 * 0.044715 * root * square)
            slope_ref[:, start:end] = (0.5 + half_tanh + inner * bend).astype(BF16)

    return whole_call(
        kernel,
        "expand_hidden",
        [
            ((length, width), F32),
            ((length, width), BF16),
            ((length, columns), BF16),
            ((length, columns), BF16),
        ],
        stream, *own, *other, vectors, weight, shift,
    )


def back_hidden(d_result, weight, slope):
    length, columns = slope.shape

    def kernel(d_ref, weight_ref, slope_ref, out_ref, sums_ref):
        for start, end in tiles(columns):
            d_hidden = dot(d_ref[...], weight_ref[start:end, :], 1, 1)
            d_pre = (d_hidden * slope_ref[:, start:end].astype(F32)).astype(BF16)
            out_ref[:, start:end] = d_pre
            sums_ref[:, start:end] = jnp.sum(d_pre.astype(F32), axis=0, keepdims=True)

    return whole_call(
        kernel,
        "back_hidden",
        [((length, columns), BF16), ((1, columns), F32)],
        d_result, weight, slope,
    )


def back_norm(base, own, other, stream, gain, weight):
    length, width = base.shape

    def kernel(*refs):
        base_ref, *refs = refs
        own_refs, other_refs, refs = refs[:PIECES], refs[PIECES : 2 * PIECES], refs[2 * PIECES :]
        stream_ref, gain_ref, *refs = refs
        unit, inverse = norm_parts(stream_ref[...].astype(F32))
        d_normed = join_pieces(own_refs) + join_pieces(other_refs)
        d_unit = d_normed * gain_ref[...]
        mean_d = jnp.mean(d_unit, axis=-1, keepdims=True)
        mean_du = jnp.mean(d_unit * unit, axis=-1, keepdims=True)
        base_wide = base_ref[...].astype(F32)
        total = base_wide + inverse * (d_unit - mean_d - unit * mean_du)
        if weight is None:
            low_ref, sums_ref = refs
        else:
            weight_ref, low_ref, sums_ref, wide_ref, product_ref = refs
            wide_ref[...] = total
        low_ref[...] = total.astype(BF16)
        sums_ref[0:1, :] = jnp.sum(d_normed * unit, axis=0, keepdims=True)
        sums_ref[1:2, :] = jnp.sum(d_normed, axis=0, keepdims=True)
        sums_ref[2:3, :] = jnp.sum(low_ref[...].astype(F32), axis=0, keepdims=True)
        sums_ref[3:4, :] = jnp.sum(base_wide, axis=0, keepdims=True)
        if weight is not None:
            for start, end in tiles(weight.shape[0]):
                product = dot(low_ref[...], weight_ref[start:end, :], 1, 1)
                product_ref[:, start:end] = product.astype(BF16)

    shapes = [((length, width), BF16), ((4, width), F32)]
    arrays = [base, *own, *other, stream, gain]
    if weight is not None:
        arrays.append(weight)
        shapes += [((length, width), F32), ((length, weight.shape[0]), BF16)]
    return whole_call(kernel, "back_norm", shapes, *arrays)


def column_sums(array):
    return jnp.sum(array.astype(F32), axis=0)


def on_device(
    section_inputs,
    key_mask,
    attention_in,
    attention_out,
    expand_weight,
    contract_weight,
    norm_gains,
    biases,
    expand_bias,
):
    core = lax.axis_index("section")
    here = lax.axis_index("seq")
    line = lax.axis_index("dp")
    count = lax.axis_size("dp")
    first = core == 0
    core_ref = core.astype(jnp.int32).reshape(1)

    width = attention_out.shape[2]
    own_rows = attention_out.shape[1]
    half_heads = own_rows // 2
    own_hidden = contract_weight.shape[1]
    half_hidden = round_up(round_up(own_hidden, 2) // 2, 16)
    in_runs = half_runs(3 * count * own_rows, 3 * count, half_heads, half_heads)
    hidden_runs = half_runs(count * own_hidden, count, half_hidden, half_hidden)
    in_width = 3 * count * half_heads
    hidden_width = count * half_hidden

    gate = Order(core)

    def both_layers(keep, send):
        received = swap_cores(send)
        return jnp.where(first, keep, received), jnp.where(first, received, keep)

    def pad_rows(array, step=32):
        extra = round_up(array.shape[-2], step) - array.shape[-2]
        if extra == 0:
            return array
        spec = [(0, 0)] * (array.ndim - 2) + [(0, extra), (0, 0)]
        return jnp.pad(array, spec)

    def prepared(halves):
        quarters = [quarters_of(pad_rows(half)) for half in halves]
        return quarters, [pick(quarter, here) for quarter in quarters]

    def built(own, near, others, rows):
        whole = assemble(own, near, *others)
        whole = whole.reshape(count, -1, whole.shape[3])[:, :rows]
        return whole.reshape(count * rows, whole.shape[2])

    micro, images, block, _ = section_inputs.shape[1:]
    tokens = section_inputs[0].reshape(micro * images, block, width)
    token_blocks = [pick(tokens, here ^ bits) for bits in range(4)]
    hidden_shift = jnp.pad(expand_bias[0], (0, 2 * half_hidden - own_hidden))
    packed = jnp.concatenate([norm_gains[0].reshape(-1), biases[0].reshape(-1), hidden_shift])
    small_size = packed.size
    packed = jnp.concatenate(both_layers(packed, packed))
    in_own, in_mine = prepared(
        both_layers(*split_columns(attention_in[0], in_runs, in_width, core_ref))
    )
    packed_rows = round_up(round_up(packed.size, in_width) // in_width, 8)
    packed = jnp.pad(packed, (0, packed_rows * in_width - packed.size)).reshape(-1, in_width)
    first_rows = in_mine[0].shape[0]
    in_first = jnp.concatenate([in_mine[0], packed], axis=0)
    token_blocks, in_first, expand_weight, attention_out, contract_weight = gate(
        token_blocks, in_first, expand_weight, attention_out, contract_weight
    )
    near_in_0 = line_shifts(in_first)
    inputs = [swap_seq(token_blocks[bits], (bits, 0)) for bits in range(1, 4)]
    out_parts = attention_out[0].reshape(2, half_heads, width)
    out_halves = both_layers(pick(out_parts, core), pick(out_parts, 1 - core))
    expand_halves = both_layers(
        *split_columns(expand_weight[0], hidden_runs, hidden_width, core_ref)
    )
    expand_own, expand_mine = prepared(
        [
            jnp.concatenate([high, low.reshape(own_rows, -1)], axis=1)
            for high, low in zip(expand_halves, out_halves)
        ]
    )
    expand_mine = gate(expand_mine)
    near_expand_0 = line_gather(expand_mine[0])

    def heads_of(merged):
        return merged[:, hidden_width:].reshape(count * half_heads, width)

    contract_parts = jnp.pad(
        contract_weight[0], ((0, 2 * half_hidden - own_hidden), (0, 0))
    ).reshape(2, half_hidden, width)
    contract_own, contract_mine = prepared(
        both_layers(pick(contract_parts, core), pick(contract_parts, 1 - core))
    )
    contract_mine = gate(contract_mine)
    near_contract_0 = line_gather(contract_mine[0])
    near_in_0, inputs = gate(near_in_0, inputs)
    packed = [packed] + [part[first_rows:] for part in near_in_0]
    near_in_0 = jnp.stack([part[:first_rows] for part in near_in_0])
    beside_in_0, near_expand_0 = gate(spread(near_in_0), near_expand_0)
    across_in_0 = spread_on(beside_in_0)
    image = jnp.concatenate([token_blocks[0], *inputs], axis=0)
    start = jnp.where(first, image, swap_cores(image))
    mask = pick(key_mask.reshape(micro * images, 4, block), here)
    mask = jnp.concatenate([pick(mask, here ^ bits) for bits in range(4)])
    hidden_keys = jnp.where(mask > 0, 0.0, 1.0).astype(F32)[:, None]

    packed = jnp.stack([part.reshape(-1) for part in packed])
    packed = lax.dynamic_slice_in_dim(
        jnp.concatenate([packed, packed], 0), lax.rem(count - line, count), count, 0
    ).astype(F32)

    def small_of(packed):
        vectors = packed[:, : 8 * own_rows].reshape(count, 8, own_rows)
        hidden = packed[:, 8 * own_rows :].reshape(count, 2, half_hidden)
        heads_part = pick(vectors.reshape(count, 8, 2, half_heads), core, 2)
        vectors = vectors.transpose(1, 0, 2).reshape(8, width)
        query, value = heads_part[:, 4].reshape(-1), heads_part[:, 5].reshape(-1)
        qkv_shift = jnp.concatenate([query, jnp.zeros_like(query), value])
        hidden_shift = pick(hidden, core, 1).reshape(1, -1)
        return vectors, qkv_shift.reshape(1, -1), hidden_shift

    vectors_0, qkv_shift_0, hidden_shift_0 = small_of(packed[:, :small_size])
    vectors_1, qkv_shift_1, hidden_shift_1 = small_of(packed[:, small_size : 2 * small_size])
    across_in_0, start, hidden_keys, qkv_shift_0, in_mine, expand_mine = gate(
        across_in_0, start, hidden_keys, qkv_shift_0, in_mine, expand_mine
    )

    beside_expand_0 = spread(near_expand_0)
    near_in_1 = line_shifts(in_mine[1])
    attn_in_0 = built(in_own[0], near_in_0, (*beside_in_0, across_in_0), own_rows)
    stream_0, normed_0, qkv_0 = project_in(start, None, vectors_0, attn_in_0, qkv_shift_0)
    beside_expand_0, near_in_1, qkv_0, expand_mine = gate(
        beside_expand_0, near_in_1, qkv_0, expand_mine
    )
    across_expand_0 = spread_on(beside_expand_0)
    near_in_1 = jnp.stack(near_in_1)
    beside_in_1 = spread(near_in_1)
    near_expand_1 = line_gather(expand_mine[1])
    mixed_0, lse_0 = attention_forward(qkv_0, hidden_keys)
    mixed_0, across_expand_0 = gate(mixed_0, across_expand_0)
    expand_0 = built(expand_own[0], near_expand_0, (*beside_expand_0, across_expand_0), own_rows)
    attn_out_0 = heads_of(expand_0)
    own = partial_product(mixed_0, attn_out_0, False, "project_heads")
    own, beside_in_1, near_contract_0, contract_mine = gate(
        own, beside_in_1, near_contract_0, contract_mine
    )
    across_in_1 = spread_on(beside_in_1)
    beside_contract_0 = spread(near_contract_0)
    near_contract_1 = line_gather(contract_mine[1])
    own, other = gate(own, swap_cores(own))
    middle_0, normed_mid_0, hidden_0, slope_0 = expand_hidden(
        stream_0, own, other, vectors_0, expand_0, hidden_shift_0
    )
    hidden_0, across_in_1, beside_contract_0, near_expand_1 = gate(
        hidden_0, across_in_1, beside_contract_0, near_expand_1
    )
    across_contract_0 = spread_on(beside_contract_0)
    beside_expand_1 = spread(near_expand_1)
    attn_in_1 = built(in_own[1], near_in_1, (*beside_in_1, across_in_1), own_rows)
    attn_in_1, across_contract_0 = gate(attn_in_1, across_contract_0)
    contract_0 = built(
        contract_own[0], near_contract_0, (*beside_contract_0, across_contract_0), half_hidden
    )
    own = gate(partial_product(hidden_0, contract_0, False, "contract_hidden"))
    own, other, token_blocks = gate(own, swap_cores(own), token_blocks)

    cotangents = [swap_seq(token_blocks[bits], (0, bits)) for bits in range(1, 3)]
    partials = (own, other, vectors_0[7:8])
    stream_1, normed_1, qkv_1 = project_in(middle_0, partials, vectors_1, attn_in_1, qkv_shift_1)
    beside_expand_1, near_contract_1, qkv_1, cotangents, token_blocks = gate(
        beside_expand_1, near_contract_1, qkv_1, cotangents, token_blocks
    )
    across_expand_1 = spread_on(beside_expand_1)
    beside_contract_1 = spread(near_contract_1)
    cotangents.append(swap_seq(token_blocks[3], (0, 3)))
    mixed_1, lse_1 = attention_forward(qkv_1, hidden_keys)
    mixed_1, across_expand_1 = gate(mixed_1, across_expand_1)
    expand_1 = built(expand_own[1], near_expand_1, (*beside_expand_1, across_expand_1), own_rows)
    attn_out_1 = heads_of(expand_1)
    own = partial_product(mixed_1, attn_out_1, False, "project_heads")
    own, beside_contract_1, cotangents = gate(own, beside_contract_1, cotangents)
    across_contract_1 = spread_on(beside_contract_1)
    image = jnp.concatenate([token_blocks[0], *cotangents], axis=0)
    own, other = gate(own, swap_cores(own))
    cotangent = jnp.where(first, swap_cores(image), image)
    middle_1, normed_mid_1, hidden_1, slope_1 = expand_hidden(
        stream_1, own, other, vectors_1, expand_1, hidden_shift_1
    )
    hidden_1, across_contract_1, cotangent = gate(hidden_1, across_contract_1, cotangent)

    small_rows = round_up(7 + round_up(hidden_width, width) // width, 16)

    def out_sum(grad, in_sums, mid_sums, hidden_sums, qkv_sums):
        heads = [qkv_sums[:, : width // 2], qkv_sums[:, width:]]
        rows = [in_sums[:1], mid_sums[:1], in_sums[1:2], mid_sums[1:], jnp.concatenate(heads, axis=1)]
        spare = (small_rows - 7) * width - hidden_width
        rows.append(jnp.pad(hidden_sums, ((0, 0), (0, spare))).reshape(-1, width))
        small = jnp.concatenate(rows, axis=0).astype(BF16)
        small = jnp.broadcast_to(small, (count, small_rows, width))
        parts = [grad.reshape(count, half_heads, width), small]
        part = gate(jnp.concatenate(parts, axis=1))
        return lax.psum_scatter(part, "dp", scatter_dimension=0, tiled=True)[0]

    def own_layer(low, high):
        return jnp.stack([jnp.where(first, low, high), swap_cores(jnp.where(first, high, low))])

    def last_place():
        return jnp.stack([gate.token, *(here ^ bits for bits in relative_bits())]).astype(jnp.int32)

    def rows_of(pieces, total):
        return join_rows(pieces, total, last_place())

    def columns_of(pieces, runs, total):
        return join_columns(pieces, runs, total, last_place())

    contract_sum_1 = Sum(hidden_1, cotangent, count)
    gate.sent(contract_sum_1)
    contract_sum_1.first()
    contract_1 = built(
        contract_own[1], near_contract_1, (*beside_contract_1, across_contract_1), half_hidden
    )
    d_pre_1, hidden_sums_1 = back_hidden(cotangent, contract_1, slope_1)
    d_pre_1 = gate(d_pre_1)
    expand_sum_1 = Sum(normed_mid_1, d_pre_1, count)
    gate.sent(expand_sum_1)
    expand_sum_1.first()
    own = gate(partial_product(gate(d_pre_1), expand_1, True, "back_expand"))
    gate.arrived(contract_sum_1)
    contract_sum_1.add()
    own_out = partial_product(hidden_1, contract_1, False, "contract_hidden")
    own, other, own_out = gate(own, swap_cores(own), own_out)
    gate.sent(contract_sum_1)
    contract_sum_1.second()
    d_branch_1, mid_sums_1, d_middle_1, d_mixed_1 = back_norm(
        cotangent, own, other, middle_1, vectors_1[1:2], attn_out_1
    )
    d_branch_1, d_mixed_1 = gate(d_branch_1, d_mixed_1)
    out_grad_1 = gate(plain_grad(mixed_1, d_branch_1))
    d_qkv_1, qkv_sums_1 = gate(attention_backward(qkv_1, gate(d_mixed_1), lse_1, hidden_keys))
    gate.arrived(contract_sum_1)
    contract_sum_1.over_line(gate)
    gate.arrived(expand_sum_1)
    expand_sum_1.add()
    gate.sent(expand_sum_1)
    expand_sum_1.second()
    in_sum_1 = Sum(normed_1, gate(d_qkv_1), count)
    gate.sent(in_sum_1)
    in_sum_1.first()
    own = gate(partial_product(gate(d_qkv_1), attn_in_1, True, "back_in"))
    own, other, other_out = gate(own, swap_cores(own), swap_cores(own_out))
    gate.arrived(expand_sum_1)
    expand_sum_1.over_line(gate)
    own_out, other_out = jnp.concatenate(own_out, axis=1), jnp.concatenate(other_out, axis=1)
    output = middle_1 + own_out.astype(F32) + other_out.astype(F32) + vectors_1[7:8]
    output = output.astype(BF16)
    d_result_0, in_sums_1 = back_norm(d_middle_1, own, other, stream_1, vectors_1[0:1], None)
    d_result_0 = gate(d_result_0)

    contract_sum_0 = Sum(hidden_0, gate(d_result_0), count)
    gate.sent(contract_sum_0)
    contract_sum_0.first()
    gate.arrived(in_sum_1)
    in_sum_1.add()
    gate.sent(in_sum_1)
    in_sum_1.second()
    d_pre_0, hidden_sums_0 = back_hidden(gate(d_result_0), contract_0, slope_0)
    d_pre_0, output = gate(d_pre_0, output)
    expand_sum_0 = Sum(normed_mid_0, gate(d_pre_0), count)
    gate.sent(expand_sum_0)
    expand_sum_0.first()
    gate.arrived(in_sum_1)
    in_sum_1.over_line(gate)
    gate.summed(contract_sum_1)
    own = gate(partial_product(gate(d_pre_0), expand_0, True, "back_expand"))
    gate.arrived(contract_sum_0)
    contract_sum_0.add()
    own, other = gate(own, swap_cores(own))
    gate.sent(contract_sum_0)
    contract_sum_0.second()
    d_branch_0, mid_sums_0, d_middle_0, d_mixed_0 = back_norm(
        d_result_0, gate(own), other, middle_0, vectors_0[1:2], attn_out_0
    )
    d_branch_0, d_mixed_0 = gate(d_branch_0, d_mixed_0)
    out_grad_0 = gate(plain_grad(mixed_0, d_branch_0))
    gate.summed(expand_sum_1)
    out_line_1 = out_sum(out_grad_1, in_sums_1, mid_sums_1, hidden_sums_1, qkv_sums_1)
    output = output.reshape(4, block, width)
    outputs = [swap_seq(output[bits], (0, bits)) for bits in range(1, 4)]
    d_qkv_0, qkv_sums_0 = gate(attention_backward(qkv_0, gate(d_mixed_0), lse_0, hidden_keys))
    outputs = gate(outputs)
    gate.arrived(expand_sum_0)
    expand_sum_0.add()
    gate.sent(expand_sum_0)
    expand_sum_0.second()
    gate.arrived(contract_sum_0)
    contract_sum_0.over_line(gate)
    in_sum_0 = Sum(normed_0, gate(d_qkv_0), count)
    gate.sent(in_sum_0)
    in_sum_0.first()
    gate.summed(in_sum_1)
    own = gate(partial_product(gate(d_qkv_0), attn_in_0, True, "back_in"))
    own, other = gate(own, swap_cores(own))
    gate.arrived(expand_sum_0)
    expand_sum_0.over_line(gate)
    d_input_0, in_sums_0 = back_norm(d_middle_0, gate(own), other, stream_0, vectors_0[0:1], None)
    d_input_0, out_line_1 = gate(d_input_0, out_line_1)

    d_input_0 = d_input_0.reshape(4, block, width)
    gate.arrived(in_sum_0)
    in_sum_0.add()
    gate.summed(contract_sum_0)
    gate.sent(in_sum_0)
    in_sum_0.second()
    contract_near = own_layer(contract_sum_0.line, contract_sum_1.line)
    gate.arrived(in_sum_0)
    contract_near = gate(contract_near)
    contract_beside = spread(contract_near)
    in_sum_0.over_line(gate)
    gate.summed(expand_sum_0)
    contract_beside = gate(contract_beside)
    contract_across = spread_on(contract_beside)
    inputs_back = [swap_seq(d_input_0[bits], (bits, 0)) for bits in range(1, 3)]
    expand_near = own_layer(expand_sum_0.line, expand_sum_1.line)
    contract_across, inputs_back, expand_near = gate(contract_across, inputs_back, expand_near)
    expand_beside = spread(expand_near)
    inputs_back.append(swap_seq(d_input_0[3], (3, 0)))
    grad_contract = rows_of([contract_near, *contract_beside, contract_across], own_hidden)
    gate.summed(in_sum_0)
    out_line_0 = out_sum(out_grad_0, in_sums_0, mid_sums_0, hidden_sums_0, qkv_sums_0)
    expand_beside, grad_contract, inputs_back = gate(expand_beside, grad_contract, inputs_back)
    in_near = gate(own_layer(in_sum_0.line, in_sum_1.line))
    in_beside = spread(in_near)
    expand_across = spread_on(expand_beside)
    in_beside, expand_across = gate(in_beside, expand_across)
    in_across = spread_on(in_beside)
    grad_expand = columns_of(
        [expand_near, *expand_beside, expand_across], hidden_runs, count * own_hidden
    )
    out_line_0, in_across, grad_expand = gate(out_line_0, in_across, grad_expand)
    out_near = gate(own_layer(out_line_0, out_line_1))
    out_moved = swap_seq(out_near, FIRST)
    grad_in = columns_of([in_near, *in_beside, in_across], in_runs, 3 * width)
    out_moved, grad_in = gate(out_moved, grad_in)
    out_near = add_low(out_near, out_moved)
    out_moved = swap_seq(out_near, SECOND)
    returned = [
        jnp.where(first, low, high)
        for low, high in zip([d_input_0[0], *inputs_back], [output[0], *outputs])
    ]
    results = in_order(jnp.stack(returned)).astype(F32)
    results = results.reshape(1, micro, images, block, width)
    out_near = add_low(out_near, gate(out_moved)).astype(F32)
    mine, other = out_near[0, :half_heads], out_near[1, :half_heads]
    grad_out = jnp.concatenate([jnp.where(first, mine, other), jnp.where(first, other, mine)])

    def own_part(rows, size):
        return lax.dynamic_slice_in_dim(rows, line * size, size, rows.ndim - 1)

    def halves_of(mine, other, size):
        mine, other = own_part(mine, size), own_part(other, size)
        low, high = jnp.where(first, mine, other), jnp.where(first, other, mine)
        return jnp.concatenate([low, high], axis=-1)

    mine, other = out_near[0, half_heads:], out_near[1, half_heads:]
    shared = own_part(mine[:6], own_rows)
    query = halves_of(mine[6, : width // 2], other[6, : width // 2], half_heads)
    value = halves_of(mine[6, width // 2 :], other[6, width // 2 :], half_heads)
    hidden = [rows[7:].reshape(-1)[:hidden_width] for rows in (mine, other)]
    hidden = halves_of(*hidden, half_hidden)[:own_hidden]
    grad_shifts = jnp.concatenate([shared[2:4], query[None], value[None], shared[4:6]])

    return (
        results,
        grad_in[None],
        grad_out[None],
        grad_expand[None],
        grad_contract.transpose(1, 0, 2),
        shared[None, :2],
        grad_shifts[None],
        hidden[None],
    )


def plain_passed_along(value, axis, steps):
    count = lax.axis_size(axis)
    initial, last = (max(0, -steps), min(count, count - steps))
    return lax.ppermute(value, axis, [(source, source + steps) for source in range(initial, last)])


def plain_layer_norm(stream, gain, shift):
    centre = jnp.mean(stream, axis=-1, keepdims=True)
    offset = stream - centre
    spread = jnp.mean(offset * offset, axis=-1, keepdims=True)
    return offset * lax.rsqrt(spread + 1e-06) * gain + shift


def plain_matmul(left, right):
    return jnp.dot(left, right, preferred_element_type=F32)


def plain_left_matmul(left, right):
    return lax.dot_general(
        left, right, (((0,), (0,)), ((), ())), preferred_element_type=F32
    )


def plain_right_matmul(left, right):
    return lax.dot_general(
        left, right, (((1,), (1,)), ((), ())), preferred_element_type=F32
    )


def plain_gather_once(local):
    whole = (
        lax.all_gather(local[0], "dp", axis=1, tiled=True),
        lax.all_gather(local[1], "dp", axis=1, tiled=True),
        lax.all_gather(local[2], "dp", axis=1, tiled=True),
        lax.all_gather(local[3], "dp", axis=1, tiled=True),
        lax.all_gather(local[4], "dp", axis=2, tiled=True),
        lax.all_gather(local[5], "dp", axis=2, tiled=True),
        lax.all_gather(local[6], "dp", axis=1, tiled=True),
    )
    return tuple((piece[0] for piece in whole))


def plain_split_heads(heads):
    images, length, _, width = heads.shape
    count = width // HEAD_DIM
    queries = heads[:, :, 0].reshape(images, length, count, HEAD_DIM)
    key_rows = heads[:, :, 1].reshape(images, length, count, HEAD_DIM)
    value_rows = heads[:, :, 2].reshape(images, length, count, HEAD_DIM)
    return (queries, key_rows, value_rows)


def plain_head_scores(queries, key_rows, visible):
    scores = jnp.einsum(
        "nqhd,nkhd->nhqk", queries, key_rows, preferred_element_type=F32
    ) * HEAD_DIM ** (-0.5)
    return jnp.where(visible[:, None, None, :], scores, -1000000000.0)


def plain_attend(heads, visible):
    images, length, _, width = heads.shape
    queries, key_rows, value_rows = plain_split_heads(heads)
    scores = plain_head_scores(queries, key_rows, visible)
    row_max = jnp.max(scores, axis=-1, keepdims=True)
    expon = jnp.exp(scores - row_max)
    total = jnp.sum(expon, axis=-1, keepdims=True)
    softmaxed = (expon / total).astype(BF16)
    log_total = (row_max + jnp.log(total))[..., 0]
    mixture = jnp.einsum(
        "nhqk,nkhd->nqhd", softmaxed, value_rows, preferred_element_type=F32
    )
    return (mixture.astype(BF16).reshape(images, length, width), log_total)


def plain_attend_back(heads, log_total, visible, d_mixture):
    images, length, _, width = heads.shape
    queries, key_rows, value_rows = plain_split_heads(heads)
    d_rows = d_mixture.reshape(queries.shape)
    scores = plain_head_scores(queries, key_rows, visible)
    softmaxed = jnp.exp(scores - log_total[..., None])
    d_soft = jnp.einsum("nqhd,nkhd->nhqk", d_rows, value_rows, preferred_element_type=F32)
    inner = jnp.sum(softmaxed * d_soft, axis=-1, keepdims=True)
    d_scores = (softmaxed * (d_soft - inner)).astype(BF16)
    scale = HEAD_DIM ** (-0.5)
    d_queries = (
        jnp.einsum("nhqk,nkhd->nqhd", d_scores, key_rows, preferred_element_type=F32)
        * scale
    ).astype(BF16)
    d_keys = (
        jnp.einsum("nhqk,nqhd->nkhd", d_scores, queries, preferred_element_type=F32) * scale
    ).astype(BF16)
    d_values = jnp.einsum(
        "nhqk,nqhd->nkhd",
        softmaxed.astype(BF16),
        d_rows,
        preferred_element_type=F32,
    ).astype(BF16)
    return jnp.stack([d_queries, d_keys, d_values], axis=2).reshape(images, length, 3, width)


def plain_forward_layer(stream_in, visible, params):
    attn_in, attn_out, expand, contract, gains, shifts, expand_shift = params
    images, rows_seq, width = stream_in.shape
    stream = stream_in.astype(F32).reshape(-1, width)
    gains32 = gains.astype(F32)
    shifts32 = shifts.astype(F32)
    normed = plain_layer_norm(stream, gains32[0], shifts32[0]).astype(BF16)
    qkv_shift = jnp.stack([shifts32[2], jnp.zeros_like(shifts32[2]), shifts32[3]])
    projected = (plain_matmul(normed, attn_in).reshape(images, rows_seq, 3, width) + qkv_shift).astype(
        BF16
    )
    heads = lax.all_to_all(projected, "seq", split_axis=3, concat_axis=1, tiled=True)
    mixture, log_total = plain_attend(heads, visible)
    mixed_rows = lax.all_to_all(mixture, "seq", split_axis=1, concat_axis=2, tiled=True).reshape(
        -1, width
    )
    middle = stream + plain_matmul(mixed_rows, attn_out) + shifts32[4]
    normed_mid = plain_layer_norm(middle, gains32[1], shifts32[1]).astype(BF16)
    hidden_pre = plain_matmul(normed_mid, expand) + expand_shift.astype(F32)
    hidden = jax.nn.gelu(hidden_pre, approximate=True).astype(BF16)
    result = middle + plain_matmul(hidden, contract) + shifts32[5]
    saved = (
        stream_in,
        normed,
        heads,
        log_total,
        mixed_rows,
        middle,
        normed_mid,
        hidden_pre,
        hidden,
        visible,
    )
    return (result.reshape(images, rows_seq, width), saved)


def plain_backward_layer(d_result, saved, params):
    attn_in, attn_out, expand, contract, gains, shifts, expand_shift = params
    (
        stream_in,
        normed,
        heads,
        log_total,
        mixed_rows,
        middle,
        normed_mid,
        hidden_pre,
        hidden,
        visible,
    ) = saved
    images, rows_seq, width = d_result.shape
    gains32 = gains.astype(F32)
    shifts32 = shifts.astype(F32)
    d_flat = d_result.reshape(-1, width)
    d_wide = d_flat.astype(F32)
    grad_contract = plain_left_matmul(hidden, d_flat)
    grad_last_bias = jnp.sum(d_wide, axis=0)
    d_hidden = plain_right_matmul(d_flat, contract)
    _, gelu_back = jax.vjp(lambda inner: jax.nn.gelu(inner, approximate=True), hidden_pre)
    d_pre = gelu_back(d_hidden)[0].astype(BF16)
    grad_expand = plain_left_matmul(normed_mid, d_pre)
    grad_expand_bias = jnp.sum(d_pre.astype(F32), axis=0)
    d_normed_mid = plain_right_matmul(d_pre, expand)
    _, norm_back_mid = jax.vjp(plain_layer_norm, middle, gains32[1], shifts32[1])
    d_middle_part, grad_gain_mid, grad_shift_mid = norm_back_mid(d_normed_mid)
    d_middle = d_wide + d_middle_part
    d_branch = d_middle.astype(BF16)
    grad_out_bias = jnp.sum(d_branch.astype(F32), axis=0)
    grad_attn_out = plain_left_matmul(mixed_rows, d_branch)
    d_mixture = (
        plain_right_matmul(d_branch, attn_out).astype(BF16).reshape(images, rows_seq, width)
    )
    d_heads = lax.all_to_all(d_mixture, "seq", split_axis=2, concat_axis=1, tiled=True)
    d_projected_heads = plain_attend_back(heads, log_total, visible, d_heads)
    d_projected = lax.all_to_all(
        d_projected_heads, "seq", split_axis=1, concat_axis=3, tiled=True
    ).reshape(-1, 3 * width)
    grad_attn_in = plain_left_matmul(normed, d_projected)
    column_sums = jnp.sum(d_projected.astype(F32), axis=0).reshape(3, width)
    d_normed = plain_right_matmul(d_projected, attn_in)
    stream = stream_in.astype(F32).reshape(-1, width)
    _, norm_back_in = jax.vjp(plain_layer_norm, stream, gains32[0], shifts32[0])
    d_stream_part, grad_gain_in, grad_shift_in = norm_back_in(d_normed)
    d_stream = d_middle + d_stream_part
    grad_gains = jnp.stack([grad_gain_in, grad_gain_mid])
    grad_shifts = jnp.stack(
        [
            grad_shift_in,
            grad_shift_mid,
            column_sums[0],
            column_sums[2],
            grad_out_bias,
            grad_last_bias,
        ]
    )
    grads = (
        grad_attn_in,
        grad_attn_out,
        grad_expand,
        grad_contract,
        grad_gains,
        grad_shifts,
        grad_expand_bias,
    )
    return (d_stream.reshape(images, rows_seq, width), grads)


def plain_send_forward(values):
    return plain_passed_along(values, "section", 1)


def plain_send_backward(values):
    return plain_passed_along(values, "section", -1)


def on_device_any(
    section_inputs,
    key_mask,
    attention_in,
    attention_out,
    expand_weight,
    contract_weight,
    norm_gains,
    biases,
    expand_bias,
):
    micro = section_inputs.shape[1]
    leading = lax.axis_index("section") == 0
    local = (
        attention_in,
        attention_out,
        expand_weight,
        contract_weight,
        norm_gains,
        biases,
        expand_bias,
    )
    sources = section_inputs[0]
    visible_all = key_mask > 0
    blank = jnp.zeros_like(sources[0])
    recv_forward = blank
    recv_backward = blank
    saves = {}
    outputs = [None] * micro
    input_grads = [None] * micro
    totals = None
    params = plain_gather_once(local)
    for tick in range(micro + 2):
        if tick <= micro:
            source = sources[tick] if tick < micro else blank
            stream_now = jnp.where(leading, source, recv_forward)
            visible_now = jnp.where(
                leading, visible_all[min(tick, micro - 1)], visible_all[max(tick - 1, 0)]
            )
            result, saved = plain_forward_layer(stream_now, visible_now, params)
            saves[tick] = saved
            if tick >= 1:
                outputs[tick - 1] = result
            sent_forward = plain_send_forward(result.astype(BF16))
        if tick >= 1:
            early = saves[tick - 2] if tick - 2 in saves else saves[tick]
            later = saves[tick] if tick in saves else saves[tick - 2]
            chosen = jax.tree.map(
                lambda left_one, right_one: jnp.where(leading, left_one, right_one), early, later
            )
            cotangent = sources[tick - 1] if tick <= micro else blank
            d_result = jnp.where(leading, recv_backward, cotangent)
            d_stream, grads = plain_backward_layer(d_result, chosen, params)
            active = jnp.where(leading, tick >= 2, tick <= micro)
            grads = tuple((jnp.where(active, piece, 0.0) for piece in grads))
            if tick >= 2:
                input_grads[tick - 2] = d_stream
            totals = (
                grads if totals is None else tuple((old + new for old, new in zip(totals, grads)))
            )
            recv_backward = plain_send_backward(d_stream.astype(BF16))
        if tick <= micro:
            recv_forward = sent_forward
    totals = (
        lax.psum_scatter(
            totals[0].astype(BF16), "dp", scatter_dimension=0, tiled=True
        ).astype(F32),
        lax.psum_scatter(
            totals[1].astype(BF16), "dp", scatter_dimension=0, tiled=True
        ).astype(F32),
        lax.psum_scatter(
            totals[2].astype(BF16), "dp", scatter_dimension=0, tiled=True
        ).astype(F32),
        lax.psum_scatter(
            totals[3].astype(BF16), "dp", scatter_dimension=0, tiled=True
        ).astype(F32),
        lax.psum_scatter(
            totals[4].astype(BF16), "dp", scatter_dimension=1, tiled=True
        ).astype(F32),
        lax.psum_scatter(
            totals[5].astype(BF16), "dp", scatter_dimension=1, tiled=True
        ).astype(F32),
        lax.psum_scatter(
            totals[6].astype(BF16), "dp", scatter_dimension=0, tiled=True
        ).astype(F32),
    )
    totals = (
        lax.psum(totals[0].astype(BF16), "seq").astype(F32),
        lax.psum(totals[1].astype(BF16), "seq").astype(F32),
        lax.psum(totals[2].astype(BF16), "seq").astype(F32),
        lax.psum(totals[3].astype(BF16), "seq").astype(F32),
        lax.psum(totals[4].astype(BF16), "seq").astype(F32),
        lax.psum(totals[5].astype(BF16), "seq").astype(F32),
        lax.psum(totals[6].astype(BF16), "seq").astype(F32),
    )
    results = jnp.stack(
        [jnp.where(leading, input_grads[index], outputs[index]) for index in range(micro)]
    )[None]
    return (
        results,
        totals[0][None],
        totals[1][None],
        totals[2][None],
        totals[3][None],
        totals[4][None],
        totals[5][None],
        totals[6][None],
    )


def solution(mesh):
    in_specs = (
        P("section", None, "dp", "seq", None),
        P(None, "dp", None),
        P("section", "dp", None),
        P("section", "dp", None),
        P("section", "dp", None),
        P("section", "dp", None),
        P("section", None, "dp"),
        P("section", None, "dp"),
        P("section", "dp"),
    )
    out_specs = (
        P("section", None, "dp", "seq", None),
        P("section", "dp", None),
        P("section", "dp", None),
        P("section", "dp", None),
        P("section", "dp", None),
        P("section", None, "dp"),
        P("section", None, "dp"),
        P("section", "dp"),
    )

    def by_size(section_inputs, *others):
        _, micro, images, _, _ = section_inputs.shape
        one_image_each = micro * images == lax.axis_size("seq") == 4
        rows, hidden = others[2].shape[1], others[4].shape[1]
        even = rows % (2 * HEAD_DIM) == 0 and rows % 32 == 0
        even = even and round_up(round_up(hidden, 2) // 2, 16) % 32 == 0
        plan = on_device if one_image_each and even else on_device_any
        return plan(section_inputs, *others)

    return jax.shard_map(
        by_size, mesh=mesh, in_specs=in_specs, out_specs=out_specs, check_vma=False
    )
```

```python
import jax
import jax.numpy as jnp
from jax import lax
from jax.experimental import pallas as pl
from jax.experimental.pallas import tpu as pltpu
from jax.sharding import PartitionSpec as P

HEAD_DIM = 72
SCALE = HEAD_DIM**-0.5
VMEM_LIMIT = 32 * 1024 * 1024
F32 = jnp.float32
BF16 = jnp.bfloat16
LIGHT = pl.CostEstimate(flops=1, bytes_accessed=1, transcendentals=0)


def round_up(value, step):
    return -(-value // step) * step


def pick(array, index, axis=0):
    return lax.dynamic_index_in_dim(array, index, axis, keepdims=False)


def swap_cores(value):
    swap = [(0, 1), (1, 0)]
    return jax.tree.map(lambda array: lax.ppermute(array, "section", swap), value)


def swap_seq(value, bits):
    bits = bits if isinstance(bits, tuple) else (bits, bits)
    count = lax.axis_size("seq")
    pairs = [
        (core * count + index, core * count + (index ^ bits[core]))
        for core in range(2)
        for index in range(count)
        if bits[core]
    ]
    return lax.ppermute(value, ("section", "seq"), pairs)


FIRST, SECOND = (1, 2), (2, 1)


def relative_bits():
    core = lax.axis_index("section")
    return (0, 1 + core, 2 - core, 3)


def dot(left, right, left_axis, right_axis):
    return lax.dot_general(
        left, right, (((left_axis,), (right_axis,)), ((), ())), preferred_element_type=F32
    )


def params_of(limit=VMEM_LIMIT):
    return pltpu.CompilerParams(vmem_limit_bytes=limit)


def whole_vmem(count):
    return [pl.BlockSpec(memory_space=pltpu.VMEM)] * count


def half_runs(total, parts, half, width):
    size = total // parts
    runs = [[], []]
    for part in range(parts):
        runs[0].append((part * size, half, part * width))
        runs[1].append((part * size + half, size - half, part * width))
    return runs


def split_columns(weight, runs, width, core):
    rows = weight.shape[0]

    def kernel(core_ref, whole_ref, keep_ref, send_ref):
        def write(ref, pieces):
            if sum(size for _, size, _ in pieces) < width:
                ref[...] = jnp.zeros_like(ref)
            for start, size, place in pieces:
                ref[:, place : place + size] = whole_ref[:, start : start + size]

        @pl.when(core_ref[0] == 0)
        def _():
            write(keep_ref, runs[0])
            write(send_ref, runs[1])

        @pl.when(core_ref[0] == 1)
        def _():
            write(keep_ref, runs[1])
            write(send_ref, runs[0])

    shape = jax.ShapeDtypeStruct((rows, width), weight.dtype)
    return pl.pallas_call(
        kernel,
        out_shape=(shape, shape),
        in_specs=[pl.BlockSpec(memory_space=pltpu.SMEM)] + whole_vmem(1),
        out_specs=tuple(whole_vmem(2)),
        compiler_params=params_of(),
        cost_estimate=LIGHT,
        name="split_columns",
    )(core, weight)


def join_columns(pieces, runs, total, place):
    count = len(pieces)
    _, rows, width = pieces[0].shape

    def kernel(place_ref, *refs):
        out_ref = refs[count]

        def write(piece_ref, halves):
            for half, parts in zip(halves, runs):
                for start, size, at in parts:
                    value = piece_ref[half, :, at : at + size]
                    out_ref[0, :, start : start + size] = value.astype(F32)

        for index in range(count):
            for core, halves in enumerate(((0, 1), (1, 0))):

                @pl.when(jnp.logical_and(pl.program_id(0) == index, place_ref[0] == core))
                def _(index=index, halves=halves):
                    write(refs[index], halves)

    whole = pl.BlockSpec((2, rows, width), lambda j, place: (0, 0, 0))
    out = pl.pallas_call(
        kernel,
        out_shape=jax.ShapeDtypeStruct((count, rows, total), F32),
        grid_spec=pltpu.PrefetchScalarGridSpec(
            num_scalar_prefetch=1,
            grid=(count,),
            in_specs=[whole] * count,
            out_specs=pl.BlockSpec((1, rows, total), lambda j, place: (place[1 + j], 0, 0)),
        ),
        compiler_params=params_of(),
        cost_estimate=LIGHT,
        name="join_columns",
    )(place, *pieces)
    return out.reshape(count * rows, total)


def join_rows(pieces, total, place):
    count = len(pieces)
    _, rows, width = pieces[0].shape

    def kernel(place_ref, *refs):
        out_ref = refs[count]
        half, step = pl.program_id(0) // count, lax.rem(pl.program_id(0), count)
        which = jnp.where(half == place_ref[0], 0, 1)
        for index in range(count):

            @pl.when(step == index)
            def _(index=index):
                out_ref[:, 0, :] = refs[index][which].astype(F32)

    whole = pl.BlockSpec((2, rows, width), lambda t, place: (0, 0, 0))
    return pl.pallas_call(
        kernel,
        out_shape=jax.ShapeDtypeStruct((total, 1, width), F32),
        grid_spec=pltpu.PrefetchScalarGridSpec(
            num_scalar_prefetch=1,
            grid=(2 * count,),
            in_specs=[whole] * count,
            out_specs=pl.BlockSpec(
                (rows, 1, width),
                lambda t, place: (
                    lax.div(t, count) * count + place[1 + lax.rem(t, count)],
                    0,
                    0,
                ),
            ),
        ),
        compiler_params=params_of(),
        cost_estimate=LIGHT,
        name="join_rows",
    )(place, *pieces)


def assemble(own, near, first, second, across):
    parts, rows, columns = near.shape
    count = parts + 1
    here = lax.axis_index("seq")
    place = [lax.axis_index("dp")] + [here ^ bits for bits in relative_bits()]
    place = jnp.stack(place).astype(jnp.int32)

    def kernel(place_ref, own_ref, near_ref, first_ref, second_ref, across_ref, out_ref, sem):
        along = place_ref[0]
        copies = [pltpu.make_async_copy(own_ref, out_ref.at[along], sem.at[0])]
        for step in range(parts):
            there = lax.rem(along + step + 1, count)
            for index, ref in enumerate((near_ref, first_ref, second_ref, across_ref)):
                copies.append(
                    pltpu.make_async_copy(
                        ref.at[step], out_ref.at[there, place_ref[1 + index]], sem.at[len(copies)]
                    )
                )
        for copy in copies:
            copy.start()
        for copy in copies:
            copy.wait()

    return pl.pallas_call(
        kernel,
        out_shape=jax.ShapeDtypeStruct((count, 4, rows, columns), own.dtype),
        in_specs=[pl.BlockSpec(memory_space=pltpu.SMEM)]
        + [pl.BlockSpec(memory_space=pl.ANY)] * 5,
        out_specs=pl.BlockSpec(memory_space=pltpu.VMEM),
        scratch_shapes=[pltpu.SemaphoreType.DMA((1 + 4 * parts,))],
        compiler_params=params_of(),
        cost_estimate=LIGHT,
        name="assemble",
    )(place, own, near, first, second, across)


def line_shifts(value):
    count = lax.axis_size("dp")
    return [
        lax.ppermute(value, "dp", [((to + step) % count, to) for to in range(count)])
        for step in range(1, count)
    ]


def line_gather(value):
    count = lax.axis_size("dp")
    line = lax.all_gather(value, "dp", axis=0)
    return lax.dynamic_slice_in_dim(
        jnp.concatenate([line, line], 0), lax.axis_index("dp") + 1, count - 1, 0
    )


def quarters_of(shard):
    return shard.reshape(4, shard.shape[0] // 4, shard.shape[1])


def spread(near):
    return swap_seq(near, FIRST), swap_seq(near, SECOND)


def spread_on(neighbours):
    return swap_seq(neighbours[1], FIRST)


def bits_of_place():
    core, here = lax.axis_index("section"), lax.axis_index("seq")
    x, y = lax.rem(here, 2), lax.div(here, 2)
    first, second = jnp.where(core == 0, x, y), jnp.where(core == 0, y, x)
    return jnp.stack([core, first, second]).astype(jnp.int32)


def grad_halves(left, right, count):
    length, depth = left.shape
    columns = right.shape[1]
    rows = depth // count
    quarter = round_up(rows, 32) // 4

    def kernel(bits_ref, left_ref, right_ref, keep_ref, send_ref, turned):
        block = pl.program_id(0)

        @pl.when(block == 0)
        def _():
            turned[...] = left_ref[...].astype(F32).T.astype(BF16).reshape(turned.shape)

        grad = dot(turned[block], right_ref[...], 1, 0)
        if 4 * quarter > rows:
            empty = jnp.zeros((4 * quarter - rows, columns), F32)
            grad = jnp.concatenate([grad, empty], axis=0)
        for at in range(4):
            part = grad[at * quarter : (at + 1) * quarter].astype(BF16)
            x, y = at % 2, at // 2
            first = jnp.where(bits_ref[0] == 0, x, y)
            second = jnp.where(bits_ref[0] == 0, y, x)

            @pl.when(first == bits_ref[1])
            def _():
                keep_ref[0, second] = part

            @pl.when(first != bits_ref[1])
            def _():
                send_ref[0, second] = part

    out = pl.BlockSpec((1, 2, quarter, columns), lambda z, bits: (z, 0, 0, 0))
    shape = jax.ShapeDtypeStruct((count, 2, quarter, columns), BF16)
    return pl.pallas_call(
        kernel,
        out_shape=(shape, shape),
        grid_spec=pltpu.PrefetchScalarGridSpec(
            num_scalar_prefetch=1,
            grid=(count,),
            in_specs=[
                pl.BlockSpec((length, depth), lambda z, bits: (0, 0)),
                pl.BlockSpec((length, columns), lambda z, bits: (0, 0)),
            ],
            out_specs=(out, out),
            scratch_shapes=[pltpu.VMEM((count, rows, length), BF16)],
        ),
        compiler_params=params_of(),
        cost_estimate=LIGHT,
        name="grad_halves",
    )(bits_of_place(), left, right)


def add_half(held, moved):
    count, _, rows, columns = held.shape

    def kernel(bits_ref, held_ref, moved_ref, keep_ref, send_ref):
        def total(index):
            return (held_ref[0, index].astype(F32) + moved_ref[0, index].astype(F32)).astype(BF16)

        keep_ref[0] = total(bits_ref[2])
        send_ref[0] = total(1 - bits_ref[2])

    both = pl.BlockSpec((1, 2, rows, columns), lambda z, bits: (z, 0, 0, 0))
    out = pl.BlockSpec((1, rows, columns), lambda z, bits: (z, 0, 0))
    shape = jax.ShapeDtypeStruct((count, rows, columns), BF16)
    return pl.pallas_call(
        kernel,
        out_shape=(shape, shape),
        grid_spec=pltpu.PrefetchScalarGridSpec(
            num_scalar_prefetch=1, grid=(count,), in_specs=[both, both], out_specs=(out, out)
        ),
        compiler_params=params_of(),
        cost_estimate=LIGHT,
        name="add_half",
    )(bits_of_place(), held, moved)


def add_low(left, right):
    return (left.astype(F32) + right.astype(F32)).astype(BF16)


class Sum:
    def __init__(self, left, right, count):
        self.keep, self.send = grad_halves(left, right, count)

    def first(self):
        self.moved = swap_seq(self.send, FIRST)

    def add(self):
        self.keep, self.send = add_half(self.keep, self.moved)

    def second(self):
        self.moved = swap_seq(self.send, SECOND)

    def over_line(self, gate):
        part = gate(add_low(self.keep, self.moved))
        self.line = lax.psum_scatter(part, "dp", scatter_dimension=0, tiled=True)[0]


def line_sum(part):
    line, count = lax.axis_index("dp"), lax.axis_size("dp")
    total = pick(part, line).astype(F32)
    for step in range(1, count):
        moved = lax.ppermute(
            pick(part, lax.rem(line + step, count)),
            "dp",
            [(source, (source + step) % count) for source in range(count)],
        )
        total = total + moved.astype(F32)
    return total.astype(BF16)


def plain_grad(left, right):
    depth, columns = left.shape[1], right.shape[1]

    def kernel(left_ref, right_ref, out_ref):
        turned = left_ref[...].astype(F32).T.astype(BF16)
        for start, end in tiles(columns):
            out_ref[:, start:end] = dot(turned, right_ref[:, start:end], 1, 0).astype(BF16)

    return whole_call(kernel, "plain_grad", [((depth, columns), BF16)], left, right)[0]


class Order:
    def __init__(self, token):
        self.token = token

    def __call__(self, *values):
        values, self.token = lax.optimization_barrier((values, self.token))
        return values if len(values) > 1 else values[0]

    def sent(self, *sums):
        for each in sums:
            each.send = self(each.send)

    def summed(self, *sums):
        for each in sums:
            each.line = self(each.line)

    def arrived(self, *sums):
        for each in sums:
            each.moved = self(each.moved)


def in_order(pieces):
    here = lax.axis_index("seq")
    return jnp.stack([pick(pieces, here ^ index) for index in range(4)])


def attention_forward(qkv, hidden_keys):
    length, width = qkv.shape
    width //= 3
    heads = width // HEAD_DIM

    def kernel(qkv_ref, hidden_ref, out_ref, lse_ref, q_s, k_s, v_s, o_s):
        head = pl.program_id(0)

        @pl.when(head == 0)
        def _():
            for index in range(heads):
                at = index * HEAD_DIM
                q_s[index] = qkv_ref[:, at : at + HEAD_DIM]
                k_s[index] = qkv_ref[:, width + at : width + at + HEAD_DIM]
                v_s[index] = qkv_ref[:, 2 * width + at : 2 * width + at + HEAD_DIM]

        scores = dot(k_s[head], q_s[head], 1, 1) * SCALE
        scores = jnp.where(hidden_ref[...] > 0, -1e9, scores)
        top = jnp.max(scores, axis=0, keepdims=True)
        expon = jnp.exp(scores - top)
        total = jnp.sum(expon, axis=0, keepdims=True)
        lse_ref[0] = top + jnp.log(total)
        mixed = dot(v_s[head], expon.astype(BF16), 0, 0) / total
        o_s[head] = mixed.T.astype(BF16)

        @pl.when(head == heads - 1)
        def _():
            for index in range(heads):
                out_ref[:, index * HEAD_DIM : (index + 1) * HEAD_DIM] = o_s[index]

    slab = pltpu.VMEM((heads, length, HEAD_DIM), BF16)
    return pl.pallas_call(
        kernel,
        grid=(heads,),
        out_shape=(
            jax.ShapeDtypeStruct((length, width), BF16),
            jax.ShapeDtypeStruct((heads, 1, length), F32),
        ),
        in_specs=[
            pl.BlockSpec((length, 3 * width), lambda h: (0, 0)),
            pl.BlockSpec((length, 1), lambda h: (0, 0)),
        ],
        out_specs=(
            pl.BlockSpec((length, width), lambda h: (0, 0)),
            pl.BlockSpec((1, 1, length), lambda h: (h, 0, 0)),
        ),
        scratch_shapes=[slab, slab, slab, slab],
        compiler_params=params_of(),
        cost_estimate=LIGHT,
        name="attention_forward",
    )(qkv, hidden_keys)


def attention_backward(qkv, d_out, lse, hidden_keys):
    length, width = d_out.shape
    heads = width // HEAD_DIM

    def kernel(
        qkv_ref, do_ref, lse_ref, hidden_ref, out_ref, sums_ref, q_s, k_s, v_s, do_s, dq_s, dk_s, dv_s
    ):
        head = pl.program_id(0)

        @pl.when(head == 0)
        def _():
            for index in range(heads):
                at = index * HEAD_DIM
                q_s[index] = qkv_ref[:, at : at + HEAD_DIM]
                k_s[index] = qkv_ref[:, width + at : width + at + HEAD_DIM]
                v_s[index] = qkv_ref[:, 2 * width + at : 2 * width + at + HEAD_DIM]
                do_s[index] = do_ref[:, at : at + HEAD_DIM]

        queries, keys, values, d_rows = q_s[head], k_s[head], v_s[head], do_s[head]
        scores = dot(keys, queries, 1, 1) * SCALE
        scores = jnp.where(hidden_ref[...] > 0, -1e9, scores)
        soft = jnp.exp(scores - lse_ref[0])
        d_soft = dot(values, d_rows, 1, 1)
        inner = jnp.sum(soft * d_soft, axis=0, keepdims=True)
        d_scores = (soft * (d_soft - inner)).astype(BF16)
        dv_s[head] = dot(soft.astype(BF16), d_rows, 1, 0).astype(BF16)
        dk_s[head] = (dot(d_scores, queries, 1, 0) * SCALE).astype(BF16)
        dq_s[head] = (dot(keys, d_scores, 0, 0) * SCALE).T.astype(BF16)

        @pl.when(head == heads - 1)
        def _():
            for index in range(heads):
                at = index * HEAD_DIM
                out_ref[:, at : at + HEAD_DIM] = dq_s[index]
                out_ref[:, width + at : width + at + HEAD_DIM] = dk_s[index]
                out_ref[:, 2 * width + at : 2 * width + at + HEAD_DIM] = dv_s[index]
            sums_ref[...] = jnp.sum(out_ref[...].astype(F32), axis=0, keepdims=True)

    slab = pltpu.VMEM((heads, length, HEAD_DIM), BF16)
    return pl.pallas_call(
        kernel,
        grid=(heads,),
        out_shape=(
            jax.ShapeDtypeStruct((length, 3 * width), BF16),
            jax.ShapeDtypeStruct((1, 3 * width), F32),
        ),
        in_specs=[
            pl.BlockSpec((length, 3 * width), lambda h: (0, 0)),
            pl.BlockSpec((length, width), lambda h: (0, 0)),
            pl.BlockSpec((1, 1, length), lambda h: (h, 0, 0)),
            pl.BlockSpec((length, 1), lambda h: (0, 0)),
        ],
        out_specs=(
            pl.BlockSpec((length, 3 * width), lambda h: (0, 0)),
            pl.BlockSpec((1, 3 * width), lambda h: (0, 0)),
        ),
        scratch_shapes=[slab] * 7,
        compiler_params=params_of(),
        cost_estimate=LIGHT,
        name="attention_backward",
    )(qkv, d_out, lse, hidden_keys)


def norm_parts(stream):
    centre = jnp.mean(stream, axis=-1, keepdims=True)
    offset = stream - centre
    spread = jnp.mean(offset * offset, axis=-1, keepdims=True)
    inverse = lax.rsqrt(spread + 1e-06)
    return offset * inverse, inverse


def tiles(total, step=256):
    return [(at, min(at + step, total)) for at in range(0, total, step)]


def whole_call(kernel, name, out_shapes, *arrays):
    shapes = tuple(jax.ShapeDtypeStruct(shape, dtype) for shape, dtype in out_shapes)
    return pl.pallas_call(
        kernel,
        out_shape=shapes,
        in_specs=whole_vmem(len(arrays)),
        out_specs=tuple(whole_vmem(len(shapes))),
        compiler_params=params_of(),
        cost_estimate=LIGHT,
        name=name,
    )(*arrays)


PIECES = 2


def piece_bounds(columns):
    step = round_up(columns // PIECES, 128)
    return [(at * step, min((at + 1) * step, columns)) for at in range(PIECES)]


def join_pieces(refs):
    return jnp.concatenate([ref[...] for ref in refs], axis=1).astype(F32)


def partial_product(left, weight, turned, name):
    length, depth = left.shape
    columns = weight.shape[0 if turned else 1]
    bounds = piece_bounds(columns)

    def kernel(left_ref, weight_ref, *out_refs):
        for start, end in tiles(columns):
            if turned:
                product = dot(left_ref[...], weight_ref[start:end, :depth], 1, 1)
            else:
                product = dot(left_ref[...], weight_ref[:, start:end], 1, 0)
            product = product.astype(BF16)
            for ref, (first, last) in zip(out_refs, bounds):
                low, high = max(start, first), min(end, last)
                if low < high:
                    ref[:, low - first : high - first] = product[:, low - start : high - start]

    shapes = [((length, last - first), BF16) for first, last in bounds]
    return whole_call(kernel, name, shapes, left, weight)


def project_in(base, partials, vectors, weight, shift):
    length, width = base.shape
    columns = weight.shape[1]

    def kernel(*refs):
        if partials is None:
            base_ref, vectors_ref, weight_ref, shift_ref, normed_ref, qkv_ref = refs
            stream = base_ref[...].astype(F32)
        else:
            base_ref, *refs = refs
            own_refs, other_refs = refs[:PIECES], refs[PIECES : 2 * PIECES]
            bias_ref, vectors_ref, weight_ref, shift_ref = refs[2 * PIECES : 2 * PIECES + 4]
            normed_ref, qkv_ref, stream_ref = refs[2 * PIECES + 4 :]
            stream = base_ref[...] + join_pieces(own_refs) + join_pieces(other_refs)
            stream_ref[...] = (stream + bias_ref[...]).astype(BF16)
            stream = stream_ref[...].astype(F32)
        normed = norm_parts(stream)[0] * vectors_ref[0:1, :] + vectors_ref[2:3, :]
        normed_ref[...] = normed.astype(BF16)
        for start, end in tiles(columns):
            product = dot(normed_ref[...], weight_ref[:, start:end], 1, 0)
            qkv_ref[:, start:end] = (product + shift_ref[:, start:end]).astype(BF16)

    shapes = [((length, width), BF16), ((length, columns), BF16)]
    if partials is None:
        normed, qkv = whole_call(kernel, "project_in", shapes, base, vectors, weight, shift)
        return base, normed, qkv
    shapes.append(((length, width), BF16))
    normed, qkv, stream = whole_call(
        kernel,
        "project_in",
        shapes,
        base,
        *partials[0],
        *partials[1],
        partials[2],
        vectors,
        weight,
        shift,
    )
    return stream, normed, qkv


def expand_hidden(stream, own, other, vectors, weight, shift):
    length, width = stream.shape
    columns = shift.shape[1]
    root = 0.7978845608028654

    def kernel(stream_ref, *refs):
        own_refs, other_refs, refs = refs[:PIECES], refs[PIECES : 2 * PIECES], refs[2 * PIECES :]
        vectors_ref, weight_ref, shift_ref, mid_ref, normed_ref, hidden_ref, slope_ref = refs
        middle = stream_ref[...].astype(F32) + join_pieces(own_refs)
        middle = middle + join_pieces(other_refs) + vectors_ref[6:7, :]
        mid_ref[...] = middle
        normed = norm_parts(middle)[0] * vectors_ref[1:2, :] + vectors_ref[3:4, :]
        normed_ref[...] = normed.astype(BF16)
        for start, end in tiles(columns):
            inner = dot(normed_ref[...], weight_ref[:, start:end], 1, 0) + shift_ref[:, start:end]
            square = inner * inner
            half_tanh = 0.5 * jnp.tanh(root * (inner + 0.044715 * square * inner))
            hidden_ref[:, start:end] = (inner * (0.5 + half_tanh)).astype(BF16)
            bend = (0.5 - 2.0 * half_tanh * half_tanh) * (root + 3 * 0.044715 * root * square)
            slope_ref[:, start:end] = (0.5 + half_tanh + inner * bend).astype(BF16)

    return whole_call(
        kernel,
        "expand_hidden",
        [
            ((length, width), F32),
            ((length, width), BF16),
            ((length, columns), BF16),
            ((length, columns), BF16),
        ],
        stream, *own, *other, vectors, weight, shift,
    )


def back_hidden(d_result, weight, slope):
    length, columns = slope.shape

    def kernel(d_ref, weight_ref, slope_ref, out_ref, sums_ref):
        for start, end in tiles(columns):
            d_hidden = dot(d_ref[...], weight_ref[start:end, :], 1, 1)
            d_pre = (d_hidden * slope_ref[:, start:end].astype(F32)).astype(BF16)
            out_ref[:, start:end] = d_pre
            sums_ref[:, start:end] = jnp.sum(d_pre.astype(F32), axis=0, keepdims=True)

    return whole_call(
        kernel,
        "back_hidden",
        [((length, columns), BF16), ((1, columns), F32)],
        d_result, weight, slope,
    )


def back_norm(base, own, other, stream, gain, weight):
    length, width = base.shape

    def kernel(*refs):
        base_ref, *refs = refs
        own_refs, other_refs, refs = refs[:PIECES], refs[PIECES : 2 * PIECES], refs[2 * PIECES :]
        stream_ref, gain_ref, *refs = refs
        unit, inverse = norm_parts(stream_ref[...].astype(F32))
        d_normed = join_pieces(own_refs) + join_pieces(other_refs)
        d_unit = d_normed * gain_ref[...]
        mean_d = jnp.mean(d_unit, axis=-1, keepdims=True)
        mean_du = jnp.mean(d_unit * unit, axis=-1, keepdims=True)
        base_wide = base_ref[...].astype(F32)
        total = base_wide + inverse * (d_unit - mean_d - unit * mean_du)
        if weight is None:
            low_ref, sums_ref = refs
        else:
            weight_ref, low_ref, sums_ref, wide_ref, product_ref = refs
            wide_ref[...] = total
        low_ref[...] = total.astype(BF16)
        sums_ref[0:1, :] = jnp.sum(d_normed * unit, axis=0, keepdims=True)
        sums_ref[1:2, :] = jnp.sum(d_normed, axis=0, keepdims=True)
        sums_ref[2:3, :] = jnp.sum(low_ref[...].astype(F32), axis=0, keepdims=True)
        sums_ref[3:4, :] = jnp.sum(base_wide, axis=0, keepdims=True)
        if weight is not None:
            for start, end in tiles(weight.shape[0]):
                product = dot(low_ref[...], weight_ref[start:end, :], 1, 1)
                product_ref[:, start:end] = product.astype(BF16)

    shapes = [((length, width), BF16), ((4, width), F32)]
    arrays = [base, *own, *other, stream, gain]
    if weight is not None:
        arrays.append(weight)
        shapes += [((length, width), F32), ((length, weight.shape[0]), BF16)]
    return whole_call(kernel, "back_norm", shapes, *arrays)


def column_sums(array):
    return jnp.sum(array.astype(F32), axis=0)


def on_device(
    section_inputs,
    key_mask,
    attention_in,
    attention_out,
    expand_weight,
    contract_weight,
    norm_gains,
    biases,
    expand_bias,
):
    core = lax.axis_index("section")
    here = lax.axis_index("seq")
    line = lax.axis_index("dp")
    count = lax.axis_size("dp")
    first = core == 0
    core_ref = core.astype(jnp.int32).reshape(1)

    width = attention_out.shape[2]
    own_rows = attention_out.shape[1]
    half_heads = own_rows // 2
    own_hidden = contract_weight.shape[1]
    half_hidden = round_up(round_up(own_hidden, 2) // 2, 16)
    in_runs = half_runs(3 * count * own_rows, 3 * count, half_heads, half_heads)
    hidden_runs = half_runs(count * own_hidden, count, half_hidden, half_hidden)
    in_width = 3 * count * half_heads
    hidden_width = count * half_hidden

    gate = Order(core)

    def both_layers(keep, send):
        received = swap_cores(send)
        return jnp.where(first, keep, received), jnp.where(first, received, keep)

    def pad_rows(array, step=32):
        extra = round_up(array.shape[-2], step) - array.shape[-2]
        if extra == 0:
            return array
        spec = [(0, 0)] * (array.ndim - 2) + [(0, extra), (0, 0)]
        return jnp.pad(array, spec)

    def prepared(halves):
        quarters = [quarters_of(pad_rows(half)) for half in halves]
        return quarters, [pick(quarter, here) for quarter in quarters]

    def built(own, near, others, rows):
        whole = assemble(own, near, *others)
        whole = whole.reshape(count, -1, whole.shape[3])[:, :rows]
        return whole.reshape(count * rows, whole.shape[2])

    micro, images, block, _ = section_inputs.shape[1:]
    tokens = section_inputs[0].reshape(micro * images, block, width)
    token_blocks = [pick(tokens, here ^ bits) for bits in range(4)]
    hidden_shift = jnp.pad(expand_bias[0], (0, 2 * half_hidden - own_hidden))
    packed = jnp.concatenate([norm_gains[0].reshape(-1), biases[0].reshape(-1), hidden_shift])
    small_size = packed.size
    packed = jnp.concatenate(both_layers(packed, packed))
    in_own, in_mine = prepared(
        both_layers(*split_columns(attention_in[0], in_runs, in_width, core_ref))
    )
    packed_rows = round_up(round_up(packed.size, in_width) // in_width, 8)
    packed = jnp.pad(packed, (0, packed_rows * in_width - packed.size)).reshape(-1, in_width)
    first_rows = in_mine[0].shape[0]
    in_first = jnp.concatenate([in_mine[0], packed], axis=0)
    token_blocks, in_first, expand_weight, attention_out, contract_weight = gate(
        token_blocks, in_first, expand_weight, attention_out, contract_weight
    )
    near_in_0 = line_shifts(in_first)
    inputs = [swap_seq(token_blocks[bits], (bits, 0)) for bits in range(1, 4)]
    out_parts = attention_out[0].reshape(2, half_heads, width)
    out_halves = both_layers(pick(out_parts, core), pick(out_parts, 1 - core))
    expand_halves = both_layers(
        *split_columns(expand_weight[0], hidden_runs, hidden_width, core_ref)
    )
    expand_own, expand_mine = prepared(
        [
            jnp.concatenate([high, low.reshape(own_rows, -1)], axis=1)
            for high, low in zip(expand_halves, out_halves)
        ]
    )
    expand_mine = gate(expand_mine)
    near_expand_0 = line_gather(expand_mine[0])

    def heads_of(merged):
        return merged[:, hidden_width:].reshape(count * half_heads, width)

    contract_parts = jnp.pad(
        contract_weight[0], ((0, 2 * half_hidden - own_hidden), (0, 0))
    ).reshape(2, half_hidden, width)
    contract_own, contract_mine = prepared(
        both_layers(pick(contract_parts, core), pick(contract_parts, 1 - core))
    )
    contract_mine = gate(contract_mine)
    near_contract_0 = line_gather(contract_mine[0])
    near_in_0, inputs, in_own, expand_own, contract_own = gate(
        near_in_0, inputs, in_own, expand_own, contract_own
    )
    packed = [packed] + [part[first_rows:] for part in near_in_0]
    near_in_0 = jnp.stack([part[:first_rows] for part in near_in_0])
    beside_in_0, near_expand_0 = gate(spread(near_in_0), near_expand_0)
    across_in_0 = spread_on(beside_in_0)
    image = jnp.concatenate([token_blocks[0], *inputs], axis=0)
    start = jnp.where(first, image, swap_cores(image))
    mask = pick(key_mask.reshape(micro * images, 4, block), here)
    mask = jnp.concatenate([pick(mask, here ^ bits) for bits in range(4)])
    hidden_keys = jnp.where(mask > 0, 0.0, 1.0).astype(F32)[:, None]

    packed = jnp.stack([part.reshape(-1) for part in packed])
    packed = lax.dynamic_slice_in_dim(
        jnp.concatenate([packed, packed], 0), lax.rem(count - line, count), count, 0
    ).astype(F32)

    def small_of(packed):
        vectors = packed[:, : 8 * own_rows].reshape(count, 8, own_rows)
        hidden = packed[:, 8 * own_rows :].reshape(count, 2, half_hidden)
        heads_part = pick(vectors.reshape(count, 8, 2, half_heads), core, 2)
        vectors = vectors.transpose(1, 0, 2).reshape(8, width)
        query, value = heads_part[:, 4].reshape(-1), heads_part[:, 5].reshape(-1)
        qkv_shift = jnp.concatenate([query, jnp.zeros_like(query), value])
        hidden_shift = pick(hidden, core, 1).reshape(1, -1)
        return vectors, qkv_shift.reshape(1, -1), hidden_shift

    vectors_0, qkv_shift_0, hidden_shift_0 = small_of(packed[:, :small_size])
    vectors_1, qkv_shift_1, hidden_shift_1 = small_of(packed[:, small_size : 2 * small_size])
    across_in_0, start, hidden_keys, qkv_shift_0, in_mine, expand_mine = gate(
        across_in_0, start, hidden_keys, qkv_shift_0, in_mine, expand_mine
    )

    beside_expand_0 = spread(near_expand_0)
    near_in_1 = line_shifts(in_mine[1])
    attn_in_0 = built(in_own[0], near_in_0, (*beside_in_0, across_in_0), own_rows)
    stream_0, normed_0, qkv_0 = project_in(start, None, vectors_0, attn_in_0, qkv_shift_0)
    beside_expand_0, near_in_1, qkv_0, expand_mine = gate(
        beside_expand_0, near_in_1, qkv_0, expand_mine
    )
    across_expand_0 = spread_on(beside_expand_0)
    near_in_1 = jnp.stack(near_in_1)
    beside_in_1 = spread(near_in_1)
    near_expand_1 = line_gather(expand_mine[1])
    mixed_0, lse_0 = attention_forward(qkv_0, hidden_keys)
    mixed_0, across_expand_0 = gate(mixed_0, across_expand_0)
    expand_0 = built(expand_own[0], near_expand_0, (*beside_expand_0, across_expand_0), own_rows)
    attn_out_0 = heads_of(expand_0)
    own = partial_product(mixed_0, attn_out_0, False, "project_heads")
    own, beside_in_1, near_contract_0, contract_mine = gate(
        own, beside_in_1, near_contract_0, contract_mine
    )
    across_in_1 = spread_on(beside_in_1)
    beside_contract_0 = spread(near_contract_0)
    near_contract_1 = line_gather(contract_mine[1])
    own, other = gate(own, swap_cores(own))
    middle_0, normed_mid_0, hidden_0, slope_0 = expand_hidden(
        stream_0, own, other, vectors_0, expand_0, hidden_shift_0
    )
    hidden_0, across_in_1, beside_contract_0, near_expand_1 = gate(
        hidden_0, across_in_1, beside_contract_0, near_expand_1
    )
    across_contract_0 = spread_on(beside_contract_0)
    beside_expand_1 = spread(near_expand_1)
    attn_in_1 = built(in_own[1], near_in_1, (*beside_in_1, across_in_1), own_rows)
    attn_in_1, across_contract_0 = gate(attn_in_1, across_contract_0)
    contract_0 = built(
        contract_own[0], near_contract_0, (*beside_contract_0, across_contract_0), half_hidden
    )
    own = gate(partial_product(hidden_0, contract_0, False, "contract_hidden"))
    own, other, token_blocks = gate(own, swap_cores(own), token_blocks)

    cotangents = [swap_seq(token_blocks[bits], (0, bits)) for bits in range(1, 3)]
    partials = (own, other, vectors_0[7:8])
    stream_1, normed_1, qkv_1 = project_in(middle_0, partials, vectors_1, attn_in_1, qkv_shift_1)
    beside_expand_1, near_contract_1, qkv_1, cotangents, token_blocks = gate(
        beside_expand_1, near_contract_1, qkv_1, cotangents, token_blocks
    )
    across_expand_1 = spread_on(beside_expand_1)
    beside_contract_1 = spread(near_contract_1)
    cotangents.append(swap_seq(token_blocks[3], (0, 3)))
    mixed_1, lse_1 = attention_forward(qkv_1, hidden_keys)
    mixed_1, across_expand_1 = gate(mixed_1, across_expand_1)
    expand_1 = built(expand_own[1], near_expand_1, (*beside_expand_1, across_expand_1), own_rows)
    attn_out_1 = heads_of(expand_1)
    own = partial_product(mixed_1, attn_out_1, False, "project_heads")
    own, beside_contract_1, cotangents = gate(own, beside_contract_1, cotangents)
    across_contract_1 = spread_on(beside_contract_1)
    image = jnp.concatenate([token_blocks[0], *cotangents], axis=0)
    own, other = gate(own, swap_cores(own))
    cotangent = jnp.where(first, swap_cores(image), image)
    middle_1, normed_mid_1, hidden_1, slope_1 = expand_hidden(
        stream_1, own, other, vectors_1, expand_1, hidden_shift_1
    )
    hidden_1, across_contract_1, cotangent = gate(hidden_1, across_contract_1, cotangent)

    small_rows = round_up(7 + round_up(hidden_width, width) // width, 16)

    def out_sum(grad, in_sums, mid_sums, hidden_sums, qkv_sums):
        heads = [qkv_sums[:, : width // 2], qkv_sums[:, width:]]
        rows = [in_sums[:1], mid_sums[:1], in_sums[1:2], mid_sums[1:], jnp.concatenate(heads, axis=1)]
        spare = (small_rows - 7) * width - hidden_width
        rows.append(jnp.pad(hidden_sums, ((0, 0), (0, spare))).reshape(-1, width))
        small = jnp.concatenate(rows, axis=0).astype(BF16)
        small = jnp.broadcast_to(small, (count, small_rows, width))
        parts = [grad.reshape(count, half_heads, width), small]
        part = gate(jnp.concatenate(parts, axis=1))
        return lax.psum_scatter(part, "dp", scatter_dimension=0, tiled=True)[0]

    def own_layer(low, high):
        return jnp.stack([jnp.where(first, low, high), swap_cores(jnp.where(first, high, low))])

    def last_place():
        return jnp.stack([gate.token, *(here ^ bits for bits in relative_bits())]).astype(jnp.int32)

    def rows_of(pieces, total):
        return join_rows(pieces, total, last_place())

    def columns_of(pieces, runs, total):
        return join_columns(pieces, runs, total, last_place())

    contract_sum_1 = Sum(hidden_1, cotangent, count)
    gate.sent(contract_sum_1)
    contract_sum_1.first()
    contract_1 = built(
        contract_own[1], near_contract_1, (*beside_contract_1, across_contract_1), half_hidden
    )
    d_pre_1, hidden_sums_1 = back_hidden(cotangent, contract_1, slope_1)
    d_pre_1 = gate(d_pre_1)
    expand_sum_1 = Sum(normed_mid_1, d_pre_1, count)
    gate.sent(expand_sum_1)
    expand_sum_1.first()
    own = gate(partial_product(gate(d_pre_1), expand_1, True, "back_expand"))
    gate.arrived(contract_sum_1)
    contract_sum_1.add()
    own_out = partial_product(hidden_1, contract_1, False, "contract_hidden")
    own, other, own_out = gate(own, swap_cores(own), own_out)
    gate.sent(contract_sum_1)
    contract_sum_1.second()
    d_branch_1, mid_sums_1, d_middle_1, d_mixed_1 = back_norm(
        cotangent, own, other, middle_1, vectors_1[1:2], attn_out_1
    )
    d_branch_1, d_mixed_1 = gate(d_branch_1, d_mixed_1)
    out_grad_1 = gate(plain_grad(mixed_1, d_branch_1))
    d_qkv_1, qkv_sums_1 = gate(attention_backward(qkv_1, gate(d_mixed_1), lse_1, hidden_keys))
    gate.arrived(contract_sum_1)
    contract_sum_1.over_line(gate)
    gate.arrived(expand_sum_1)
    expand_sum_1.add()
    gate.sent(expand_sum_1)
    expand_sum_1.second()
    in_sum_1 = Sum(normed_1, gate(d_qkv_1), count)
    gate.sent(in_sum_1)
    in_sum_1.first()
    own = gate(partial_product(gate(d_qkv_1), attn_in_1, True, "back_in"))
    own, other, other_out = gate(own, swap_cores(own), swap_cores(own_out))
    gate.arrived(expand_sum_1)
    expand_sum_1.over_line(gate)
    own_out, other_out = jnp.concatenate(own_out, axis=1), jnp.concatenate(other_out, axis=1)
    output = middle_1 + own_out.astype(F32) + other_out.astype(F32) + vectors_1[7:8]
    output = output.astype(BF16)
    d_result_0, in_sums_1 = back_norm(d_middle_1, own, other, stream_1, vectors_1[0:1], None)
    d_result_0 = gate(d_result_0)

    contract_sum_0 = Sum(hidden_0, gate(d_result_0), count)
    gate.sent(contract_sum_0)
    contract_sum_0.first()
    gate.arrived(in_sum_1)
    in_sum_1.add()
    gate.sent(in_sum_1)
    in_sum_1.second()
    d_pre_0, hidden_sums_0 = back_hidden(gate(d_result_0), contract_0, slope_0)
    d_pre_0, output = gate(d_pre_0, output)
    expand_sum_0 = Sum(normed_mid_0, gate(d_pre_0), count)
    gate.sent(expand_sum_0)
    expand_sum_0.first()
    gate.arrived(in_sum_1)
    in_sum_1.over_line(gate)
    gate.summed(contract_sum_1)
    own = gate(partial_product(gate(d_pre_0), expand_0, True, "back_expand"))
    gate.arrived(contract_sum_0)
    contract_sum_0.add()
    own, other = gate(own, swap_cores(own))
    gate.sent(contract_sum_0)
    contract_sum_0.second()
    d_branch_0, mid_sums_0, d_middle_0, d_mixed_0 = back_norm(
        d_result_0, gate(own), other, middle_0, vectors_0[1:2], attn_out_0
    )
    d_branch_0, d_mixed_0 = gate(d_branch_0, d_mixed_0)
    out_grad_0 = gate(plain_grad(mixed_0, d_branch_0))
    gate.summed(expand_sum_1)
    out_line_1 = out_sum(out_grad_1, in_sums_1, mid_sums_1, hidden_sums_1, qkv_sums_1)
    output = output.reshape(4, block, width)
    outputs = [swap_seq(output[bits], (0, bits)) for bits in range(1, 4)]
    d_qkv_0, qkv_sums_0 = gate(attention_backward(qkv_0, gate(d_mixed_0), lse_0, hidden_keys))
    outputs = gate(outputs)
    gate.arrived(expand_sum_0)
    expand_sum_0.add()
    gate.sent(expand_sum_0)
    expand_sum_0.second()
    gate.arrived(contract_sum_0)
    contract_sum_0.over_line(gate)
    in_sum_0 = Sum(normed_0, gate(d_qkv_0), count)
    gate.sent(in_sum_0)
    in_sum_0.first()
    gate.summed(in_sum_1)
    own = gate(partial_product(gate(d_qkv_0), attn_in_0, True, "back_in"))
    own, other = gate(own, swap_cores(own))
    gate.arrived(expand_sum_0)
    expand_sum_0.over_line(gate)
    d_input_0, in_sums_0 = back_norm(d_middle_0, gate(own), other, stream_0, vectors_0[0:1], None)
    d_input_0, out_line_1 = gate(d_input_0, out_line_1)

    d_input_0 = d_input_0.reshape(4, block, width)
    gate.arrived(in_sum_0)
    in_sum_0.add()
    gate.summed(contract_sum_0)
    gate.sent(in_sum_0)
    in_sum_0.second()
    contract_near = own_layer(contract_sum_0.line, contract_sum_1.line)
    gate.arrived(in_sum_0)
    contract_near = gate(contract_near)
    contract_beside = spread(contract_near)
    in_sum_0.over_line(gate)
    gate.summed(expand_sum_0)
    contract_beside = gate(contract_beside)
    contract_across = spread_on(contract_beside)
    inputs_back = [swap_seq(d_input_0[bits], (bits, 0)) for bits in range(1, 3)]
    expand_near = own_layer(expand_sum_0.line, expand_sum_1.line)
    contract_across, inputs_back, expand_near = gate(contract_across, inputs_back, expand_near)
    expand_beside = spread(expand_near)
    inputs_back.append(swap_seq(d_input_0[3], (3, 0)))
    grad_contract = rows_of([contract_near, *contract_beside, contract_across], own_hidden)
    gate.summed(in_sum_0)
    out_line_0 = out_sum(out_grad_0, in_sums_0, mid_sums_0, hidden_sums_0, qkv_sums_0)
    expand_beside, grad_contract, inputs_back = gate(expand_beside, grad_contract, inputs_back)
    in_near = gate(own_layer(in_sum_0.line, in_sum_1.line))
    in_beside = spread(in_near)
    expand_across = spread_on(expand_beside)
    in_beside, expand_across = gate(in_beside, expand_across)
    in_across = spread_on(in_beside)
    grad_expand = columns_of(
        [expand_near, *expand_beside, expand_across], hidden_runs, count * own_hidden
    )
    out_line_0, in_across, grad_expand = gate(out_line_0, in_across, grad_expand)
    out_near = gate(own_layer(out_line_0, out_line_1))
    out_moved = swap_seq(out_near, FIRST)
    grad_in = columns_of([in_near, *in_beside, in_across], in_runs, 3 * width)
    out_moved, grad_in = gate(out_moved, grad_in)
    out_near = add_low(out_near, out_moved)
    out_moved = swap_seq(out_near, SECOND)
    returned = [
        jnp.where(first, low, high)
        for low, high in zip([d_input_0[0], *inputs_back], [output[0], *outputs])
    ]
    results = in_order(jnp.stack(returned)).astype(F32)
    results = results.reshape(1, micro, images, block, width)
    out_near = add_low(out_near, gate(out_moved)).astype(F32)
    mine, other = out_near[0, :half_heads], out_near[1, :half_heads]
    grad_out = jnp.concatenate([jnp.where(first, mine, other), jnp.where(first, other, mine)])

    def own_part(rows, size):
        return lax.dynamic_slice_in_dim(rows, line * size, size, rows.ndim - 1)

    def halves_of(mine, other, size):
        mine, other = own_part(mine, size), own_part(other, size)
        low, high = jnp.where(first, mine, other), jnp.where(first, other, mine)
        return jnp.concatenate([low, high], axis=-1)

    mine, other = out_near[0, half_heads:], out_near[1, half_heads:]
    shared = own_part(mine[:6], own_rows)
    query = halves_of(mine[6, : width // 2], other[6, : width // 2], half_heads)
    value = halves_of(mine[6, width // 2 :], other[6, width // 2 :], half_heads)
    hidden = [rows[7:].reshape(-1)[:hidden_width] for rows in (mine, other)]
    hidden = halves_of(*hidden, half_hidden)[:own_hidden]
    grad_shifts = jnp.concatenate([shared[2:4], query[None], value[None], shared[4:6]])

    return (
        results,
        grad_in[None],
        grad_out[None],
        grad_expand[None],
        grad_contract.transpose(1, 0, 2),
        shared[None, :2],
        grad_shifts[None],
        hidden[None],
    )


def plain_passed_along(value, axis, steps):
    count = lax.axis_size(axis)
    initial, last = (max(0, -steps), min(count, count - steps))
    return lax.ppermute(value, axis, [(source, source + steps) for source in range(initial, last)])


def plain_layer_norm(stream, gain, shift):
    centre = jnp.mean(stream, axis=-1, keepdims=True)
    offset = stream - centre
    spread = jnp.mean(offset * offset, axis=-1, keepdims=True)
    return offset * lax.rsqrt(spread + 1e-06) * gain + shift


def plain_matmul(left, right):
    return jnp.dot(left, right, preferred_element_type=F32)


def plain_left_matmul(left, right):
    return lax.dot_general(
        left, right, (((0,), (0,)), ((), ())), preferred_element_type=F32
    )


def plain_right_matmul(left, right):
    return lax.dot_general(
        left, right, (((1,), (1,)), ((), ())), preferred_element_type=F32
    )


def plain_gather_once(local):
    whole = (
        lax.all_gather(local[0], "dp", axis=1, tiled=True),
        lax.all_gather(local[1], "dp", axis=1, tiled=True),
        lax.all_gather(local[2], "dp", axis=1, tiled=True),
        lax.all_gather(local[3], "dp", axis=1, tiled=True),
        lax.all_gather(local[4], "dp", axis=2, tiled=True),
        lax.all_gather(local[5], "dp", axis=2, tiled=True),
        lax.all_gather(local[6], "dp", axis=1, tiled=True),
    )
    return tuple((piece[0] for piece in whole))


def plain_split_heads(heads):
    images, length, _, width = heads.shape
    count = width // HEAD_DIM
    queries = heads[:, :, 0].reshape(images, length, count, HEAD_DIM)
    key_rows = heads[:, :, 1].reshape(images, length, count, HEAD_DIM)
    value_rows = heads[:, :, 2].reshape(images, length, count, HEAD_DIM)
    return (queries, key_rows, value_rows)


def plain_head_scores(queries, key_rows, visible):
    scores = jnp.einsum(
        "nqhd,nkhd->nhqk", queries, key_rows, preferred_element_type=F32
    ) * HEAD_DIM ** (-0.5)
    return jnp.where(visible[:, None, None, :], scores, -1000000000.0)


def plain_attend(heads, visible):
    images, length, _, width = heads.shape
    queries, key_rows, value_rows = plain_split_heads(heads)
    scores = plain_head_scores(queries, key_rows, visible)
    row_max = jnp.max(scores, axis=-1, keepdims=True)
    expon = jnp.exp(scores - row_max)
    total = jnp.sum(expon, axis=-1, keepdims=True)
    softmaxed = (expon / total).astype(BF16)
    log_total = (row_max + jnp.log(total))[..., 0]
    mixture = jnp.einsum(
        "nhqk,nkhd->nqhd", softmaxed, value_rows, preferred_element_type=F32
    )
    return (mixture.astype(BF16).reshape(images, length, width), log_total)


def plain_attend_back(heads, log_total, visible, d_mixture):
    images, length, _, width = heads.shape
    queries, key_rows, value_rows = plain_split_heads(heads)
    d_rows = d_mixture.reshape(queries.shape)
    scores = plain_head_scores(queries, key_rows, visible)
    softmaxed = jnp.exp(scores - log_total[..., None])
    d_soft = jnp.einsum("nqhd,nkhd->nhqk", d_rows, value_rows, preferred_element_type=F32)
    inner = jnp.sum(softmaxed * d_soft, axis=-1, keepdims=True)
    d_scores = (softmaxed * (d_soft - inner)).astype(BF16)
    scale = HEAD_DIM ** (-0.5)
    d_queries = (
        jnp.einsum("nhqk,nkhd->nqhd", d_scores, key_rows, preferred_element_type=F32)
        * scale
    ).astype(BF16)
    d_keys = (
        jnp.einsum("nhqk,nqhd->nkhd", d_scores, queries, preferred_element_type=F32) * scale
    ).astype(BF16)
    d_values = jnp.einsum(
        "nhqk,nqhd->nkhd",
        softmaxed.astype(BF16),
        d_rows,
        preferred_element_type=F32,
    ).astype(BF16)
    return jnp.stack([d_queries, d_keys, d_values], axis=2).reshape(images, length, 3, width)


def plain_forward_layer(stream_in, visible, params):
    attn_in, attn_out, expand, contract, gains, shifts, expand_shift = params
    images, rows_seq, width = stream_in.shape
    stream = stream_in.astype(F32).reshape(-1, width)
    gains32 = gains.astype(F32)
    shifts32 = shifts.astype(F32)
    normed = plain_layer_norm(stream, gains32[0], shifts32[0]).astype(BF16)
    qkv_shift = jnp.stack([shifts32[2], jnp.zeros_like(shifts32[2]), shifts32[3]])
    projected = (plain_matmul(normed, attn_in).reshape(images, rows_seq, 3, width) + qkv_shift).astype(
        BF16
    )
    heads = lax.all_to_all(projected, "seq", split_axis=3, concat_axis=1, tiled=True)
    mixture, log_total = plain_attend(heads, visible)
    mixed_rows = lax.all_to_all(mixture, "seq", split_axis=1, concat_axis=2, tiled=True).reshape(
        -1, width
    )
    middle = stream + plain_matmul(mixed_rows, attn_out) + shifts32[4]
    normed_mid = plain_layer_norm(middle, gains32[1], shifts32[1]).astype(BF16)
    hidden_pre = plain_matmul(normed_mid, expand) + expand_shift.astype(F32)
    hidden = jax.nn.gelu(hidden_pre, approximate=True).astype(BF16)
    result = middle + plain_matmul(hidden, contract) + shifts32[5]
    saved = (
        stream_in,
        normed,
        heads,
        log_total,
        mixed_rows,
        middle,
        normed_mid,
        hidden_pre,
        hidden,
        visible,
    )
    return (result.reshape(images, rows_seq, width), saved)


def plain_backward_layer(d_result, saved, params):
    attn_in, attn_out, expand, contract, gains, shifts, expand_shift = params
    (
        stream_in,
        normed,
        heads,
        log_total,
        mixed_rows,
        middle,
        normed_mid,
        hidden_pre,
        hidden,
        visible,
    ) = saved
    images, rows_seq, width = d_result.shape
    gains32 = gains.astype(F32)
    shifts32 = shifts.astype(F32)
    d_flat = d_result.reshape(-1, width)
    d_wide = d_flat.astype(F32)
    grad_contract = plain_left_matmul(hidden, d_flat)
    grad_last_bias = jnp.sum(d_wide, axis=0)
    d_hidden = plain_right_matmul(d_flat, contract)
    _, gelu_back = jax.vjp(lambda inner: jax.nn.gelu(inner, approximate=True), hidden_pre)
    d_pre = gelu_back(d_hidden)[0].astype(BF16)
    grad_expand = plain_left_matmul(normed_mid, d_pre)
    grad_expand_bias = jnp.sum(d_pre.astype(F32), axis=0)
    d_normed_mid = plain_right_matmul(d_pre, expand)
    _, norm_back_mid = jax.vjp(plain_layer_norm, middle, gains32[1], shifts32[1])
    d_middle_part, grad_gain_mid, grad_shift_mid = norm_back_mid(d_normed_mid)
    d_middle = d_wide + d_middle_part
    d_branch = d_middle.astype(BF16)
    grad_out_bias = jnp.sum(d_branch.astype(F32), axis=0)
    grad_attn_out = plain_left_matmul(mixed_rows, d_branch)
    d_mixture = (
        plain_right_matmul(d_branch, attn_out).astype(BF16).reshape(images, rows_seq, width)
    )
    d_heads = lax.all_to_all(d_mixture, "seq", split_axis=2, concat_axis=1, tiled=True)
    d_projected_heads = plain_attend_back(heads, log_total, visible, d_heads)
    d_projected = lax.all_to_all(
        d_projected_heads, "seq", split_axis=1, concat_axis=3, tiled=True
    ).reshape(-1, 3 * width)
    grad_attn_in = plain_left_matmul(normed, d_projected)
    column_sums = jnp.sum(d_projected.astype(F32), axis=0).reshape(3, width)
    d_normed = plain_right_matmul(d_projected, attn_in)
    stream = stream_in.astype(F32).reshape(-1, width)
    _, norm_back_in = jax.vjp(plain_layer_norm, stream, gains32[0], shifts32[0])
    d_stream_part, grad_gain_in, grad_shift_in = norm_back_in(d_normed)
    d_stream = d_middle + d_stream_part
    grad_gains = jnp.stack([grad_gain_in, grad_gain_mid])
    grad_shifts = jnp.stack(
        [
            grad_shift_in,
            grad_shift_mid,
            column_sums[0],
            column_sums[2],
            grad_out_bias,
            grad_last_bias,
        ]
    )
    grads = (
        grad_attn_in,
        grad_attn_out,
        grad_expand,
        grad_contract,
        grad_gains,
        grad_shifts,
        grad_expand_bias,
    )
    return (d_stream.reshape(images, rows_seq, width), grads)


def plain_send_forward(values):
    return plain_passed_along(values, "section", 1)


def plain_send_backward(values):
    return plain_passed_along(values, "section", -1)


def on_device_any(
    section_inputs,
    key_mask,
    attention_in,
    attention_out,
    expand_weight,
    contract_weight,
    norm_gains,
    biases,
    expand_bias,
):
    micro = section_inputs.shape[1]
    leading = lax.axis_index("section") == 0
    local = (
        attention_in,
        attention_out,
        expand_weight,
        contract_weight,
        norm_gains,
        biases,
        expand_bias,
    )
    sources = section_inputs[0]
    visible_all = key_mask > 0
    blank = jnp.zeros_like(sources[0])
    recv_forward = blank
    recv_backward = blank
    saves = {}
    outputs = [None] * micro
    input_grads = [None] * micro
    totals = None
    params = plain_gather_once(local)
    for tick in range(micro + 2):
        if tick <= micro:
            source = sources[tick] if tick < micro else blank
            stream_now = jnp.where(leading, source, recv_forward)
            visible_now = jnp.where(
                leading, visible_all[min(tick, micro - 1)], visible_all[max(tick - 1, 0)]
            )
            result, saved = plain_forward_layer(stream_now, visible_now, params)
            saves[tick] = saved
            if tick >= 1:
                outputs[tick - 1] = result
            sent_forward = plain_send_forward(result.astype(BF16))
        if tick >= 1:
            early = saves[tick - 2] if tick - 2 in saves else saves[tick]
            later = saves[tick] if tick in saves else saves[tick - 2]
            chosen = jax.tree.map(
                lambda left_one, right_one: jnp.where(leading, left_one, right_one), early, later
            )
            cotangent = sources[tick - 1] if tick <= micro else blank
            d_result = jnp.where(leading, recv_backward, cotangent)
            d_stream, grads = plain_backward_layer(d_result, chosen, params)
            active = jnp.where(leading, tick >= 2, tick <= micro)
            grads = tuple((jnp.where(active, piece, 0.0) for piece in grads))
            if tick >= 2:
                input_grads[tick - 2] = d_stream
            totals = (
                grads if totals is None else tuple((old + new for old, new in zip(totals, grads)))
            )
            recv_backward = plain_send_backward(d_stream.astype(BF16))
        if tick <= micro:
            recv_forward = sent_forward
    totals = (
        lax.psum_scatter(
            totals[0].astype(BF16), "dp", scatter_dimension=0, tiled=True
        ).astype(F32),
        lax.psum_scatter(
            totals[1].astype(BF16), "dp", scatter_dimension=0, tiled=True
        ).astype(F32),
        lax.psum_scatter(
            totals[2].astype(BF16), "dp", scatter_dimension=0, tiled=True
        ).astype(F32),
        lax.psum_scatter(
            totals[3].astype(BF16), "dp", scatter_dimension=0, tiled=True
        ).astype(F32),
        lax.psum_scatter(
            totals[4].astype(BF16), "dp", scatter_dimension=1, tiled=True
        ).astype(F32),
        lax.psum_scatter(
            totals[5].astype(BF16), "dp", scatter_dimension=1, tiled=True
        ).astype(F32),
        lax.psum_scatter(
            totals[6].astype(BF16), "dp", scatter_dimension=0, tiled=True
        ).astype(F32),
    )
    totals = (
        lax.psum(totals[0].astype(BF16), "seq").astype(F32),
        lax.psum(totals[1].astype(BF16), "seq").astype(F32),
        lax.psum(totals[2].astype(BF16), "seq").astype(F32),
        lax.psum(totals[3].astype(BF16), "seq").astype(F32),
        lax.psum(totals[4].astype(BF16), "seq").astype(F32),
        lax.psum(totals[5].astype(BF16), "seq").astype(F32),
        lax.psum(totals[6].astype(BF16), "seq").astype(F32),
    )
    results = jnp.stack(
        [jnp.where(leading, input_grads[index], outputs[index]) for index in range(micro)]
    )[None]
    return (
        results,
        totals[0][None],
        totals[1][None],
        totals[2][None],
        totals[3][None],
        totals[4][None],
        totals[5][None],
        totals[6][None],
    )


def solution(mesh):
    in_specs = (
        P("section", None, "dp", "seq", None),
        P(None, "dp", None),
        P("section", "dp", None),
        P("section", "dp", None),
        P("section", "dp", None),
        P("section", "dp", None),
        P("section", None, "dp"),
        P("section", None, "dp"),
        P("section", "dp"),
    )
    out_specs = (
        P("section", None, "dp", "seq", None),
        P("section", "dp", None),
        P("section", "dp", None),
        P("section", "dp", None),
        P("section", "dp", None),
        P("section", None, "dp"),
        P("section", None, "dp"),
        P("section", "dp"),
    )

    def by_size(section_inputs, *others):
        _, micro, images, _, _ = section_inputs.shape
        one_image_each = micro * images == lax.axis_size("seq") == 4
        rows, hidden = others[2].shape[1], others[4].shape[1]
        even = rows % (2 * HEAD_DIM) == 0 and rows % 32 == 0
        even = even and round_up(round_up(hidden, 2) // 2, 16) % 32 == 0
        plan = on_device if one_image_each and even else on_device_any
        return plan(section_inputs, *others)

    return jax.shard_map(
        by_size, mesh=mesh, in_specs=in_specs, out_specs=out_specs, check_vma=False
    )
```
